32 devices in a mesh: dp: 2 (over x), seq: 8 (over z, y), mp: 2 (over core).
Axes of the slice: x: 2, y: 2, z: 4, core: 2. Of those that a mesh axis runs over, the one named last changes fastest.
Arguments:
- hidden_in: bfloat16 [4, 1024, 2048], P('dp', 'seq'), may hold values from -6 to 6
- doc_lengths: int32 [4, 4], P('dp'), may hold values from 1 to 1020, as said below
- attn_gain: bfloat16 [2048], P(('dp', 'seq')), may hold values from 0.5 to 1.5
- query_weight: bfloat16 [2048, 2048], P(('dp', 'seq'), 'mp'), may hold values from -0.125 to 0.125
- key_weight: bfloat16 [2048, 512], P(('dp', 'seq'), 'mp'), may hold values from -0.125 to 0.125
- value_weight: bfloat16 [2048, 512], P(('dp', 'seq'), 'mp'), may hold values from -0.125 to 0.125
- output_weight: bfloat16 [2048, 2048], P('mp', ('dp', 'seq')), may hold values from -2 to 2
- ffn_gain: bfloat16 [2048], P(('dp', 'seq')), may hold values from 0.5 to 1.5
- gate_weight: bfloat16 [2048, 8192], P(('dp', 'seq'), 'mp'), may hold values from -0.125 to 0.125
- up_weight: bfloat16 [2048, 8192], P(('dp', 'seq'), 'mp'), may hold values from -0.125 to 0.125
- down_weight: bfloat16 [8192, 2048], P('mp', ('dp', 'seq')), may hold values from -0.0625 to 0.0625
- out_grad: bfloat16 [4, 1024, 2048], P('dp', 'seq'), may hold values from -6 to 6
Outputs:
- layer_out: bfloat16 [4, 1024, 2048], P('dp', 'seq')
- input_grad: bfloat16 [4, 1024, 2048], P('dp', 'seq')
- attn_gain_grad: float32 [2048], P(('dp', 'seq'))
- query_grad: float32 [2048, 2048], P(('dp', 'seq'), 'mp')
- key_grad: float32 [2048, 512], P(('dp', 'seq'), 'mp')
- value_grad: float32 [2048, 512], P(('dp', 'seq'), 'mp')
- output_grad: float32 [2048, 2048], P('mp', ('dp', 'seq'))
- ffn_gain_grad: float32 [2048], P(('dp', 'seq'))
- gate_grad: float32 [2048, 8192], P(('dp', 'seq'), 'mp')
- up_grad: float32 [2048, 8192], P(('dp', 'seq'), 'mp')
- down_grad: float32 [8192, 2048], P('mp', ('dp', 'seq'))
The draws below stay inside these ranges and needn't reach their ends.
Inputs may be any that keep to these rules, and one draw needn't show every extreme that they name: `doc_lengths`: in each row the lengths sum to less than 1024; the positions after the last document are padding. In each row one document starts within the first 128 positions and ends within the last 128.
All inputs are finite; a program needn't handle non-finite values.
Results may differ from the reference program's by a relative error of at most 0.018.
Values may be sent and summed in bfloat16 or wider, within the bound.
A program may use at most 256 MiB of HBM per device.

```python
import math
import jax
import jax.numpy as jnp
from jax import lax

D = 2048
H = 32
KVH = 8
HD = 64
FF = 8192
LEN_DEV = 128
NDOC = 4
LEN = 1024
ROWS = 4


def draw_doc_lengths(key, part):
    key = jax.random.fold_in(key, 11)
    key_short, key_choice, key_padding = jax.random.split(key, 3)
    short_most = max(LEN_DEV // 8, 1)
    lengths = jax.random.randint(key_short, (ROWS, NDOC), 1, short_most + 1)
    chosen = jax.random.randint(key_choice, (ROWS, 1), 0, NDOC)
    padding = jax.random.randint(key_padding, (ROWS, 1), 1, short_most + 1)
    longest = jnp.arange(NDOC)[None, :] == chosen
    others = jnp.sum(jnp.where(longest, 0, lengths), axis=1, keepdims=True)
    return jnp.where(longest, LEN - padding - others, lengths).astype(jnp.int32)


def block_scale(own_key, shape, shards, smallest, high):
    def one(axis_at, parts):
        steps = jax.random.uniform(jax.random.fold_in(jax.random.fold_in(own_key, 6), axis_at), (parts,), jnp.float32, smallest / len(shards), high / len(shards))
        return jnp.repeat(jnp.exp(steps), shape[axis_at] // parts).reshape((-1,) + (1,) * (len(shape) - axis_at - 1))

    factor_of = one(*shards[0])
    for cut in shards[1:]:
        factor_of = factor_of * one(*cut)
    return factor_of


def scatter_about(stream_key, extent, deviation, reach, cuts=(), held_as=jnp.bfloat16):
    level = block_scale(stream_key, extent, cuts, -0.22, 0.18) if cuts else 1.0
    drawn = jax.random.normal(stream_key, extent, jnp.float32) * deviation * level
    return jnp.minimum(jnp.maximum(drawn, -reach), reach).astype(held_as)


def setup_inputs(seed: int = 0) -> dict:
    key_list = jax.random.split(jax.random.key(seed), 13)
    hidden_in = scatter_about(key_list[0], (ROWS, LEN, D), 1.0, 6.0, ((0, 2), (1, 8)))
    doc_lengths = draw_doc_lengths(jax.random.fold_in(key_list[12], 71), 0)
    attn_gain = jnp.clip(1.0 + 0.1 * jax.random.normal(key_list[2], (D,), jnp.float32), 0.5, 1.5).astype(jnp.bfloat16)
    query_weight = scatter_about(key_list[3], (D, H * HD), D ** -0.5, 0.125, ((0, 16), (1, 2)))
    key_weight = scatter_about(key_list[4], (D, KVH * HD), D ** -0.5, 0.125, ((0, 16), (1, 2)))
    value_weight = scatter_about(key_list[5], (D, KVH * HD), D ** -0.5, 0.125, ((0, 16), (1, 2)))
    output_weight = scatter_about(key_list[6], (H * HD, D), (max(H * HD * 4 // LEN, 1)) ** -0.5, 2.0, ((0, 2), (1, 16)))
    ffn_gain = jnp.clip(1.0 + 0.1 * jax.random.normal(key_list[7], (D,), jnp.float32), 0.5, 1.5).astype(jnp.bfloat16)
    gate_weight = scatter_about(key_list[8], (D, FF), D ** -0.5, 0.125, ((0, 16), (1, 2)))
    up_weight = scatter_about(key_list[9], (D, FF), D ** -0.5, 0.125, ((0, 16), (1, 2)))
    down_weight = scatter_about(key_list[10], (FF, D), FF ** -0.5, 0.0625, ((0, 2), (1, 16)))
    out_grad = scatter_about(key_list[11], (ROWS, LEN, D), 1.0, 6.0, ((0, 2), (1, 8)))
    return {"hidden_in": hidden_in, "doc_lengths": doc_lengths, "attn_gain": attn_gain, "query_weight": query_weight, "key_weight": key_weight, "value_weight": value_weight, "output_weight": output_weight, "ffn_gain": ffn_gain, "gate_weight": gate_weight, "up_weight": up_weight, "down_weight": down_weight, "out_grad": out_grad}


EPSILON = 1e-05
MASKED = -1e+30
ROPE_THETA = 500000.0
ROPE_FACTOR = 32.0
LOW_FACTOR = 1.0
HIGH_FACTOR = 4.0
PRIOR_CONTEXT = 8192.0

@jax.custom_vjp
def low(v):
    return lax.optimization_barrier(v.astype(jnp.bfloat16)).astype(jnp.float32)

@jax.custom_vjp
def low_back(v):
    return v

def low_keep(v):
    return (low(v), None)

def low_pass(kept, grad):
    return (grad,)

def back_keep(v):
    return (v, None)

def back_low(kept, grad):
    return (low(grad),)
low.defvjp(low_keep, low_pass)
low_back.defvjp(back_keep, back_low)

def matmul(left, right):
    return jnp.dot(left, right, precision=lax.Precision.HIGHEST, preferred_element_type=jnp.float32)

def inverse_freqs(head_dim):
    ladder = jnp.arange(head_dim // 2, dtype=jnp.float32)
    base = ROPE_THETA ** (-2.0 * ladder / head_dim)
    wavelen = 2.0 * math.pi / base
    smooth = (PRIOR_CONTEXT / wavelen - LOW_FACTOR) / (HIGH_FACTOR - LOW_FACTOR)
    blended = (1.0 - smooth) * base / ROPE_FACTOR + smooth * base
    low_limit = PRIOR_CONTEXT / LOW_FACTOR
    high_limit = PRIOR_CONTEXT / HIGH_FACTOR
    return jnp.where(wavelen < high_limit, base, jnp.where(wavelen > low_limit, base / ROPE_FACTOR, blended))

def rope_tables(position, head_dim):
    angles = position[..., None] * inverse_freqs(head_dim)
    angles = jnp.concatenate([angles, angles], axis=-1)
    return (jnp.cos(angles)[..., None, :], jnp.sin(angles)[..., None, :])

def rotate(values, cosine, sine):
    middle = values.shape[-1] // 2
    turned = jnp.concatenate([-values[..., middle:], values[..., :middle]], axis=-1)
    return values * cosine + turned * sine

def doc_tables(lengths, total_len):
    ends = jnp.cumsum(lengths, axis=-1).astype(jnp.int32)
    starts = (ends - lengths).astype(jnp.int32)
    places = jnp.arange(total_len, dtype=jnp.int32)
    doc_count = lengths.shape[-1]
    doc_index = lax.optimization_barrier(jnp.sum((places[None, :, None] >= ends[:, None, :]).astype(jnp.int32), axis=-1)).astype(jnp.int32)
    segment = jnp.where(doc_index < doc_count, doc_index + 1, 0).astype(jnp.int32)
    bounds = jnp.concatenate([starts, ends[:, -1:]], axis=-1)
    chosen = doc_index[:, :, None] == jnp.arange(doc_count + 1, dtype=jnp.int32)[None, None, :]
    begin = lax.optimization_barrier(jnp.sum(jnp.where(chosen, bounds[:, None, :], 0), axis=-1)).astype(jnp.int32)
    position = (places[None, :] - begin).astype(jnp.float32)
    return (segment, position)

def attend_block(query_block, segment_block, start, keys, values, segment):
    block_len = query_block.shape[0]
    places = start + jnp.arange(block_len, dtype=jnp.int32)
    key_places = jnp.arange(keys.shape[0], dtype=jnp.int32)
    allowed = (segment_block[:, None] == segment[None, :]) & (places[:, None] >= key_places[None, :])
    scores = low_back(jnp.einsum('ikgd,jkd->kgij', query_block, keys, precision=lax.Precision.HIGHEST) * HD ** (-0.5))
    masked = jnp.where(allowed, scores, MASKED)
    row_max = lax.optimization_barrier(jnp.max(masked, axis=-1, keepdims=True))
    row_total = lax.optimization_barrier(jnp.sum(jnp.exp(masked - row_max), axis=-1, keepdims=True))
    attn_probs = low(jnp.exp(masked - (row_max + jnp.log(row_total))))
    mixed_out = jnp.einsum('kgij,jkd->ikgd', attn_probs, values, precision=lax.Precision.HIGHEST)
    return mixed_out.reshape(block_len, H * HD)

def layer_forward(inputs, attn_gain, query_weight, key_weight, value_weight, output_weight, ffn_gain, gate_weight, up_weight, down_weight, segment, cosine, sine):
    scale_one = lax.rsqrt(lax.optimization_barrier(jnp.mean(inputs * inputs, axis=-1, keepdims=True)) + EPSILON)
    normed_one = low(inputs * scale_one * attn_gain)
    query_pre = low_back(matmul(normed_one, query_weight)).reshape(LEN, H, HD)
    queries = low(rotate(query_pre, cosine, sine)).reshape(LEN, KVH, H // KVH, HD)
    key_pre = low_back(matmul(normed_one, key_weight)).reshape(LEN, KVH, HD)
    keys = low(rotate(key_pre, cosine, sine))
    values = low(low_back(matmul(normed_one, value_weight))).reshape(LEN, KVH, HD)
    block_len = min(512, LEN)
    block_count = LEN // block_len
    query_blocks = queries.reshape(block_count, block_len, KVH, H // KVH, HD)
    segment_blocks = segment.reshape(block_count, block_len)
    starts = jnp.arange(block_count, dtype=jnp.int32) * block_len
    attend = jax.checkpoint(attend_block)
    attn_out = lax.map(lambda items: attend(items[0], items[1], items[2], keys, values, segment), (query_blocks, segment_blocks, starts)).reshape(LEN, H * HD)
    attn_out = low(low_back(attn_out))
    residual = inputs + low_back(matmul(attn_out, output_weight))
    scale_two = lax.rsqrt(lax.optimization_barrier(jnp.mean(residual * residual, axis=-1, keepdims=True)) + EPSILON)
    normed_two = low(residual * scale_two * ffn_gain)
    gate_proj = low_back(matmul(normed_two, gate_weight))
    up_proj = low_back(matmul(normed_two, up_weight))
    hidden_units = low(jax.nn.silu(gate_proj) * up_proj)
    return residual + low_back(matmul(hidden_units, down_weight))

def reference(hidden_in, doc_lengths, attn_gain, query_weight, key_weight, value_weight, output_weight, ffn_gain, gate_weight, up_weight, down_weight, out_grad):
    weights = tuple((array.astype(jnp.float32) for array in (attn_gain, query_weight, key_weight, value_weight, output_weight, ffn_gain, gate_weight, up_weight, down_weight)))

    def one_row(totals, items):
        row_in, row_lengths, row_grad = items
        segment, position = doc_tables(row_lengths[None, :], LEN)
        cosine, sine = rope_tables(position[0], HD)

        def run(row_values, *params):
            return layer_forward(row_values, *params, segment[0], cosine, sine)
        row_out, pull = jax.vjp(run, row_in.astype(jnp.float32), *weights)
        grads = pull(row_grad.astype(jnp.float32))
        totals = tuple((summed + fresh for summed, fresh in zip(totals, grads[1:])))
        return (totals, (row_out.astype(jnp.bfloat16), grads[0].astype(jnp.bfloat16)))
    zeros = tuple((jnp.zeros(array.shape, jnp.float32) for array in weights))
    totals, outputs = lax.scan(one_row, zeros, (hidden_in, doc_lengths, out_grad))
    return (outputs[0], outputs[1], totals[0], totals[1], totals[2], totals[3], totals[4], totals[5], totals[6], totals[7], totals[8])
```

```python
import functools
import math

import jax
import jax.numpy as jnp
from jax import lax
from jax.experimental import pallas as pl
from jax.experimental.pallas import tpu as pltpu
from jax.sharding import PartitionSpec as P

H = 32
KVH = 8
HD = 64
SQUARE = 4

EPSILON = 1e-05
MASKED = -1e30
ROPE_THETA = 500000.0
ROPE_FACTOR = 32.0
LOW_FACTOR = 1.0
HIGH_FACTOR = 4.0
PRIOR_CONTEXT = 8192.0
VMEM = 56 * 1024 * 1024


def inverse_freqs(head_dim):
    ladder = jnp.arange(head_dim // 2, dtype=jnp.float32)
    base = ROPE_THETA ** (-2.0 * ladder / head_dim)
    wavelen = 2.0 * math.pi / base
    smooth = (PRIOR_CONTEXT / wavelen - LOW_FACTOR) / (HIGH_FACTOR - LOW_FACTOR)
    blended = (1.0 - smooth) * base / ROPE_FACTOR + smooth * base
    low_limit = PRIOR_CONTEXT / LOW_FACTOR
    high_limit = PRIOR_CONTEXT / HIGH_FACTOR
    return jnp.where(
        wavelen < high_limit, base, jnp.where(wavelen > low_limit, base / ROPE_FACTOR, blended)
    )


def rope_tables(position, head_dim):
    angles = position[..., None] * inverse_freqs(head_dim)
    angles = jnp.concatenate([angles, angles], axis=-1)
    return (jnp.cos(angles)[..., None, :], jnp.sin(angles)[..., None, :])


def rotate(values, cosine, sine):
    middle = values.shape[-1] // 2
    turned = jnp.concatenate([-values[..., middle:], values[..., :middle]], axis=-1)
    return values * cosine + turned * sine


def unrotate(grads, cosine, sine):
    middle = grads.shape[-1] // 2
    scaled = grads * sine
    turned = jnp.concatenate([scaled[..., middle:], -scaled[..., :middle]], axis=-1)
    return grads * cosine + turned


def dot(left, right, dims=((1,), (0,))):
    return lax.dot_general(left, right, (dims, ((), ())), preferred_element_type=jnp.float32)


def swap(value, axis, mask):
    size = lax.axis_size(axis)
    return lax.ppermute(value, axis, [(i, i ^ mask) for i in range(size)])


def cut(value, start, length, axis):
    return lax.dynamic_slice_in_dim(value, start, length, axis)


def put(whole, part, start, axis):
    return lax.dynamic_update_slice_in_dim(whole, part, start, axis)


def mask_of(info, row, row_count, local, keys):
    span = SQUARE * local
    low, high = info[0], info[1]

    def place_of(index):
        block = (index // local) % SQUARE
        part = index // span
        return (high ^ part) * span + (low ^ block) * local + index % local

    def segment_of(place):
        total = jnp.zeros_like(place)
        for doc in range(4):
            total = total + (place >= info[2 + row * 4 + doc]).astype(jnp.int32)
        return total

    query = place_of(lax.broadcasted_iota(jnp.int32, (span, 1), 0))
    key = place_of(lax.broadcasted_iota(jnp.int32, (1, keys), 1))
    return (segment_of(query) == segment_of(key)) & (query >= key)


def attend_kernel(local, keys, group, info, q_ref, kv_ref, out_ref, lse_ref):
    row = pl.program_id(0)
    span = SQUARE * local
    allowed = mask_of(info, row, None, local, keys)
    kv = kv_ref[...].reshape(keys, 2 * HD)
    k, v = kv[:, :HD], kv[:, HD:]
    q_all = q_ref[...].reshape(span, group * HD)
    outs, sums = [], []
    for head in range(group):
        q = q_all[:, head * HD : (head + 1) * HD]
        score = dot(q, k, ((1,), (1,))) * HD ** (-0.5)
        score = jnp.where(allowed, score, MASKED)
        top = jnp.max(score, axis=1, keepdims=True)
        grown = jnp.exp(score - top)
        total = jnp.sum(grown, axis=1, keepdims=True)
        lse = top + jnp.log(total)
        probs = (grown * (1.0 / total)).astype(jnp.bfloat16)
        outs.append(dot(probs, v))
        sums.append(lse)
    out_ref[...] = jnp.concatenate(outs, axis=1).reshape(out_ref.shape)
    lse_ref[...] = jnp.concatenate(sums, axis=1).reshape(lse_ref.shape)


def attend(info, queries, kv):
    blocks, rows, local, width = queries.shape
    parts = kv.shape[0]
    keys = parts * blocks * local
    group = width // HD
    return pl.pallas_call(
        functools.partial(attend_kernel, local, keys, group),
        grid=(rows,),
        out_shape=(
            jax.ShapeDtypeStruct((blocks, rows, local, width), jnp.float32),
            jax.ShapeDtypeStruct((blocks, rows, local, group), jnp.float32),
        ),
        in_specs=[
            pl.BlockSpec(memory_space=pltpu.SMEM),
            pl.BlockSpec((blocks, 1, local, width), lambda r: (0, r, 0, 0)),
            pl.BlockSpec((parts, blocks, 1, local, 2 * HD), lambda r: (0, 0, r, 0, 0)),
        ],
        out_specs=(
            pl.BlockSpec((blocks, 1, local, width), lambda r: (0, r, 0, 0)),
            pl.BlockSpec((blocks, 1, local, group), lambda r: (0, r, 0, 0)),
        ),
        compiler_params=pltpu.CompilerParams(vmem_limit_bytes=VMEM),
        cost_estimate=pl.CostEstimate(
            flops=8 * rows * blocks * local * keys * width,
            bytes_accessed=rows * blocks * local * width * 8,
            transcendentals=rows * blocks * local * keys * group,
        ),
        name="attend",
    )(info, queries, kv)


def attend_back_kernel(
    local, keys, group, info, q_ref, kv_ref, go_ref, out_ref, lse_ref, dq_ref, dkv_ref
):
    row = pl.program_id(0)
    span = SQUARE * local
    allowed = mask_of(info, row, None, local, keys)
    kv = kv_ref[...].reshape(keys, 2 * HD)
    k, v = kv[:, :HD], kv[:, HD:]
    q_all = q_ref[...].reshape(span, group * HD)
    go_all = go_ref[...].reshape(span, group * HD)
    out_all = out_ref[...].reshape(span, group * HD)
    lse_all = lse_ref[...].reshape(span, group)
    dq = []
    dk = jnp.zeros((keys, HD), jnp.float32)
    dv = jnp.zeros((keys, HD), jnp.float32)
    scale = HD ** (-0.5)
    for head in range(group):
        q = q_all[:, head * HD : (head + 1) * HD]
        go = go_all[:, head * HD : (head + 1) * HD]
        out = out_all[:, head * HD : (head + 1) * HD]
        delta = jnp.sum(go.astype(jnp.float32) * out, axis=1, keepdims=True)
        score = dot(q, k, ((1,), (1,))) * scale
        probs = jnp.exp(jnp.where(allowed, score, MASKED) - lse_all[:, head : head + 1])
        dv = dv + dot(probs.astype(jnp.bfloat16), go, ((0,), (0,)))
        prob_grad = dot(go, v, ((1,), (1,)))
        score_grad = (probs * (prob_grad - delta)).astype(jnp.bfloat16)
        dq.append(dot(score_grad, k) * scale)
        dk = dk + dot(score_grad, q, ((0,), (0,)))
    dq_ref[...] = jnp.concatenate(dq, axis=1).reshape(dq_ref.shape)
    dkv_ref[...] = jnp.concatenate([dk * scale, dv], axis=1).reshape(dkv_ref.shape)


def attend_back(info, queries, kv, out_grads, out, lse):
    blocks, rows, local, width = queries.shape
    parts = kv.shape[0]
    keys = parts * blocks * local
    group = width // HD
    wide = pl.BlockSpec((blocks, 1, local, width), lambda r: (0, r, 0, 0))
    kv_spec = pl.BlockSpec((parts, blocks, 1, local, 2 * HD), lambda r: (0, 0, r, 0, 0))
    return pl.pallas_call(
        functools.partial(attend_back_kernel, local, keys, group),
        grid=(rows,),
        out_shape=(
            jax.ShapeDtypeStruct(queries.shape, jnp.float32),
            jax.ShapeDtypeStruct(kv.shape, jnp.float32),
        ),
        in_specs=[
            pl.BlockSpec(memory_space=pltpu.SMEM),
            wide,
            kv_spec,
            wide,
            wide,
            pl.BlockSpec((blocks, 1, local, group), lambda r: (0, r, 0, 0)),
        ],
        out_specs=(wide, kv_spec),
        compiler_params=pltpu.CompilerParams(vmem_limit_bytes=VMEM),
        cost_estimate=pl.CostEstimate(
            flops=20 * rows * blocks * local * keys * width,
            bytes_accessed=rows * blocks * local * width * 16,
            transcendentals=rows * blocks * local * keys * group,
        ),
        name="attend_back",
    )(info, queries, kv, out_grads, out, lse)


def bits_of(size):
    return [1 << b for b in range(size.bit_length() - 1)]


def spread_weight(shard, axis, place):
    dp, high, low, dp_size, high_size = place
    other = 1 - axis
    block = shard.shape[axis]
    width = shard.shape[other] // SQUARE
    pieces = [cut(shard, low * width, width, other)]
    for mask in range(1, SQUARE):
        pieces.append(swap(cut(shard, (low ^ mask) * width, width, other), "seq", mask))
    shape = [0, 0]
    shape[axis], shape[other] = SQUARE * block, width
    square = jnp.zeros(shape, shard.dtype)
    for mask in range(SQUARE):
        square = put(square, pieces[mask], (low ^ mask) * block, axis)
    parts = {(0, 0): square}
    for bit in bits_of(high_size):
        for (a, b) in list(parts):
            parts[a, b ^ bit] = swap(parts[a, b], "seq", SQUARE * bit)
    for bit in bits_of(dp_size):
        for (a, b) in list(parts):
            parts[a ^ bit, b] = swap(parts[a, b], "dp", bit)
    shape[axis] = SQUARE * block * high_size * dp_size
    whole = jnp.zeros(shape, shard.dtype)
    for (a, b), part in parts.items():
        index = (dp ^ a) * high_size + (high ^ b)
        whole = put(whole, part, index * SQUARE * block, axis)
    return whole


def settle_grad(grad, axis, place):
    dp, high, low, dp_size, high_size = place
    other = 1 - axis
    width = grad.shape[other]
    kept = grad
    for index, size, name, unit in ((dp, dp_size, "dp", 1), (high, high_size, "seq", SQUARE)):
        for bit in reversed(bits_of(size)):
            half = kept.shape[axis] // 2
            mine = (index // bit) % 2
            sent = cut(kept, (1 - mine) * half, half, axis).astype(jnp.bfloat16)
            kept = cut(kept, mine * half, half, axis) + swap(sent, name, unit * bit).astype(
                jnp.float32
            )
    block = kept.shape[axis] // SQUARE
    shape = [0, 0]
    shape[axis], shape[other] = block, SQUARE * width
    whole = jnp.zeros(shape, jnp.float32)
    whole = put(whole, cut(kept, low * block, block, axis), low * width, other)
    for mask in range(1, SQUARE):
        sent = cut(kept, (low ^ mask) * block, block, axis).astype(jnp.bfloat16)
        got = swap(sent, "seq", mask).astype(jnp.float32)
        whole = put(whole, got, (low ^ mask) * width, other)
    return whole


def gather_square(own, core):
    tokens, width = own.shape
    half = width // 2
    mine = cut(own, core * half, half, 1)
    got = jnp.concatenate([swap(mine, "seq", mask) for mask in range(1, SQUARE)], axis=0)
    across = swap(got, "mp", 1)
    first = jnp.where(core == 0, got, across)
    second = jnp.where(core == 0, across, got)
    return jnp.concatenate([own, jnp.concatenate([first, second], axis=1)], axis=0)


def scatter_square(partial, core):
    tokens, width = partial.shape[0] // SQUARE, partial.shape[1]
    half = width // 2
    kept = cut(partial, core * half, half, 1)
    sent = cut(partial, (1 - core) * half, half, 1).astype(jnp.bfloat16)
    kept = kept + swap(sent, "mp", 1).astype(jnp.float32)
    total = kept[:tokens]
    for mask in range(1, SQUARE):
        part = kept[mask * tokens : (mask + 1) * tokens].astype(jnp.bfloat16)
        total = total + swap(part, "seq", mask).astype(jnp.float32)
    mine = total.astype(jnp.bfloat16)
    across = swap(mine, "mp", 1)
    return jnp.concatenate(
        [jnp.where(core == 0, mine, across), jnp.where(core == 0, across, mine)], axis=1
    ).astype(jnp.float32)


def norm_back(values, scale, gain, grad):
    weighted = grad * gain
    gain_grad = jnp.sum(grad * values * scale, axis=0)
    inner = jnp.mean(weighted * values, axis=-1, keepdims=True)
    return (weighted * scale - values * scale**3 * inner, gain_grad)


def shards(
    hidden_in,
    doc_lengths,
    attn_gain,
    query_weight,
    key_weight,
    value_weight,
    output_weight,
    ffn_gain,
    gate_weight,
    up_weight,
    down_weight,
    out_grad,
):
    rows, local, model = hidden_in.shape
    tokens = rows * local
    seq = lax.axis_index("seq")
    core = lax.axis_index("mp")
    low, high = seq % SQUARE, seq // SQUARE
    high_size = lax.axis_size("seq") // SQUARE
    place = (lax.axis_index("dp"), high, low, lax.axis_size("dp"), high_size)
    group = H // KVH
    span = SQUARE * local

    ends = jnp.cumsum(doc_lengths, axis=-1)
    info = jnp.concatenate([jnp.stack([low, high]), ends.reshape(-1)]).astype(jnp.int32)

    gains = lax.all_gather(jnp.stack([attn_gain, ffn_gain]), ("dp", "seq"), axis=1, tiled=True)
    gain_one, gain_two = gains[0].astype(jnp.float32), gains[1].astype(jnp.float32)

    own_in = hidden_in.reshape(tokens, model)
    all_in = gather_square(own_in, core).astype(jnp.float32)
    query_own = spread_weight(query_weight, 0, place)
    key_own = spread_weight(key_weight, 0, place)
    value_own = spread_weight(value_weight, 0, place)
    output_own = spread_weight(output_weight, 1, place)
    gate_own = spread_weight(gate_weight, 0, place)
    up_own = spread_weight(up_weight, 0, place)
    down_own = spread_weight(down_weight, 1, place)
    all_grad = gather_square(out_grad.reshape(tokens, model), core)

    blocks = low ^ jnp.arange(SQUARE, dtype=jnp.int32)
    spots = (high * span + blocks[:, None] * local + jnp.arange(local, dtype=jnp.int32)[None, :])
    reached = spots[:, None, :, None] >= ends[None, :, None, :]
    begin = jnp.max(jnp.where(reached, ends[None, :, None, :], 0), axis=-1)
    position = (spots[:, None, :] - begin).astype(jnp.float32)
    cosine, sine = rope_tables(position, HD)

    scale_one = lax.rsqrt(jnp.mean(all_in * all_in, axis=-1, keepdims=True) + EPSILON)
    normed_one = (all_in * scale_one * gain_one).astype(jnp.bfloat16)
    query_pre = dot(normed_one, query_own).reshape(SQUARE, rows, local, group, HD)
    key_pre = dot(normed_one, key_own).reshape(SQUARE, rows, local, 1, HD)
    value_pre = dot(normed_one, value_own).reshape(SQUARE, rows, local, HD)
    queries = rotate(query_pre, cosine, sine).astype(jnp.bfloat16)
    queries = queries.reshape(SQUARE, rows, local, group * HD)
    keys = rotate(key_pre, cosine, sine).astype(jnp.bfloat16).reshape(value_pre.shape)
    kv = jnp.concatenate([keys, value_pre.astype(jnp.bfloat16)], axis=-1)[None]
    for bit in bits_of(high_size):
        kv = jnp.concatenate([kv, swap(kv, "seq", SQUARE * bit)], axis=0)
    attn, lse = attend(info, queries, kv)
    attn_low = attn.reshape(SQUARE * tokens, group * HD).astype(jnp.bfloat16)
    residual = own_in.astype(jnp.float32) + scatter_square(dot(attn_low, output_own), core)

    scale_two = lax.rsqrt(jnp.mean(residual * residual, axis=-1, keepdims=True) + EPSILON)
    normed_two = (residual * scale_two * gain_two).astype(jnp.bfloat16)
    normed_two = gather_square(normed_two, core)
    gate_proj = dot(normed_two, gate_own)
    up_proj = dot(normed_two, up_own)
    sigmoid_gate = jax.nn.sigmoid(gate_proj)
    silu_gate = gate_proj * sigmoid_gate
    hidden_units = (silu_gate * up_proj).astype(jnp.bfloat16)
    hidden_grad = dot(all_grad, down_own, ((1,), (1,)))
    gate_act = (
        hidden_grad * up_proj * sigmoid_gate * (1.0 + gate_proj * (1.0 - sigmoid_gate))
    ).astype(jnp.bfloat16)
    up_act = (hidden_grad * silu_gate).astype(jnp.bfloat16)
    down_grad = settle_grad(dot(hidden_units, all_grad, ((0,), (0,))), 1, place)
    normed_two_grad = scatter_square(
        dot(gate_act, gate_own, ((1,), (1,))) + dot(up_act, up_own, ((1,), (1,))), core
    )
    layer_out = residual + scatter_square(dot(hidden_units, down_own), core)
    layer_out = layer_out.astype(jnp.bfloat16).reshape(hidden_in.shape)
    gate_grad = settle_grad(dot(normed_two, gate_act, ((0,), (0,))), 0, place)
    up_grad = settle_grad(dot(normed_two, up_act, ((0,), (0,))), 0, place)

    residual_part, ffn_gain_grad = norm_back(residual, scale_two, gain_two, normed_two_grad)
    residual_grad = out_grad.reshape(tokens, model).astype(jnp.float32) + residual_part
    residual_low = gather_square(residual_grad.astype(jnp.bfloat16), core)
    output_grad = settle_grad(dot(attn_low, residual_low, ((0,), (0,))), 1, place)
    attn_grad = dot(residual_low, output_own, ((1,), (1,))).astype(jnp.bfloat16)
    attn_grad = attn_grad.reshape(queries.shape)
    query_acc, kv_acc = attend_back(info, queries, kv, attn_grad, attn, lse)
    for bit in reversed(bits_of(high_size)):
        sent = kv_acc[bit:].astype(jnp.bfloat16)
        kv_acc = kv_acc[:bit] + swap(sent, "seq", SQUARE * bit).astype(jnp.float32)
    kv_acc = kv_acc[0]
    query_back = unrotate(query_acc.reshape(query_pre.shape), cosine, sine).astype(jnp.bfloat16)
    key_back = unrotate(kv_acc[..., :HD].reshape(key_pre.shape), cosine, sine)
    key_back = key_back.astype(jnp.bfloat16).reshape(SQUARE * tokens, HD)
    value_back = kv_acc[..., HD:].astype(jnp.bfloat16).reshape(SQUARE * tokens, HD)
    query_back = query_back.reshape(SQUARE * tokens, group * HD)
    normed_one_grad = scatter_square(
        dot(query_back, query_own, ((1,), (1,)))
        + dot(key_back, key_own, ((1,), (1,)))
        + dot(value_back, value_own, ((1,), (1,))),
        core,
    )
    query_grad = settle_grad(dot(normed_one, query_back, ((0,), (0,))), 0, place)
    key_grad = settle_grad(dot(normed_one, key_back, ((0,), (0,))), 0, place)
    value_grad = settle_grad(dot(normed_one, value_back, ((0,), (0,))), 0, place)
    own_32 = own_in.astype(jnp.float32)
    own_scale = lax.rsqrt(jnp.mean(own_32 * own_32, axis=-1, keepdims=True) + EPSILON)
    input_part, attn_gain_grad = norm_back(own_32, own_scale, gain_one, normed_one_grad)
    input_grad = (residual_grad + input_part).astype(jnp.bfloat16).reshape(hidden_in.shape)
    gain_grads = lax.psum_scatter(
        jnp.stack([attn_gain_grad, ffn_gain_grad]), ("dp", "seq"), scatter_dimension=1, tiled=True
    )
    return (
        layer_out,
        input_grad,
        gain_grads[0],
        query_grad,
        key_grad,
        value_grad,
        output_grad,
        gain_grads[1],
        gate_grad,
        up_grad,
        down_grad,
    )


def solution(mesh):
    return jax.shard_map(
        shards,
        mesh=mesh,
        in_specs=(
            P("dp", "seq", None),
            P("dp", None),
            P(("dp", "seq")),
            P(("dp", "seq"), "mp"),
            P(("dp", "seq"), "mp"),
            P(("dp", "seq"), "mp"),
            P("mp", ("dp", "seq")),
            P(("dp", "seq")),
            P(("dp", "seq"), "mp"),
            P(("dp", "seq"), "mp"),
            P("mp", ("dp", "seq")),
            P("dp", "seq", None),
        ),
        out_specs=(
            P("dp", "seq", None),
            P("dp", "seq", None),
            P(("dp", "seq")),
            P(("dp", "seq"), "mp"),
            P(("dp", "seq"), "mp"),
            P(("dp", "seq"), "mp"),
            P("mp", ("dp", "seq")),
            P(("dp", "seq")),
            P(("dp", "seq"), "mp"),
            P(("dp", "seq"), "mp"),
            P("mp", ("dp", "seq")),
        ),
        check_vma=False,
    )
```

```python
import functools
import math

import jax
import jax.numpy as jnp
from jax import lax
from jax.experimental import pallas as pl
from jax.experimental.pallas import tpu as pltpu
from jax.sharding import PartitionSpec as P

H = 32
KVH = 8
HD = 64
SQUARE = 4

EPSILON = 1e-05
MASKED = -1e30
ROPE_THETA = 500000.0
ROPE_FACTOR = 32.0
LOW_FACTOR = 1.0
HIGH_FACTOR = 4.0
PRIOR_CONTEXT = 8192.0
VMEM = 62 * 1024 * 1024


def inverse_freqs(head_dim):
    ladder = jnp.arange(head_dim // 2, dtype=jnp.float32)
    base = ROPE_THETA ** (-2.0 * ladder / head_dim)
    wavelen = 2.0 * math.pi / base
    smooth = (PRIOR_CONTEXT / wavelen - LOW_FACTOR) / (HIGH_FACTOR - LOW_FACTOR)
    blended = (1.0 - smooth) * base / ROPE_FACTOR + smooth * base
    low_limit = PRIOR_CONTEXT / LOW_FACTOR
    high_limit = PRIOR_CONTEXT / HIGH_FACTOR
    return jnp.where(
        wavelen < high_limit, base, jnp.where(wavelen > low_limit, base / ROPE_FACTOR, blended)
    )


def rope_tables(position, head_dim):
    angles = position[..., None] * inverse_freqs(head_dim)
    angles = jnp.concatenate([angles, angles], axis=-1)
    return (jnp.cos(angles)[..., None, :], jnp.sin(angles)[..., None, :])


def rotate(values, cosine, sine):
    middle = values.shape[-1] // 2
    turned = jnp.concatenate([-values[..., middle:], values[..., :middle]], axis=-1)
    return values * cosine + turned * sine


def unrotate(grads, cosine, sine):
    middle = grads.shape[-1] // 2
    scaled = grads * sine
    turned = jnp.concatenate([scaled[..., middle:], -scaled[..., :middle]], axis=-1)
    return grads * cosine + turned


def dot(left, right, dims=((1,), (0,))):
    return lax.dot_general(left, right, (dims, ((), ())), preferred_element_type=jnp.float32)


def swap(value, axis, mask):
    size = lax.axis_size(axis)
    return lax.ppermute(value, axis, [(i, i ^ mask) for i in range(size)])


def cut(value, start, length, axis):
    return lax.dynamic_slice_in_dim(value, start, length, axis)


def put(whole, part, start, axis):
    return lax.dynamic_update_slice_in_dim(whole, part, start, axis)


def mask_of(info, row, row_count, local, keys):
    span = SQUARE * local
    low, high = info[0], info[1]

    def place_of(index):
        block = (index // local) % SQUARE
        part = index // span
        return (high ^ part) * span + (low ^ block) * local + index % local

    def segment_of(place):
        total = jnp.zeros_like(place)
        for doc in range(4):
            total = total + (place >= info[2 + row * 4 + doc]).astype(jnp.int32)
        return total

    query = place_of(lax.broadcasted_iota(jnp.int32, (span, 1), 0))
    key = place_of(lax.broadcasted_iota(jnp.int32, (1, keys), 1))
    return (segment_of(query) == segment_of(key)) & (query >= key)


def attend_kernel(local, keys, group, info, q_ref, kv_ref, out_ref, lse_ref):
    row = pl.program_id(0)
    span = SQUARE * local
    allowed = mask_of(info, row, None, local, keys)
    kv = kv_ref[...].reshape(keys, 2 * HD)
    k, v = kv[:, :HD], kv[:, HD:]
    q_all = q_ref[...].reshape(span, group * HD)
    outs, sums = [], []
    for head in range(group):
        q = q_all[:, head * HD : (head + 1) * HD]
        score = dot(q, k, ((1,), (1,))) * HD ** (-0.5)
        score = jnp.where(allowed, score, MASKED)
        top = jnp.max(score, axis=1, keepdims=True)
        grown = jnp.exp(score - top)
        total = jnp.sum(grown, axis=1, keepdims=True)
        lse = top + jnp.log(total)
        probs = (grown * (1.0 / total)).astype(jnp.bfloat16)
        outs.append(dot(probs, v))
        sums.append(lse)
    out_ref[...] = jnp.concatenate(outs, axis=1).reshape(out_ref.shape)
    lse_ref[...] = jnp.concatenate(sums, axis=1).reshape(lse_ref.shape)


def attend(info, queries, kv):
    blocks, rows, local, width = queries.shape
    parts = kv.shape[0]
    keys = parts * blocks * local
    group = width // HD
    return pl.pallas_call(
        functools.partial(attend_kernel, local, keys, group),
        grid=(rows,),
        out_shape=(
            jax.ShapeDtypeStruct((blocks, rows, local, width), jnp.float32),
            jax.ShapeDtypeStruct((blocks, rows, local, group), jnp.float32),
        ),
        in_specs=[
            pl.BlockSpec(memory_space=pltpu.SMEM),
            pl.BlockSpec((blocks, 1, local, width), lambda r: (0, r, 0, 0)),
            pl.BlockSpec((parts, blocks, 1, local, 2 * HD), lambda r: (0, 0, r, 0, 0)),
        ],
        out_specs=(
            pl.BlockSpec((blocks, 1, local, width), lambda r: (0, r, 0, 0)),
            pl.BlockSpec((blocks, 1, local, group), lambda r: (0, r, 0, 0)),
        ),
        compiler_params=pltpu.CompilerParams(vmem_limit_bytes=VMEM),
        cost_estimate=pl.CostEstimate(
            flops=8 * rows * blocks * local * keys * width,
            bytes_accessed=rows * blocks * local * width * 8,
            transcendentals=rows * blocks * local * keys * group,
        ),
        name="attend",
    )(info, queries, kv)


def attend_back_kernel(
    local, keys, group, info, q_ref, kv_ref, go_ref, out_ref, lse_ref, dq_ref, dkv_ref
):
    row = pl.program_id(0)
    span = SQUARE * local
    allowed = mask_of(info, row, None, local, keys)
    kv = kv_ref[...].reshape(keys, 2 * HD)
    k, v = kv[:, :HD], kv[:, HD:]
    q_all = q_ref[...].reshape(span, group * HD)
    go_all = go_ref[...].reshape(span, group * HD)
    out_all = out_ref[...].reshape(span, group * HD)
    lse_all = lse_ref[...].reshape(span, group)
    dq = []
    dk = jnp.zeros((keys, HD), jnp.float32)
    dv = jnp.zeros((keys, HD), jnp.float32)
    scale = HD ** (-0.5)
    for head in range(group):
        q = q_all[:, head * HD : (head + 1) * HD]
        go = go_all[:, head * HD : (head + 1) * HD]
        out = out_all[:, head * HD : (head + 1) * HD]
        delta = jnp.sum(go.astype(jnp.float32) * out, axis=1, keepdims=True)
        score = dot(q, k, ((1,), (1,))) * scale
        probs = jnp.exp(jnp.where(allowed, score, MASKED) - lse_all[:, head : head + 1])
        dv = dv + dot(probs.astype(jnp.bfloat16), go, ((0,), (0,)))
        prob_grad = dot(go, v, ((1,), (1,)))
        score_grad = (probs * (prob_grad - delta)).astype(jnp.bfloat16)
        dq.append(dot(score_grad, k) * scale)
        dk = dk + dot(score_grad, q, ((0,), (0,)))
    dq_ref[...] = jnp.concatenate(dq, axis=1).reshape(dq_ref.shape)
    dkv_ref[...] = jnp.concatenate([dk * scale, dv], axis=1).reshape(dkv_ref.shape)


def attend_back(info, queries, kv, out_grads, out, lse):
    blocks, rows, local, width = queries.shape
    parts = kv.shape[0]
    keys = parts * blocks * local
    group = width // HD
    wide = pl.BlockSpec((blocks, 1, local, width), lambda r: (0, r, 0, 0))
    kv_spec = pl.BlockSpec((parts, blocks, 1, local, 2 * HD), lambda r: (0, 0, r, 0, 0))
    return pl.pallas_call(
        functools.partial(attend_back_kernel, local, keys, group),
        grid=(rows,),
        out_shape=(
            jax.ShapeDtypeStruct(queries.shape, jnp.float32),
            jax.ShapeDtypeStruct(kv.shape, jnp.float32),
        ),
        in_specs=[
            pl.BlockSpec(memory_space=pltpu.SMEM),
            wide,
            kv_spec,
            wide,
            wide,
            pl.BlockSpec((blocks, 1, local, group), lambda r: (0, r, 0, 0)),
        ],
        out_specs=(wide, kv_spec),
        compiler_params=pltpu.CompilerParams(vmem_limit_bytes=VMEM),
        cost_estimate=pl.CostEstimate(
            flops=20 * rows * blocks * local * keys * width,
            bytes_accessed=rows * blocks * local * width * 16,
            transcendentals=rows * blocks * local * keys * group,
        ),
        name="attend_back",
    )(info, queries, kv, out_grads, out, lse)


def bits_of(size):
    return [1 << b for b in range(size.bit_length() - 1)]


def spread_weight(shard, axis, place):
    dp, high, low, dp_size, high_size = place
    other = 1 - axis
    block = shard.shape[axis]
    width = shard.shape[other] // SQUARE
    pieces = [cut(shard, low * width, width, other)]
    for mask in range(1, SQUARE):
        pieces.append(swap(cut(shard, (low ^ mask) * width, width, other), "seq", mask))
    shape = [0, 0]
    shape[axis], shape[other] = SQUARE * block, width
    square = jnp.zeros(shape, shard.dtype)
    for mask in range(SQUARE):
        square = put(square, pieces[mask], (low ^ mask) * block, axis)
    parts = {(0, 0): square}
    for bit in bits_of(high_size):
        for (a, b) in list(parts):
            parts[a, b ^ bit] = swap(parts[a, b], "seq", SQUARE * bit)
    for bit in bits_of(dp_size):
        for (a, b) in list(parts):
            parts[a ^ bit, b] = swap(parts[a, b], "dp", bit)
    shape[axis] = SQUARE * block * high_size * dp_size
    whole = jnp.zeros(shape, shard.dtype)
    for (a, b), part in parts.items():
        index = (dp ^ a) * high_size + (high ^ b)
        whole = put(whole, part, index * SQUARE * block, axis)
    return whole


def settle_grad(grad, axis, place):
    dp, high, low, dp_size, high_size = place
    other = 1 - axis
    width = grad.shape[other]
    kept = grad
    for index, size, name, unit in ((dp, dp_size, "dp", 1), (high, high_size, "seq", SQUARE)):
        for bit in reversed(bits_of(size)):
            half = kept.shape[axis] // 2
            mine = (index // bit) % 2
            sent = cut(kept, (1 - mine) * half, half, axis).astype(jnp.bfloat16)
            kept = cut(kept, mine * half, half, axis) + swap(sent, name, unit * bit).astype(
                jnp.float32
            )
    block = kept.shape[axis] // SQUARE
    shape = [0, 0]
    shape[axis], shape[other] = block, SQUARE * width
    whole = jnp.zeros(shape, jnp.float32)
    whole = put(whole, cut(kept, low * block, block, axis), low * width, other)
    for mask in range(1, SQUARE):
        sent = cut(kept, (low ^ mask) * block, block, axis).astype(jnp.bfloat16)
        got = swap(sent, "seq", mask).astype(jnp.float32)
        whole = put(whole, got, (low ^ mask) * width, other)
    return whole


def gather_square(own, core):
    tokens, width = own.shape
    half = width // 2
    mine = cut(own, core * half, half, 1)
    got = jnp.concatenate([swap(mine, "seq", mask) for mask in range(1, SQUARE)], axis=0)
    across = swap(got, "mp", 1)
    first = jnp.where(core == 0, got, across)
    second = jnp.where(core == 0, across, got)
    return jnp.concatenate([own, jnp.concatenate([first, second], axis=1)], axis=0)


def scatter_square(partial, core):
    tokens, width = partial.shape[0] // SQUARE, partial.shape[1]
    half = width // 2
    kept = cut(partial, core * half, half, 1)
    sent = cut(partial, (1 - core) * half, half, 1).astype(jnp.bfloat16)
    kept = kept + swap(sent, "mp", 1).astype(jnp.float32)
    total = kept[:tokens]
    for mask in range(1, SQUARE):
        part = kept[mask * tokens : (mask + 1) * tokens].astype(jnp.bfloat16)
        total = total + swap(part, "seq", mask).astype(jnp.float32)
    mine = total.astype(jnp.bfloat16)
    across = swap(mine, "mp", 1)
    return jnp.concatenate(
        [jnp.where(core == 0, mine, across), jnp.where(core == 0, across, mine)], axis=1
    ).astype(jnp.float32)


MESH = pl.DeviceIdType.MESH


class Links:
    def __init__(self, send_sem, recv_sem, local_sem, high_size):
        self.send_sem, self.recv_sem, self.local_sem = send_sem, recv_sem, local_sem
        self.x, self.seq, self.core = (lax.axis_index(a) for a in ("dp", "seq", "mp"))
        self.high_size = high_size
        self.low, self.high = self.seq % SQUARE, self.seq // SQUARE
        self.count = self.local_count = 0
        self.sent = []

    def to(self, dx=0, dh=0, dl=0, dc=0):
        seq = ((self.high + dh) % self.high_size) * SQUARE + (self.low + dl) % SQUARE
        return ((self.x + dx) % 2, seq, (self.core + dc) % 2)

    def copy(self, src, dst, **step):
        k = self.count
        self.count += 1
        made = pltpu.make_async_remote_copy(
            src_ref=src,
            dst_ref=dst,
            send_sem=self.send_sem.at[k],
            recv_sem=self.recv_sem.at[k],
            device_id=self.to(**step),
            device_id_type=MESH,
        )
        made.start()
        self.sent.append(made)
        return made

    def local(self, src, dst):
        k = self.local_count
        self.local_count += 1
        made = pltpu.make_async_copy(src, dst, self.local_sem.at[k])
        made.start()
        return made

    def greet(self, steps):
        barrier = pltpu.get_barrier_semaphore()
        for step in steps:
            pl.semaphore_signal(barrier, inc=1, device_id=self.to(**step), device_id_type=MESH)
        pl.semaphore_wait(barrier, len(steps))

    def left(self, copies):
        for made in copies:
            made.wait_send()
            self.sent = [one for one in self.sent if one is not made]

    def finish(self):
        for made in self.sent:
            made.wait_send()


def arrived(copies):
    for made in copies:
        made.wait_recv()


class Weight:
    def __init__(self, links, slice_of, spot):
        self.links, self.spot = links, spot
        l = links
        self.own = l.local(slice_of(l.low), spot(l.x, l.high, l.low, 1))
        self.near, self.far = [], []
        for dh in range(2):
            for dl in range(SQUARE):
                if dh or dl:
                    made = l.copy(
                        slice_of((l.low + dl) % SQUARE),
                        spot(l.x, l.high, l.low, 1),
                        dh=dh,
                        dl=dl,
                    )
                    (self.far if dh else self.near).append(made)

    def pass_near(self):
        self.own.wait()
        arrived(self.near)
        l = self.links
        part = self.spot(l.x, l.high, 0, SQUARE)
        self.across = [l.copy(part, part, dx=1)]

    def pass_far(self):
        arrived(self.far)
        l = self.links
        part = self.spot(l.x, 1 - l.high, 0, SQUARE)
        self.across.append(l.copy(part, part, dx=1))

    def wait(self):
        arrived(self.across)


def gather_rows(l, everyone, count, half_src):
    return [
        l.copy(half_src, everyone(l.core, l.low), dl=dl) for dl in range(1, SQUARE)
    ]


def gather_across(l, everyone, pushed):
    handed = []
    for dl in range(1, SQUARE):
        pushed[dl - 1].wait_recv()
        block = everyone(l.core, (l.low + SQUARE - dl) % SQUARE)
        handed.append(l.copy(block, block, dc=1))
    return handed


def reduce_square(l, part, send_core, recv_core, send_block, recv_block, both):
    handed = []
    for j in range(SQUARE):
        send_core[j] = part(j, 1 - l.core).astype(jnp.bfloat16)
        handed.append(l.copy(send_core.at[j], recv_core.at[j], dc=1))
    arrived(handed)
    pushed = []
    for dl in range(1, SQUARE):
        j = (l.low + dl) % SQUARE
        total = part(j, l.core) + recv_core[j].astype(jnp.float32)
        send_block[dl] = total.astype(jnp.bfloat16)
        pushed.append(l.copy(send_block.at[dl], recv_block.at[dl], dl=dl))
    total = part(l.low, l.core) + recv_core[l.low].astype(jnp.float32)
    for dl in range(1, SQUARE):
        pushed[dl - 1].wait_recv()
        total = total + recv_block[dl].astype(jnp.float32)
    both[l.core] = total.astype(jnp.bfloat16)
    l.copy(both.at[l.core], both.at[l.core], dc=1).wait_recv()


def roll_heads(value):
    width = value.shape[1]
    lane = lax.broadcasted_iota(jnp.int32, value.shape, 1)
    left = pltpu.roll(value, width - HD // 2, 1)
    right = pltpu.roll(value, HD // 2, 1)
    return jnp.where(lane % HD < HD // 2, left, right)


def allowed_keys(l, ends, row, span, keys):
    def segment_of(place):
        total = jnp.zeros_like(place)
        for doc in range(4):
            total = total + (place >= ends[row * 4 + doc]).astype(jnp.int32)
        return total

    query = l.high * span + lax.broadcasted_iota(jnp.int32, (span, 1), 0)
    key = lax.broadcasted_iota(jnp.int32, (1, keys), 1)
    return (segment_of(query) == segment_of(key)) & (query >= key)


def front_kernel(
    sizes,
    ends,
    x_in,
    g_in,
    qkv_in,
    gain_in,
    wo_in,
    wg_in,
    wu_in,
    wd_in,
    cos_in,
    sin_in,
    qkv_out,
    wo_out,
    wg_out,
    wu_out,
    wd_out,
    gain_out,
    normed_one_out,
    q_out,
    kv_out,
    attn_out,
    residual_out,
    normed_two_out,
    g_out,
    x_all,
    normed,
    wqkv,
    wo,
    gains,
    gain_rows,
    cos,
    sin,
    q,
    kv,
    attn,
    low_attn,
    send_core,
    recv_core,
    send_block,
    recv_block,
    both,
    residual,
    normed_two,
    send_sem,
    recv_sem,
    local_sem,
):
    rows, local, model, high_size = sizes
    own = rows * local
    tokens = SQUARE * own
    half = model // 2
    block = qkv_in.shape[1]
    heads = q.shape[2] // HD
    span = SQUARE * local
    keys = high_size * span
    l = Links(send_sem, recv_sem, local_sem, high_size)
    near = [dict(dl=dl) for dl in range(1, SQUARE)]
    far = [dict(dh=1, dl=dl) for dl in range(SQUARE)]
    l.greet(near + far + [dict(dx=1), dict(dc=1)])

    def row_spot(ref):
        def spot(x, h, low, n):
            start = ((x * high_size + h) * SQUARE + low) * block
            return ref.at[pl.ds(pl.multiple_of(start, block), n * block)]

        return spot

    def block_spot(ref):
        return lambda x, h, low, n: ref.at[pl.ds((x * high_size + h) * SQUARE + low, n)]

    def half_spot(ref):
        def spot(x, h, low, n):
            start = pl.multiple_of((h * SQUARE + low) * block, block)
            return ref.at[x, :, pl.ds(start, n * block)]

        return spot

    def column_spot(ref):
        def spot(x, h, low, n):
            start = ((x * high_size + h) * SQUARE + low) * block
            return ref.at[:, pl.ds(pl.multiple_of(start, block), n * block)]

        return spot

    def columns(ref, width):
        return lambda j: ref.at[:, pl.ds(pl.multiple_of(j * width, width), width)]

    def lines(ref, width):
        return lambda j: ref.at[pl.ds(pl.multiple_of(j * width, width), width)]

    def x_spot(side, low):
        return x_all.at[side, pl.ds(pl.multiple_of(low * own, own), own)]

    def g_spot(side, low):
        return g_out.at[
            pl.ds(pl.multiple_of(low * own, own), own),
            pl.ds(pl.multiple_of(side * half, half), half),
        ]

    def normed_two_spot(side, low):
        return normed_two.at[side, pl.ds(pl.multiple_of(low * own, own), own)]

    def side_of(ref, side):
        return ref.at[:, pl.ds(pl.multiple_of(side * half, half), half)]

    loads = [l.local(side_of(x_in, side), x_spot(side, l.low)) for side in range(2)]
    loads += [l.local(cos_in, cos), l.local(sin_in, sin)]
    w_gain = Weight(l, lambda j: gain_in.at[pl.ds(0, 1)], block_spot(gains))
    w_qkv = Weight(l, lambda j: qkv_in.at[j], row_spot(wqkv))
    x_pushed = gather_rows(l, x_spot, 0, side_of(x_in, l.core))
    w_o = Weight(l, lines(wo_in, wo.shape[1]), half_spot(wo))
    w_gate = Weight(l, columns(wg_in, wg_out.shape[1]), row_spot(wg_out))

    w_gain.pass_near()
    w_qkv.pass_near()
    w_gain.pass_far()
    w_qkv.pass_far()
    x_handed = gather_across(l, x_spot, x_pushed)
    w_o.pass_near()
    w_o.pass_far()
    w_up = Weight(l, columns(wu_in, wu_out.shape[1]), row_spot(wu_out))
    for made in loads:
        made.wait()
    w_gain.wait()
    for b in range(gains.shape[0]):
        tile = gains[b].astype(jnp.float32)
        gain_rows[0:1, b * block : (b + 1) * block] = tile[0:1]
        gain_rows[1:2, b * block : (b + 1) * block] = tile[1:2]
    arrived(x_handed)

    step = 128

    def norm_step(i, carry):
        at = pl.ds(pl.multiple_of(i * step, step), step)
        first, second = x_all[0, at].astype(jnp.float32), x_all[1, at].astype(jnp.float32)
        total = jnp.sum(first * first, axis=1, keepdims=True)
        total = total + jnp.sum(second * second, axis=1, keepdims=True)
        scale = lax.rsqrt(total / model + EPSILON)
        normed[at, :half] = (first * scale * gain_rows[0:1, :half]).astype(jnp.bfloat16)
        normed[at, half:] = (second * scale * gain_rows[0:1, half:]).astype(jnp.bfloat16)
        return carry

    lax.fori_loop(0, tokens // step, norm_step, 0)
    stores = [l.local(normed, normed_one_out)]
    w_qkv.wait()
    stores += [l.local(wqkv, qkv_out), l.local(gain_rows, gain_out)]

    def project_step(i, carry):
        at = pl.ds(pl.multiple_of(i * local, local), local)
        pre = dot(normed[at], wqkv[...])
        times = heads // 2
        cos_all = jnp.concatenate([cos[at, : 2 * HD]] * times + [cos[at, 2 * HD :]], axis=1)
        sin_all = jnp.concatenate([sin[at, : 2 * HD]] * times + [sin[at, 2 * HD :]], axis=1)
        turned = pre * cos_all + roll_heads(pre) * sin_all
        spot = pl.ds(pl.multiple_of((i // rows) * local, local), local)
        q[i % rows, spot] = (turned[:, : heads * HD].astype(jnp.bfloat16) * HD ** (-0.5)).astype(
            jnp.bfloat16
        )
        kv[l.high, i % rows, spot] = turned[:, heads * HD :].astype(jnp.bfloat16)
        return carry

    lax.fori_loop(0, SQUARE * rows, project_step, 0)
    kv_copy = l.copy(kv.at[l.high], kv.at[l.high], dh=1)
    stores.append(l.local(q, q_out))
    w_gate.pass_near()
    kv_copy.wait_recv()
    stores.append(l.local(kv, kv_out))

    def attend_row(r, carry):
        allowed = allowed_keys(l, ends, r, span, keys)
        kv_row = kv[:, r].reshape(keys, 2 * HD)
        k, v = kv_row[:, :HD], kv_row[:, HD:]
        q_row = q[r]
        outs = []
        for head in range(heads):
            score = dot(q_row[:, head * HD : (head + 1) * HD], k, ((1,), (1,)))
            score = jnp.where(allowed, score, MASKED)
            top = jnp.max(score, axis=1, keepdims=True)
            grown = jnp.exp(score - top)
            total = jnp.sum(grown, axis=1, keepdims=True)
            probs = (grown * (1.0 / total)).astype(jnp.bfloat16)
            outs.append(dot(probs, v))
        out = jnp.concatenate(outs, axis=1)
        for j in range(SQUARE):
            at = pl.ds(pl.multiple_of(j * own + r * local, local), local)
            part = out[j * local : (j + 1) * local]
            attn[at] = part
            low_attn[at] = part.astype(jnp.bfloat16)
        return carry

    lax.fori_loop(0, rows, attend_row, 0)
    stores.append(l.local(attn, attn_out))
    w_gate.pass_far()
    w_down = Weight(l, lines(wd_in, wd_out.shape[0]), column_spot(wd_out))
    w_o.wait()
    stores.append(l.local(wo, wo_out))

    def project_out(j, side):
        at = pl.ds(pl.multiple_of(j * own, own), own)
        return dot(low_attn[at], wo[side])

    reduce_square(l, project_out, send_core, recv_core, send_block, recv_block, both)
    at_own = pl.ds(pl.multiple_of(l.low * own, own), own)
    total = jnp.zeros((own, 1), jnp.float32)
    for side in range(2):
        value = x_all[side, at_own].astype(jnp.float32) + both[side].astype(jnp.float32)
        residual[:, side * half : (side + 1) * half] = value
        total = total + jnp.sum(value * value, axis=1, keepdims=True)
    scale = lax.rsqrt(total / model + EPSILON)
    for side in range(2):
        at = slice(side * half, (side + 1) * half)
        normed_two[side, at_own] = (residual[:, at] * scale * gain_rows[1:2, at]).astype(
            jnp.bfloat16
        )
    stores.append(l.local(residual, residual_out))
    pushed = gather_rows(l, normed_two_spot, 0, normed_two_spot(l.core, l.low))
    loads = [l.local(side_of(g_in, side), g_spot(side, l.low)) for side in range(2)]
    g_pushed = gather_rows(l, g_spot, 0, side_of(g_in, l.core))
    w_up.pass_near()
    handed = gather_across(l, normed_two_spot, pushed)
    arrived(handed)
    for side in range(2):
        stores.append(l.local(normed_two.at[side], side_of(normed_two_out, side)))
    w_up.pass_far()
    g_handed = gather_across(l, g_spot, g_pushed)
    w_down.pass_near()
    w_down.pass_far()
    arrived(g_handed)
    for weight in (w_gate, w_up, w_down):
        weight.wait()
    for made in loads + stores:
        made.wait()
    l.finish()


def front(sizes, ends, x, g, qkv, gain, wo, wg, wu, wd, cos, sin):
    rows, local, model, high_size = sizes
    own = rows * local
    tokens = SQUARE * own
    half = model // 2
    heads = wo.shape[0] // SQUARE // HD
    width = qkv.shape[2]
    ff = wg.shape[1] // SQUARE
    blocks = model // qkv.shape[1]
    span = SQUARE * local
    low, f32 = jnp.bfloat16, jnp.float32
    shape = jax.ShapeDtypeStruct
    outs = (
        shape((model, width), low),
        shape((2, heads * HD, half), low),
        shape((model, ff), low),
        shape((model, ff), low),
        shape((ff, model), low),
        shape((8, model), f32),
        shape((tokens, model), low),
        shape((rows, span, heads * HD), low),
        shape((high_size, rows, span, 2 * HD), low),
        shape((tokens, heads * HD), f32),
        shape((own, model), f32),
        shape((tokens, model), low),
        shape((tokens, model), low),
    )
    anywhere = pl.BlockSpec(memory_space=pl.ANY)
    vmem = pltpu.VMEM
    return pl.pallas_call(
        functools.partial(front_kernel, sizes),
        out_shape=outs,
        in_specs=[pl.BlockSpec(memory_space=pltpu.SMEM)] + [anywhere] * 10,
        out_specs=[anywhere] * len(outs),
        scratch_shapes=[
            vmem((2, tokens, half), low),
            vmem((tokens, model), low),
            vmem((model, width), low),
            vmem((2, heads * HD, half), low),
            vmem((blocks,) + gain.shape[1:], low),
            vmem((8, model), f32),
            vmem((tokens, 4 * HD), f32),
            vmem((tokens, 4 * HD), f32),
            vmem((rows, span, heads * HD), low),
            vmem((high_size, rows, span, 2 * HD), low),
            vmem((tokens, heads * HD), f32),
            vmem((tokens, heads * HD), low),
            vmem((SQUARE, own, half), low),
            vmem((SQUARE, own, half), low),
            vmem((SQUARE, own, half), low),
            vmem((SQUARE, own, half), low),
            vmem((2, own, half), low),
            vmem((own, model), f32),
            vmem((2, tokens, half), low),
            pltpu.SemaphoreType.DMA((96,)),
            pltpu.SemaphoreType.DMA((96,)),
            pltpu.SemaphoreType.DMA((32,)),
        ],
        compiler_params=pltpu.CompilerParams(
            collective_id=0, has_side_effects=True, vmem_limit_bytes=VMEM
        ),
        name="front",
    )(ends, x, g, qkv, gain, wo, wg, wu, wd, cos, sin)


class Grad:
    def __init__(self, links, half_of, kept, crossed, block_of, landed):
        self.links, self.kept, self.crossed = links, kept, crossed
        self.block_of, self.landed = block_of, landed
        self.placed = False
        l = links
        self.own = l.local(half_of(l.x), kept) if half_of else None
        if half_of:
            self.cross = l.copy(half_of(1 - l.x), crossed, dx=1)

    def deal(self):
        l = self.links
        if self.own is not None:
            self.own.wait()
        self.cross.wait_recv()
        kept, crossed = self.kept, self.crossed
        lines = kept.shape[0]
        step = min(128, lines)

        def add(i, carry):
            at = pl.ds(pl.multiple_of(i * step, step), step)
            kept[at] = (kept[at].astype(jnp.float32) + crossed[at].astype(jnp.float32)).astype(
                jnp.bfloat16
            )
            return carry

        lax.fori_loop(0, lines // step, add, 0)
        self.dealt = []
        for dh in range(2):
            for dl in range(SQUARE):
                if dh or dl:
                    block = self.block_of((l.high + dh) % 2, (l.low + dl) % SQUARE)
                    self.dealt.append(
                        l.copy(block, self.landed.at[l.high, l.low], dh=dh, dl=dl)
                    )
        mine = self.block_of(l.high, l.low)
        self.mine = l.local(mine, self.landed.at[l.high, l.low])

    def sum(self, stage, out_of):
        l = self.links
        if not self.placed:
            self.mine.wait()
        arrived(self.dealt)
        stores = []
        landed = self.landed
        for j in range(SQUARE):
            if j >= 2:
                stores[j - 2].wait()
            stage[j % 2] = landed[0, j].astype(jnp.float32) + landed[1, j].astype(jnp.float32)
            stores.append(l.local(stage.at[j % 2], out_of(j)))
        return stores[2:]


def back_kernel(
    sizes,
    ends,
    x_in,
    g_in,
    residual_in,
    gain_in,
    normed_two_part,
    layer_part,
    dwg_in,
    dwu_in,
    dwd_in,
    qkv_in,
    wo_in,
    normed_one_in,
    q_in,
    kv_in,
    attn_in,
    cos_in,
    sin_in,
    layer_out,
    input_out,
    dqkv_out,
    dwo_out,
    dwg_out,
    dwu_out,
    dwd_out,
    gains_out,
    kept_g,
    kept_d,
    cross_g,
    cross_d,
    land_g,
    land_u,
    land_d,
    kept_q,
    cross_q,
    land_q,
    kept_o,
    cross_o,
    land_o,
    send_q,
    send_o,
    stage_q,
    stage_o,
    stage,
    stage_d,
    own_a,
    recv_core,
    recv_block,
    recv_block_b,
    both,
    both_b,
    x_own,
    g_own,
    residual,
    gain_rows,
    low_all,
    wqkv,
    wo,
    q,
    kv,
    attn,
    attn_grad,
    dkv,
    dkv_send,
    dkv_recv,
    dqkv,
    cos,
    sin,
    gain_send,
    gain_recv,
    out_low,
    gain_sum,
    send_sem,
    recv_sem,
    local_sem,
):
    rows, local, model, high_size = sizes
    own = rows * local
    tokens = SQUARE * own
    half = model // 2
    block = x_own.shape[1] // 16
    heads = q.shape[2] // HD
    span = SQUARE * local
    keys = high_size * span
    f32, b16 = jnp.float32, jnp.bfloat16
    l = Links(send_sem, recv_sem, local_sem, high_size)
    steps = [
        dict(dx=dx, dh=dh, dl=dl)
        for dx in range(2)
        for dh in range(2)
        for dl in range(SQUARE)
        if dx or dh or dl
    ]
    l.greet(steps + [dict(dc=1)])

    def side_of(ref, side):
        return ref.at[:, pl.ds(pl.multiple_of(side * half, half), half)]

    def row_half(ref):
        return lambda x: ref.at[pl.ds(pl.multiple_of(x * half, half), half)]

    def row_block(ref):
        def at(h, low):
            start = pl.multiple_of((h * SQUARE + low) * block, block)
            return ref.at[pl.ds(start, block)]

        return at

    def column_block(ref):
        def at(h, low):
            start = pl.multiple_of((h * SQUARE + low) * block, block)
            return ref.at[:, pl.ds(start, block)]

        return at

    def block_at(j):
        return pl.ds(pl.multiple_of(j * own, own), own)

    def part_at(ref, j, side):
        return ref.at[block_at(j), pl.ds(pl.multiple_of(side * half, half), half)]

    handed = [
        l.copy(part_at(normed_two_part, j, 1 - l.core), recv_core.at[j], dc=1)
        for j in range(SQUARE)
    ]
    owned = [l.local(part_at(normed_two_part, j, l.core), own_a.at[j]) for j in range(SQUARE)]
    loads = [
        l.local(residual_in, residual),
        l.local(gain_in, gain_rows),
        l.local(g_in, g_own),
    ]
    grad_d = Grad(l, lambda x: side_of(dwd_in, x), kept_d, cross_d, column_block(kept_d), land_d)
    grad_g = Grad(l, row_half(dwg_in), kept_g, cross_g, row_block(kept_g), land_g)
    later = [
        l.local(x_in, x_own),
        l.local(wo_in, wo),
        l.local(attn_in, attn),
        l.local(q_in, q),
        l.local(kv_in, kv),
        l.local(qkv_in, wqkv),
        l.local(cos_in, cos),
        l.local(sin_in, sin),
    ]

    def own_part(j):
        return own_a[j].astype(f32)

    def push_blocks(part, recv_b):
        pushed = []
        for dl in range(1, SQUARE):
            j = (l.low + dl) % SQUARE
            total = part(j) + recv_core[j].astype(f32)
            own_a[j] = total.astype(b16)
            pushed.append(l.copy(own_a.at[j], recv_b.at[dl - 1], dl=dl))
        return pushed

    def settle_block(part, recv_b, pushed, into):
        total = part(l.low) + recv_core[l.low].astype(f32)
        for dl in range(1, SQUARE):
            pushed[dl - 1].wait_recv()
            total = total + recv_b[dl - 1].astype(f32)
        into[l.core] = total.astype(b16)
        return l.copy(into.at[l.core], into.at[l.core], dc=1)

    def norm_back(value_of, gain_row, grads):
        squares = jnp.zeros((own, 1), f32)
        inner = jnp.zeros((own, 1), f32)
        for side in range(2):
            at = slice(side * half, (side + 1) * half)
            value = value_of(side)
            squares = squares + jnp.sum(value * value, axis=1, keepdims=True)
            weighted = grads[side].astype(f32) * gain_rows[gain_row : gain_row + 1, at]
            inner = inner + jnp.sum(weighted * value, axis=1, keepdims=True)
        scale = lax.rsqrt(squares / model + EPSILON)
        pull = scale * scale * scale * (inner / model)
        outs = []
        for side in range(2):
            at = slice(side * half, (side + 1) * half)
            value = value_of(side)
            grad = grads[side].astype(f32)
            summed = jnp.sum(grad * (value * scale), axis=0, keepdims=True)
            for b in range(half // block):
                gain_send[gain_row, side * (half // block) + b, 0:1] = summed[
                    :, b * block : (b + 1) * block
                ]
            weighted = grad * gain_rows[gain_row : gain_row + 1, at]
            outs.append(weighted * scale - value * pull)
        return outs

    def push_gains(gain_row):
        me = (l.x * 2 + l.high) * SQUARE + l.low
        made = []
        for step in steps:
            to = ((l.x + step["dx"]) % 2 * 2 + (l.high + step["dh"]) % 2) * SQUARE + (
                l.low + step["dl"]
            ) % SQUARE
            made.append(l.copy(gain_send.at[gain_row, to], gain_recv.at[gain_row, me], **step))
        return made, l.local(gain_send.at[gain_row, me], gain_recv.at[gain_row, me])

    for made in owned:
        made.wait()
    arrived(handed)

    pushed = push_blocks(own_part, recv_block)
    for made in loads:
        made.wait()
    swapped = settle_block(own_part, recv_block, pushed, both)
    swapped.wait_recv()
    l.left(pushed + [swapped])
    outs = norm_back(
        lambda side: residual[:, side * half : (side + 1) * half], 1, [both[0], both[1]]
    )
    for side in range(2):
        at = slice(side * half, (side + 1) * half)
        value = g_own[:, at].astype(f32) + outs[side]
        residual[:, at] = value
        low_all[side, block_at(l.low)] = value.astype(b16)

    def low_spot(side, low):
        return low_all.at[side, block_at(low)]

    low_pushed = gather_rows(l, low_spot, 0, low_spot(l.core, l.low))
    ffn_gains = push_gains(1)
    handed_b = [
        l.copy(part_at(layer_part, j, 1 - l.core), recv_core.at[j], dc=1) for j in range(SQUARE)
    ]
    owned = [l.local(part_at(layer_part, j, l.core), own_a.at[j]) for j in range(SQUARE)]
    for made in later:
        made.wait()
    low_handed = gather_across(l, low_spot, low_pushed)
    grad_d.deal()
    arrived(low_handed)

    def out_grad_step(j, carry):
        at = block_at(j)
        rows_at = attn[at].astype(b16)
        low_out = dot(low_all[0, at], wo[0], ((1,), (1,)))
        low_out = (low_out + dot(low_all[1, at], wo[1], ((1,), (1,)))).astype(b16)
        for r in range(rows):
            spot = pl.ds(pl.multiple_of(j * local, local), local)
            attn_grad[r, spot] = low_out[r * local : (r + 1) * local]
        out_low[at] = rows_at
        return carry

    lax.fori_loop(0, SQUARE, out_grad_step, 0)
    send_o[...] = dot(out_low[...], low_all[1 - l.x], ((0,), (0,))).astype(b16)
    grad_o = Grad(l, None, kept_o, cross_o, column_block(kept_o), land_o)
    grad_o.cross = l.copy(send_o, cross_o, dx=1)
    kept_o[...] = dot(out_low[...], low_all[l.x], ((0,), (0,))).astype(b16)

    for made in owned:
        made.wait()
    arrived(handed_b)
    pushed_b = push_blocks(own_part, recv_block_b)

    def attend_row(r, carry):
        allowed = allowed_keys(l, ends, r, span, keys)
        kv_row = kv[:, r].reshape(keys, 2 * HD)
        k, v = kv_row[:, :HD], kv_row[:, HD:]
        q_row, go_row = q[r], attn_grad[r]
        out_row = jnp.concatenate(
            [
                attn[pl.ds(pl.multiple_of(j * own + r * local, local), local)]
                for j in range(SQUARE)
            ],
            axis=0,
        )
        grads = []
        dk = jnp.zeros((keys, HD), f32)
        dv = jnp.zeros((keys, HD), f32)
        for head in range(heads):
            at = slice(head * HD, (head + 1) * HD)
            qh, go = q_row[:, at], go_row[:, at]
            delta = jnp.sum(go.astype(f32) * out_row[:, at], axis=1, keepdims=True)
            score = jnp.where(allowed, dot(qh, k, ((1,), (1,))), MASKED)
            top = jnp.max(score, axis=1, keepdims=True)
            grown = jnp.exp(score - top)
            probs = grown * (1.0 / jnp.sum(grown, axis=1, keepdims=True))
            dv = dv + dot(probs.astype(b16), go, ((0,), (0,)))
            pull = dot(go, v, ((1,), (1,)))
            score_grad = (probs * (pull - delta)).astype(b16)
            grads.append(dot(score_grad, k) * HD ** (-0.5))
            dk = dk + dot(score_grad, qh, ((0,), (0,)))
        turned = jnp.concatenate(grads, axis=1)
        for j in range(SQUARE):
            at = pl.ds(pl.multiple_of(j * own + r * local, local), local)
            value = turned[j * local : (j + 1) * local]
            cos_q = jnp.concatenate([cos[at, : 2 * HD]] * (heads // 2), axis=1)
            sin_q = jnp.concatenate([sin[at, : 2 * HD]] * (heads // 2), axis=1)
            dqkv[at, : heads * HD] = (value * cos_q - roll_heads(value) * sin_q).astype(b16)
        both_kv = jnp.concatenate([dk, dv], axis=1)
        for part in range(high_size):
            dkv[part, r] = both_kv[part * span : (part + 1) * span]
        return carry

    lax.fori_loop(0, 1, attend_row, 0)
    grad_g.deal()
    lax.fori_loop(1, rows, attend_row, 0)
    dkv_send[...] = dkv[1 - l.high].astype(b16)
    dkv_copy = l.copy(dkv_send, dkv_recv, dh=1)
    l.left(low_pushed + low_handed)
    normed = l.local(normed_one_in.at[:, pl.ds(0, half)], low_all.at[0])
    normed_2 = l.local(normed_one_in.at[:, pl.ds(half, half)], low_all.at[1])
    grad_o.deal()
    l.left(grad_d.dealt)
    grad_d.mine.wait()
    grad_d.placed = True
    grad_u = Grad(l, row_half(dwu_in), kept_d, cross_d, row_block(kept_d), land_u)
    both_b_copy = settle_block(own_part, recv_block_b, pushed_b, both_b)
    dkv_copy.wait_recv()

    def unrotate_step(i, carry):
        at = pl.ds(pl.multiple_of(i * local, local), local)
        spot = pl.ds(pl.multiple_of((i // rows) * local, local), local)
        kv_sum = dkv[l.high, i % rows, spot] + dkv_recv[i % rows, spot].astype(f32)
        turned = kv_sum * cos[at, 2 * HD :] - roll_heads(kv_sum) * sin[at, 2 * HD :]
        dqkv[at, heads * HD :] = turned.astype(b16)
        return carry

    lax.fori_loop(0, SQUARE * rows, unrotate_step, 0)

    def project_back(j, side):
        weight = wqkv[pl.ds(pl.multiple_of(side * half, half), half)]
        return dot(dqkv[block_at(j)], weight, ((1,), (1,)))

    both_b_copy.wait_recv()
    l.left(pushed_b)
    handed = []
    for j in range(SQUARE):
        own_a[j] = project_back(j, 1 - l.core).astype(b16)
        handed.append(l.copy(own_a.at[j], recv_core.at[j], dc=1))
    normed.wait()
    normed_2.wait()
    send_q[...] = dot(low_all[1 - l.x], dqkv[...], ((0,), (0,))).astype(b16)
    arrived(handed)

    def own_part_c(j):
        return project_back(j, l.core)

    l.left(handed)
    pushed = push_blocks(own_part_c, recv_block)
    grad_q = Grad(l, None, kept_q, cross_q, row_block(kept_q), land_q)
    grad_q.cross = l.copy(send_q, cross_q, dx=1)
    kept_q[...] = dot(low_all[l.x], dqkv[...], ((0,), (0,))).astype(b16)
    settle_block(own_part_c, recv_block, pushed, both).wait_recv()
    outs = norm_back(
        lambda side: x_own[:, side * half : (side + 1) * half].astype(f32),
        0,
        [both[0], both[1]],
    )
    attn_gains = push_gains(0)
    for side in range(2):
        at = slice(side * half, (side + 1) * half)
        x_own[:, at] = (residual[:, at] + outs[side]).astype(b16)
    stores = [l.local(x_own, input_out)]
    residual_load = l.local(residual_in, residual)
    grad_q.deal()
    grad_u.deal()

    def wide(out, width):
        return lambda j: out.at[:, pl.ds(j * width, width)]

    def tall(out, lines):
        return lambda j: out.at[pl.ds(j * lines, lines)]

    def flush(made):
        for one in made:
            one.wait()

    residual_load.wait()
    for side in range(2):
        at = slice(side * half, (side + 1) * half)
        g_own[:, at] = (residual[:, at] + both_b[side].astype(f32)).astype(b16)
    stores.append(l.local(g_own, layer_out))
    stores += grad_d.sum(stage_d, tall(dwd_out, stage_d.shape[1]))
    stores += grad_o.sum(stage_o, tall(dwo_out, stage_o.shape[1]))
    done_g = grad_g.sum(stage, wide(dwg_out, stage.shape[2]))
    stores += grad_q.sum(stage_q, lambda j: dqkv_out.at[j])
    for made, kept in (ffn_gains, attn_gains):
        arrived(made)
        kept.wait()
    for row in range(2):
        total = jnp.zeros((8, block), f32)
        for b in range(16):
            total = total + gain_recv[row, b]
        gain_sum[row : row + 1] = total[0:1]
    stores.append(l.local(gain_sum, gains_out))
    flush(done_g)
    stores += grad_u.sum(stage, wide(dwu_out, stage.shape[2]))
    flush(stores)
    l.finish()


def back(sizes, ends, *arrays):
    rows, local, model, high_size = sizes
    own = rows * local
    tokens = SQUARE * own
    half = model // 2
    block = model // 16
    ff = arrays[6].shape[1]
    width = arrays[9].shape[1]
    wide = width - 2 * HD
    span = SQUARE * local
    b16, f32 = jnp.bfloat16, jnp.float32
    shape = jax.ShapeDtypeStruct
    vmem = pltpu.VMEM
    outs = (
        shape((own, model), b16),
        shape((own, model), b16),
        shape((SQUARE, block, width), f32),
        shape((SQUARE * wide, block), f32),
        shape((block, SQUARE * ff), f32),
        shape((block, SQUARE * ff), f32),
        shape((SQUARE * ff, block), f32),
        shape((8, block), f32),
    )
    anywhere = pl.BlockSpec(memory_space=pl.ANY)
    scratch = [
        vmem((half, ff), b16),
        vmem((ff, half), b16),
        vmem((half, ff), b16),
        vmem((ff, half), b16),
        vmem((2, SQUARE, block, ff), b16),
        vmem((2, SQUARE, block, ff), b16),
        vmem((2, SQUARE, ff, block), b16),
        vmem((half, width), b16),
        vmem((half, width), b16),
        vmem((2, SQUARE, block, width), b16),
        vmem((wide, half), b16),
        vmem((wide, half), b16),
        vmem((2, SQUARE, wide, block), b16),
        vmem((half, width), b16),
        vmem((wide, half), b16),
        vmem((2, block, width), f32),
        vmem((2, wide, block), f32),
        vmem((2, block, ff), f32),
        vmem((2, ff, block), f32),
        vmem((SQUARE, own, half), b16),
        vmem((SQUARE, own, half), b16),
        vmem((SQUARE - 1, own, half), b16),
        vmem((SQUARE - 1, own, half), b16),
        vmem((2, own, half), b16),
        vmem((2, own, half), b16),
        vmem((own, model), b16),
        vmem((own, model), b16),
        vmem((own, model), f32),
        vmem((8, model), f32),
        vmem((2, tokens, half), b16),
        vmem((model, width), b16),
        vmem((2, wide, half), b16),
        vmem((rows, span, wide), b16),
        vmem((high_size, rows, span, 2 * HD), b16),
        vmem((tokens, wide), f32),
        vmem((rows, span, wide), b16),
        vmem((high_size, rows, span, 2 * HD), f32),
        vmem((rows, span, 2 * HD), b16),
        vmem((rows, span, 2 * HD), b16),
        vmem((tokens, width), b16),
        vmem((tokens, 4 * HD), f32),
        vmem((tokens, 4 * HD), f32),
        vmem((2, 16, 8, block), f32),
        vmem((2, 16, 8, block), f32),
        vmem((tokens, wide), b16),
        vmem((8, block), f32),
        pltpu.SemaphoreType.DMA((128,)),
        pltpu.SemaphoreType.DMA((128,)),
        pltpu.SemaphoreType.DMA((64,)),
    ]
    return pl.pallas_call(
        functools.partial(back_kernel, sizes),
        out_shape=outs,
        in_specs=[pl.BlockSpec(memory_space=pltpu.SMEM)] + [anywhere] * len(arrays),
        out_specs=[anywhere] * len(outs),
        scratch_shapes=scratch,
        compiler_params=pltpu.CompilerParams(
            collective_id=1, has_side_effects=True, vmem_limit_bytes=VMEM
        ),
        name="back",
    )(ends, *arrays)


def norm_back(values, scale, gain, grad):
    weighted = grad * gain
    gain_grad = jnp.sum(grad * values * scale, axis=0)
    inner = jnp.mean(weighted * values, axis=-1, keepdims=True)
    return (weighted * scale - values * scale**3 * inner, gain_grad)


def shards_exchanged(
    hidden_in,
    doc_lengths,
    attn_gain,
    query_weight,
    key_weight,
    value_weight,
    output_weight,
    ffn_gain,
    gate_weight,
    up_weight,
    down_weight,
    out_grad,
):
    rows, local, model = hidden_in.shape
    tokens = rows * local
    seq = lax.axis_index("seq")
    core = lax.axis_index("mp")
    low, high = seq % SQUARE, seq // SQUARE
    high_size = lax.axis_size("seq") // SQUARE
    place = (lax.axis_index("dp"), high, low, lax.axis_size("dp"), high_size)
    group = H // KVH
    span = SQUARE * local

    ends = jnp.cumsum(doc_lengths, axis=-1)
    info = jnp.concatenate([jnp.stack([low, high]), ends.reshape(-1)]).astype(jnp.int32)

    gains = lax.all_gather(jnp.stack([attn_gain, ffn_gain]), ("dp", "seq"), axis=1, tiled=True)
    gain_one, gain_two = gains[0].astype(jnp.float32), gains[1].astype(jnp.float32)

    own_in = hidden_in.reshape(tokens, model)
    all_in = gather_square(own_in, core).astype(jnp.float32)
    query_own = spread_weight(query_weight, 0, place)
    key_own = spread_weight(key_weight, 0, place)
    value_own = spread_weight(value_weight, 0, place)
    output_own = spread_weight(output_weight, 1, place)
    gate_own = spread_weight(gate_weight, 0, place)
    up_own = spread_weight(up_weight, 0, place)
    down_own = spread_weight(down_weight, 1, place)
    all_grad = gather_square(out_grad.reshape(tokens, model), core)

    blocks = low ^ jnp.arange(SQUARE, dtype=jnp.int32)
    spots = (high * span + blocks[:, None] * local + jnp.arange(local, dtype=jnp.int32)[None, :])
    reached = spots[:, None, :, None] >= ends[None, :, None, :]
    begin = jnp.max(jnp.where(reached, ends[None, :, None, :], 0), axis=-1)
    position = (spots[:, None, :] - begin).astype(jnp.float32)
    cosine, sine = rope_tables(position, HD)

    scale_one = lax.rsqrt(jnp.mean(all_in * all_in, axis=-1, keepdims=True) + EPSILON)
    normed_one = (all_in * scale_one * gain_one).astype(jnp.bfloat16)
    query_pre = dot(normed_one, query_own).reshape(SQUARE, rows, local, group, HD)
    key_pre = dot(normed_one, key_own).reshape(SQUARE, rows, local, 1, HD)
    value_pre = dot(normed_one, value_own).reshape(SQUARE, rows, local, HD)
    queries = rotate(query_pre, cosine, sine).astype(jnp.bfloat16)
    queries = queries.reshape(SQUARE, rows, local, group * HD)
    keys = rotate(key_pre, cosine, sine).astype(jnp.bfloat16).reshape(value_pre.shape)
    kv = jnp.concatenate([keys, value_pre.astype(jnp.bfloat16)], axis=-1)[None]
    for bit in bits_of(high_size):
        kv = jnp.concatenate([kv, swap(kv, "seq", SQUARE * bit)], axis=0)
    attn, lse = attend(info, queries, kv)
    attn_low = attn.reshape(SQUARE * tokens, group * HD).astype(jnp.bfloat16)
    residual = own_in.astype(jnp.float32) + scatter_square(dot(attn_low, output_own), core)

    scale_two = lax.rsqrt(jnp.mean(residual * residual, axis=-1, keepdims=True) + EPSILON)
    normed_two = (residual * scale_two * gain_two).astype(jnp.bfloat16)
    normed_two = gather_square(normed_two, core)
    gate_proj = dot(normed_two, gate_own)
    up_proj = dot(normed_two, up_own)
    sigmoid_gate = jax.nn.sigmoid(gate_proj)
    silu_gate = gate_proj * sigmoid_gate
    hidden_units = (silu_gate * up_proj).astype(jnp.bfloat16)
    hidden_grad = dot(all_grad, down_own, ((1,), (1,)))
    gate_act = (
        hidden_grad * up_proj * sigmoid_gate * (1.0 + gate_proj * (1.0 - sigmoid_gate))
    ).astype(jnp.bfloat16)
    up_act = (hidden_grad * silu_gate).astype(jnp.bfloat16)
    down_grad = settle_grad(dot(hidden_units, all_grad, ((0,), (0,))), 1, place)
    normed_two_grad = scatter_square(
        dot(gate_act, gate_own, ((1,), (1,))) + dot(up_act, up_own, ((1,), (1,))), core
    )
    layer_out = residual + scatter_square(dot(hidden_units, down_own), core)
    layer_out = layer_out.astype(jnp.bfloat16).reshape(hidden_in.shape)
    gate_grad = settle_grad(dot(normed_two, gate_act, ((0,), (0,))), 0, place)
    up_grad = settle_grad(dot(normed_two, up_act, ((0,), (0,))), 0, place)

    residual_part, ffn_gain_grad = norm_back(residual, scale_two, gain_two, normed_two_grad)
    residual_grad = out_grad.reshape(tokens, model).astype(jnp.float32) + residual_part
    residual_low = gather_square(residual_grad.astype(jnp.bfloat16), core)
    output_grad = settle_grad(dot(attn_low, residual_low, ((0,), (0,))), 1, place)
    attn_grad = dot(residual_low, output_own, ((1,), (1,))).astype(jnp.bfloat16)
    attn_grad = attn_grad.reshape(queries.shape)
    query_acc, kv_acc = attend_back(info, queries, kv, attn_grad, attn, lse)
    for bit in reversed(bits_of(high_size)):
        sent = kv_acc[bit:].astype(jnp.bfloat16)
        kv_acc = kv_acc[:bit] + swap(sent, "seq", SQUARE * bit).astype(jnp.float32)
    kv_acc = kv_acc[0]
    query_back = unrotate(query_acc.reshape(query_pre.shape), cosine, sine).astype(jnp.bfloat16)
    key_back = unrotate(kv_acc[..., :HD].reshape(key_pre.shape), cosine, sine)
    key_back = key_back.astype(jnp.bfloat16).reshape(SQUARE * tokens, HD)
    value_back = kv_acc[..., HD:].astype(jnp.bfloat16).reshape(SQUARE * tokens, HD)
    query_back = query_back.reshape(SQUARE * tokens, group * HD)
    normed_one_grad = scatter_square(
        dot(query_back, query_own, ((1,), (1,)))
        + dot(key_back, key_own, ((1,), (1,)))
        + dot(value_back, value_own, ((1,), (1,))),
        core,
    )
    query_grad = settle_grad(dot(normed_one, query_back, ((0,), (0,))), 0, place)
    key_grad = settle_grad(dot(normed_one, key_back, ((0,), (0,))), 0, place)
    value_grad = settle_grad(dot(normed_one, value_back, ((0,), (0,))), 0, place)
    own_32 = own_in.astype(jnp.float32)
    own_scale = lax.rsqrt(jnp.mean(own_32 * own_32, axis=-1, keepdims=True) + EPSILON)
    input_part, attn_gain_grad = norm_back(own_32, own_scale, gain_one, normed_one_grad)
    input_grad = (residual_grad + input_part).astype(jnp.bfloat16).reshape(hidden_in.shape)
    gain_grads = lax.psum_scatter(
        jnp.stack([attn_gain_grad, ffn_gain_grad]), ("dp", "seq"), scatter_dimension=1, tiled=True
    )
    return (
        layer_out,
        input_grad,
        gain_grads[0],
        query_grad,
        key_grad,
        value_grad,
        output_grad,
        gain_grads[1],
        gate_grad,
        up_grad,
        down_grad,
    )


def shards(
    hidden_in,
    doc_lengths,
    attn_gain,
    query_weight,
    key_weight,
    value_weight,
    output_weight,
    ffn_gain,
    gate_weight,
    up_weight,
    down_weight,
    out_grad,
):
    rows, local, model = hidden_in.shape
    tokens = rows * local
    seq = lax.axis_index("seq")
    high = seq // SQUARE
    high_size = lax.axis_size("seq") // SQUARE
    block = query_weight.shape[0]
    if block % 128 or high_size != 2 or lax.axis_size("dp") != 2:
        return shards_exchanged(
            hidden_in,
            doc_lengths,
            attn_gain,
            query_weight,
            key_weight,
            value_weight,
            output_weight,
            ffn_gain,
            gate_weight,
            up_weight,
            down_weight,
            out_grad,
        )
    group = H // KVH
    span = SQUARE * local
    width = (group + 2) * HD

    ends = jnp.cumsum(doc_lengths, axis=-1).astype(jnp.int32)
    spots = high * span + jnp.arange(span, dtype=jnp.int32).reshape(SQUARE, 1, local)
    reached = spots[..., None] >= ends[None, :, None, :]
    begin = jnp.max(jnp.where(reached, ends[None, :, None, :], 0), axis=-1)
    position = (spots - begin).astype(jnp.float32).reshape(SQUARE * tokens)
    angles = position[:, None] * inverse_freqs(HD)
    cos, sin = jnp.cos(angles), jnp.sin(angles)
    flat = jnp.zeros((SQUARE * tokens, HD), jnp.float32)
    cos = jnp.concatenate([cos] * 6 + [flat + 1.0], axis=1)
    sin = jnp.concatenate([-sin, sin] * 3 + [flat], axis=1)
    qkv_shard = jnp.concatenate(
        [
            query_weight.reshape(block, SQUARE, group * HD),
            key_weight.reshape(block, SQUARE, HD),
            value_weight.reshape(block, SQUARE, HD),
        ],
        axis=2,
    ).transpose(1, 0, 2)
    gain_shard = jnp.zeros((1, 16, block), jnp.bfloat16)
    gain_shard = gain_shard.at[0, 0].set(attn_gain).at[0, 1].set(ffn_gain)
    own_in = hidden_in.reshape(tokens, model)
    own_grad = out_grad.reshape(tokens, model)
    (
        qkv_own,
        output_own,
        gate_own,
        up_own,
        down_own,
        gains,
        normed_one,
        queries,
        kv,
        attn,
        residual,
        normed_two,
        all_grad,
    ) = front(
        (rows, local, model, high_size),
        ends.reshape(-1),
        own_in,
        own_grad,
        qkv_shard,
        gain_shard,
        output_weight,
        gate_weight,
        up_weight,
        down_weight,
        cos,
        sin,
    )
    gate_proj = dot(normed_two, gate_own)
    up_proj = dot(normed_two, up_own)
    sigmoid_gate = jax.nn.sigmoid(gate_proj)
    silu_gate = gate_proj * sigmoid_gate
    hidden_units = (silu_gate * up_proj).astype(jnp.bfloat16)
    hidden_grad = dot(all_grad, down_own, ((1,), (1,)))
    gate_act = (
        hidden_grad * up_proj * sigmoid_gate * (1.0 + gate_proj * (1.0 - sigmoid_gate))
    ).astype(jnp.bfloat16)
    up_act = (hidden_grad * silu_gate).astype(jnp.bfloat16)
    down_part = dot(hidden_units, all_grad, ((0,), (0,))).astype(jnp.bfloat16)
    gate_part = dot(normed_two, gate_act, ((0,), (0,))).astype(jnp.bfloat16)
    up_part = dot(normed_two, up_act, ((0,), (0,))).astype(jnp.bfloat16)
    normed_two_part = dot(gate_act, gate_own, ((1,), (1,))) + dot(up_act, up_own, ((1,), (1,)))
    layer_part = dot(hidden_units, down_own).astype(jnp.bfloat16)
    (
        layer_out,
        input_grad,
        qkv_grad,
        output_grad,
        gate_grad,
        up_grad,
        down_grad,
        gain_grads,
    ) = back(
        (rows, local, model, high_size),
        ends.reshape(-1),
        own_in,
        own_grad,
        residual,
        gains,
        normed_two_part.astype(jnp.bfloat16),
        layer_part,
        gate_part,
        up_part,
        down_part,
        qkv_own,
        output_own,
        normed_one,
        queries,
        kv,
        attn,
        cos,
        sin,
    )
    query_grad = qkv_grad[..., : group * HD].transpose(1, 0, 2).reshape(block, -1)
    key_grad = qkv_grad[..., group * HD : (group + 1) * HD].transpose(1, 0, 2).reshape(block, -1)
    value_grad = qkv_grad[..., (group + 1) * HD :].transpose(1, 0, 2).reshape(block, -1)
    return (
        layer_out.reshape(hidden_in.shape),
        input_grad.reshape(hidden_in.shape),
        gain_grads[0],
        query_grad,
        key_grad,
        value_grad,
        output_grad,
        gain_grads[1],
        gate_grad,
        up_grad,
        down_grad,
    )


def solution(mesh):
    return jax.shard_map(
        shards,
        mesh=mesh,
        in_specs=(
            P("dp", "seq", None),
            P("dp", None),
            P(("dp", "seq")),
            P(("dp", "seq"), "mp"),
            P(("dp", "seq"), "mp"),
            P(("dp", "seq"), "mp"),
            P("mp", ("dp", "seq")),
            P(("dp", "seq")),
            P(("dp", "seq"), "mp"),
            P(("dp", "seq"), "mp"),
            P("mp", ("dp", "seq")),
            P("dp", "seq", None),
        ),
        out_specs=(
            P("dp", "seq", None),
            P("dp", "seq", None),
            P(("dp", "seq")),
            P(("dp", "seq"), "mp"),
            P(("dp", "seq"), "mp"),
            P(("dp", "seq"), "mp"),
            P("mp", ("dp", "seq")),
            P(("dp", "seq")),
            P(("dp", "seq"), "mp"),
            P(("dp", "seq"), "mp"),
            P("mp", ("dp", "seq")),
        ),
        check_vma=False,
    )
```

```python
import functools
import math

import jax
import jax.numpy as jnp
from jax import lax
from jax.experimental import pallas as pl
from jax.experimental.pallas import tpu as pltpu
from jax.sharding import PartitionSpec as P

H = 32
KVH = 8
HD = 64
SQUARE = 4

EPSILON = 1e-05
MASKED = -1e30
ROPE_THETA = 500000.0
ROPE_FACTOR = 32.0
LOW_FACTOR = 1.0
HIGH_FACTOR = 4.0
PRIOR_CONTEXT = 8192.0
VMEM = 62 * 1024 * 1024


def inverse_freqs(head_dim):
    ladder = jnp.arange(head_dim // 2, dtype=jnp.float32)
    base = ROPE_THETA ** (-2.0 * ladder / head_dim)
    wavelen = 2.0 * math.pi / base
    smooth = (PRIOR_CONTEXT / wavelen - LOW_FACTOR) / (HIGH_FACTOR - LOW_FACTOR)
    blended = (1.0 - smooth) * base / ROPE_FACTOR + smooth * base
    low_limit = PRIOR_CONTEXT / LOW_FACTOR
    high_limit = PRIOR_CONTEXT / HIGH_FACTOR
    return jnp.where(
        wavelen < high_limit, base, jnp.where(wavelen > low_limit, base / ROPE_FACTOR, blended)
    )


def rope_tables(position, head_dim):
    angles = position[..., None] * inverse_freqs(head_dim)
    angles = jnp.concatenate([angles, angles], axis=-1)
    return (jnp.cos(angles)[..., None, :], jnp.sin(angles)[..., None, :])


def rotate(values, cosine, sine):
    middle = values.shape[-1] // 2
    turned = jnp.concatenate([-values[..., middle:], values[..., :middle]], axis=-1)
    return values * cosine + turned * sine


def unrotate(grads, cosine, sine):
    middle = grads.shape[-1] // 2
    scaled = grads * sine
    turned = jnp.concatenate([scaled[..., middle:], -scaled[..., :middle]], axis=-1)
    return grads * cosine + turned


def dot(left, right, dims=((1,), (0,))):
    return lax.dot_general(left, right, (dims, ((), ())), preferred_element_type=jnp.float32)


def swap(value, axis, mask):
    size = lax.axis_size(axis)
    return lax.ppermute(value, axis, [(i, i ^ mask) for i in range(size)])


def cut(value, start, length, axis):
    return lax.dynamic_slice_in_dim(value, start, length, axis)


def put(whole, part, start, axis):
    return lax.dynamic_update_slice_in_dim(whole, part, start, axis)


def mask_of(info, row, row_count, local, keys):
    span = SQUARE * local
    low, high = info[0], info[1]

    def place_of(index):
        block = (index // local) % SQUARE
        part = index // span
        return (high ^ part) * span + (low ^ block) * local + index % local

    def segment_of(place):
        total = jnp.zeros_like(place)
        for doc in range(4):
            total = total + (place >= info[2 + row * 4 + doc]).astype(jnp.int32)
        return total

    query = place_of(lax.broadcasted_iota(jnp.int32, (span, 1), 0))
    key = place_of(lax.broadcasted_iota(jnp.int32, (1, keys), 1))
    return (segment_of(query) == segment_of(key)) & (query >= key)


def attend_kernel(local, keys, group, info, q_ref, kv_ref, out_ref, lse_ref):
    row = pl.program_id(0)
    span = SQUARE * local
    allowed = mask_of(info, row, None, local, keys)
    kv = kv_ref[...].reshape(keys, 2 * HD)
    k, v = kv[:, :HD], kv[:, HD:]
    q_all = q_ref[...].reshape(span, group * HD)
    outs, sums = [], []
    for head in range(group):
        q = q_all[:, head * HD : (head + 1) * HD]
        score = dot(q, k, ((1,), (1,))) * HD ** (-0.5)
        score = jnp.where(allowed, score, MASKED)
        top = jnp.max(score, axis=1, keepdims=True)
        grown = jnp.exp(score - top)
        total = jnp.sum(grown, axis=1, keepdims=True)
        lse = top + jnp.log(total)
        probs = (grown * (1.0 / total)).astype(jnp.bfloat16)
        outs.append(dot(probs, v))
        sums.append(lse)
    out_ref[...] = jnp.concatenate(outs, axis=1).reshape(out_ref.shape)
    lse_ref[...] = jnp.concatenate(sums, axis=1).reshape(lse_ref.shape)


def attend(info, queries, kv):
    blocks, rows, local, width = queries.shape
    parts = kv.shape[0]
    keys = parts * blocks * local
    group = width // HD
    return pl.pallas_call(
        functools.partial(attend_kernel, local, keys, group),
        grid=(rows,),
        out_shape=(
            jax.ShapeDtypeStruct((blocks, rows, local, width), jnp.float32),
            jax.ShapeDtypeStruct((blocks, rows, local, group), jnp.float32),
        ),
        in_specs=[
            pl.BlockSpec(memory_space=pltpu.SMEM),
            pl.BlockSpec((blocks, 1, local, width), lambda r: (0, r, 0, 0)),
            pl.BlockSpec((parts, blocks, 1, local, 2 * HD), lambda r: (0, 0, r, 0, 0)),
        ],
        out_specs=(
            pl.BlockSpec((blocks, 1, local, width), lambda r: (0, r, 0, 0)),
            pl.BlockSpec((blocks, 1, local, group), lambda r: (0, r, 0, 0)),
        ),
        compiler_params=pltpu.CompilerParams(vmem_limit_bytes=VMEM),
        cost_estimate=pl.CostEstimate(
            flops=8 * rows * blocks * local * keys * width,
            bytes_accessed=rows * blocks * local * width * 8,
            transcendentals=rows * blocks * local * keys * group,
        ),
        name="attend",
    )(info, queries, kv)


def attend_back_kernel(
    local, keys, group, info, q_ref, kv_ref, go_ref, out_ref, lse_ref, dq_ref, dkv_ref
):
    row = pl.program_id(0)
    span = SQUARE * local
    allowed = mask_of(info, row, None, local, keys)
    kv = kv_ref[...].reshape(keys, 2 * HD)
    k, v = kv[:, :HD], kv[:, HD:]
    q_all = q_ref[...].reshape(span, group * HD)
    go_all = go_ref[...].reshape(span, group * HD)
    out_all = out_ref[...].reshape(span, group * HD)
    lse_all = lse_ref[...].reshape(span, group)
    dq = []
    dk = jnp.zeros((keys, HD), jnp.float32)
    dv = jnp.zeros((keys, HD), jnp.float32)
    scale = HD ** (-0.5)
    for head in range(group):
        q = q_all[:, head * HD : (head + 1) * HD]
        go = go_all[:, head * HD : (head + 1) * HD]
        out = out_all[:, head * HD : (head + 1) * HD]
        delta = jnp.sum(go.astype(jnp.float32) * out, axis=1, keepdims=True)
        score = dot(q, k, ((1,), (1,))) * scale
        probs = jnp.exp(jnp.where(allowed, score, MASKED) - lse_all[:, head : head + 1])
        dv = dv + dot(probs.astype(jnp.bfloat16), go, ((0,), (0,)))
        prob_grad = dot(go, v, ((1,), (1,)))
        score_grad = (probs * (prob_grad - delta)).astype(jnp.bfloat16)
        dq.append(dot(score_grad, k) * scale)
        dk = dk + dot(score_grad, q, ((0,), (0,)))
    dq_ref[...] = jnp.concatenate(dq, axis=1).reshape(dq_ref.shape)
    dkv_ref[...] = jnp.concatenate([dk * scale, dv], axis=1).reshape(dkv_ref.shape)


def attend_back(info, queries, kv, out_grads, out, lse):
    blocks, rows, local, width = queries.shape
    parts = kv.shape[0]
    keys = parts * blocks * local
    group = width // HD
    wide = pl.BlockSpec((blocks, 1, local, width), lambda r: (0, r, 0, 0))
    kv_spec = pl.BlockSpec((parts, blocks, 1, local, 2 * HD), lambda r: (0, 0, r, 0, 0))
    return pl.pallas_call(
        functools.partial(attend_back_kernel, local, keys, group),
        grid=(rows,),
        out_shape=(
            jax.ShapeDtypeStruct(queries.shape, jnp.float32),
            jax.ShapeDtypeStruct(kv.shape, jnp.float32),
        ),
        in_specs=[
            pl.BlockSpec(memory_space=pltpu.SMEM),
            wide,
            kv_spec,
            wide,
            wide,
            pl.BlockSpec((blocks, 1, local, group), lambda r: (0, r, 0, 0)),
        ],
        out_specs=(wide, kv_spec),
        compiler_params=pltpu.CompilerParams(vmem_limit_bytes=VMEM),
        cost_estimate=pl.CostEstimate(
            flops=20 * rows * blocks * local * keys * width,
            bytes_accessed=rows * blocks * local * width * 16,
            transcendentals=rows * blocks * local * keys * group,
        ),
        name="attend_back",
    )(info, queries, kv, out_grads, out, lse)


def bits_of(size):
    return [1 << b for b in range(size.bit_length() - 1)]


def spread_weight(shard, axis, place):
    dp, high, low, dp_size, high_size = place
    other = 1 - axis
    block = shard.shape[axis]
    width = shard.shape[other] // SQUARE
    pieces = [cut(shard, low * width, width, other)]
    for mask in range(1, SQUARE):
        pieces.append(swap(cut(shard, (low ^ mask) * width, width, other), "seq", mask))
    shape = [0, 0]
    shape[axis], shape[other] = SQUARE * block, width
    square = jnp.zeros(shape, shard.dtype)
    for mask in range(SQUARE):
        square = put(square, pieces[mask], (low ^ mask) * block, axis)
    parts = {(0, 0): square}
    for bit in bits_of(high_size):
        for (a, b) in list(parts):
            parts[a, b ^ bit] = swap(parts[a, b], "seq", SQUARE * bit)
    for bit in bits_of(dp_size):
        for (a, b) in list(parts):
            parts[a ^ bit, b] = swap(parts[a, b], "dp", bit)
    shape[axis] = SQUARE * block * high_size * dp_size
    whole = jnp.zeros(shape, shard.dtype)
    for (a, b), part in parts.items():
        index = (dp ^ a) * high_size + (high ^ b)
        whole = put(whole, part, index * SQUARE * block, axis)
    return whole


def settle_grad(grad, axis, place):
    dp, high, low, dp_size, high_size = place
    other = 1 - axis
    width = grad.shape[other]
    kept = grad
    for index, size, name, unit in ((dp, dp_size, "dp", 1), (high, high_size, "seq", SQUARE)):
        for bit in reversed(bits_of(size)):
            half = kept.shape[axis] // 2
            mine = (index // bit) % 2
            sent = cut(kept, (1 - mine) * half, half, axis).astype(jnp.bfloat16)
            kept = cut(kept, mine * half, half, axis) + swap(sent, name, unit * bit).astype(
                jnp.float32
            )
    block = kept.shape[axis] // SQUARE
    shape = [0, 0]
    shape[axis], shape[other] = block, SQUARE * width
    whole = jnp.zeros(shape, jnp.float32)
    whole = put(whole, cut(kept, low * block, block, axis), low * width, other)
    for mask in range(1, SQUARE):
        sent = cut(kept, (low ^ mask) * block, block, axis).astype(jnp.bfloat16)
        got = swap(sent, "seq", mask).astype(jnp.float32)
        whole = put(whole, got, (low ^ mask) * width, other)
    return whole


def gather_square(own, core):
    tokens, width = own.shape
    half = width // 2
    mine = cut(own, core * half, half, 1)
    got = jnp.concatenate([swap(mine, "seq", mask) for mask in range(1, SQUARE)], axis=0)
    across = swap(got, "mp", 1)
    first = jnp.where(core == 0, got, across)
    second = jnp.where(core == 0, across, got)
    return jnp.concatenate([own, jnp.concatenate([first, second], axis=1)], axis=0)


def scatter_square(partial, core):
    tokens, width = partial.shape[0] // SQUARE, partial.shape[1]
    half = width // 2
    kept = cut(partial, core * half, half, 1)
    sent = cut(partial, (1 - core) * half, half, 1).astype(jnp.bfloat16)
    kept = kept + swap(sent, "mp", 1).astype(jnp.float32)
    total = kept[:tokens]
    for mask in range(1, SQUARE):
        part = kept[mask * tokens : (mask + 1) * tokens].astype(jnp.bfloat16)
        total = total + swap(part, "seq", mask).astype(jnp.float32)
    mine = total.astype(jnp.bfloat16)
    across = swap(mine, "mp", 1)
    return jnp.concatenate(
        [jnp.where(core == 0, mine, across), jnp.where(core == 0, across, mine)], axis=1
    ).astype(jnp.float32)


MESH = pl.DeviceIdType.MESH


class Links:
    def __init__(self, send_sem, recv_sem, local_sem, high_size):
        self.send_sem, self.recv_sem, self.local_sem = send_sem, recv_sem, local_sem
        self.x, self.seq, self.core = (lax.axis_index(a) for a in ("dp", "seq", "mp"))
        self.high_size = high_size
        self.low, self.high = self.seq % SQUARE, self.seq // SQUARE
        self.count = self.local_count = 0
        self.sent = []

    def beside(self, flip):
        if flip == 1:
            return self.low + 1 - 2 * (self.low % 2)
        return (self.low + 2) % SQUARE if flip == 2 else SQUARE - 1 - self.low

    def to(self, dx=0, dh=0, dl=0, dc=0, flip=0):
        low = self.beside(flip) if flip else (self.low + dl) % SQUARE
        seq = ((self.high + dh) % self.high_size) * SQUARE + low
        return ((self.x + dx) % 2, seq, (self.core + dc) % 2)

    def copy(self, src, dst, **step):
        k = self.count
        self.count += 1
        made = pltpu.make_async_remote_copy(
            src_ref=src,
            dst_ref=dst,
            send_sem=self.send_sem.at[k],
            recv_sem=self.recv_sem.at[k],
            device_id=self.to(**step),
            device_id_type=MESH,
        )
        made.start()
        self.sent.append(made)
        return made

    def local(self, src, dst):
        k = self.local_count
        self.local_count += 1
        made = pltpu.make_async_copy(src, dst, self.local_sem.at[k])
        made.start()
        return made

    def greet(self, steps):
        barrier = pltpu.get_barrier_semaphore()
        for step in steps:
            pl.semaphore_signal(barrier, inc=1, device_id=self.to(**step), device_id_type=MESH)
        pl.semaphore_wait(barrier, len(steps))

    def left(self, copies):
        for made in copies:
            made.wait_send()
            self.sent = [one for one in self.sent if one is not made]

    def finish(self):
        for made in self.sent:
            made.wait_send()


def arrived(copies):
    for made in copies:
        made.wait_recv()


class Weight:
    def __init__(self, links, slice_of, spot):
        self.links, self.spot = links, spot
        l = links
        self.own = l.local(slice_of(l.low), spot(l.x, l.high, l.low, 1))
        self.near, self.far = [], []
        for dh in range(2):
            for dl in range(SQUARE):
                if dh or dl:
                    made = l.copy(
                        slice_of((l.low + dl) % SQUARE),
                        spot(l.x, l.high, l.low, 1),
                        dh=dh,
                        dl=dl,
                    )
                    (self.far if dh else self.near).append(made)

    def pass_near(self):
        self.own.wait()
        arrived(self.near)
        l = self.links
        part = self.spot(l.x, l.high, 0, SQUARE)
        self.across = [l.copy(part, part, dx=1)]

    def pass_far(self):
        arrived(self.far)
        l = self.links
        part = self.spot(l.x, 1 - l.high, 0, SQUARE)
        self.across.append(l.copy(part, part, dx=1))

    def wait(self):
        arrived(self.across)


def gather_push(l, everyone, source):
    return [
        l.copy(source(part), everyone(l.core, l.low, part), flip=flip)
        for flip, part in ((1, 0), (2, 1), (1, 1), (2, 0))
    ]


def gather_across(l, everyone, pushed):
    handed, corner = [], []
    for k, (flip, part) in enumerate(((1, 0), (2, 1), (1, 1), (2, 0))):
        pushed[k].wait_recv()
        block = everyone(l.core, l.beside(flip), part)
        if k < 2:
            corner.append(l.copy(block, block, flip=3 - flip))
        handed.append(l.copy(block, block, dc=1))
    for part in range(2):
        corner[part].wait_recv()
        block = everyone(l.core, l.beside(3), part)
        handed.append(l.copy(block, block, dc=1))
    return handed, corner


def square_push(l, total_of, send, relay, landed):
    lines = send.shape[1]
    first, second = pl.ds(0, lines // 2), pl.ds(lines // 2, lines // 2)
    one, two, corner = (l.beside(flip) for flip in (1, 2, 3))
    send[corner] = total_of(corner).astype(jnp.bfloat16)
    made = [
        l.copy(send.at[corner, first], relay.at[0], flip=1),
        l.copy(send.at[corner, second], relay.at[1], flip=2),
    ]
    send[one] = total_of(one).astype(jnp.bfloat16)
    made.append(l.copy(send.at[one, first], landed.at[0, first], flip=1))
    send[two] = total_of(two).astype(jnp.bfloat16)
    made.append(l.copy(send.at[two, second], landed.at[1, second], flip=2))
    made[0].wait_recv()
    value = send[two, first].astype(jnp.float32) + relay[0].astype(jnp.float32)
    send[two, first] = value.astype(jnp.bfloat16)
    made.append(l.copy(send.at[two, first], landed.at[1, first], flip=2))
    made[1].wait_recv()
    value = send[one, second].astype(jnp.float32) + relay[1].astype(jnp.float32)
    send[one, second] = value.astype(jnp.bfloat16)
    made.append(l.copy(send.at[one, second], landed.at[0, second], flip=1))
    return made


def square_settle(l, total_of, made, landed, both):
    total = total_of(l.low)
    arrived(made[2:])
    total = total + landed[0].astype(jnp.float32) + landed[1].astype(jnp.float32)
    both[l.core] = total.astype(jnp.bfloat16)
    return l.copy(both.at[l.core], both.at[l.core], dc=1)


def roll_heads(value):
    width = value.shape[1]
    lane = lax.broadcasted_iota(jnp.int32, value.shape, 1)
    left = pltpu.roll(value, width - HD // 2, 1)
    right = pltpu.roll(value, HD // 2, 1)
    return jnp.where(lane % HD < HD // 2, left, right)


def allowed_keys(l, ends, row, span, keys):
    def segment_of(place):
        total = jnp.zeros_like(place)
        for doc in range(4):
            total = total + (place >= ends[row * 4 + doc]).astype(jnp.int32)
        return total

    query = l.high * span + lax.broadcasted_iota(jnp.int32, (span, 1), 0)
    key = lax.broadcasted_iota(jnp.int32, (1, keys), 1)
    return (segment_of(query) == segment_of(key)) & (query >= key)


def front_kernel(
    sizes,
    ends,
    x_in,
    g_in,
    qkv_in,
    gain_in,
    wo_in,
    wg_in,
    wu_in,
    wd_in,
    cos_in,
    sin_in,
    qkv_out,
    wo_out,
    wg_out,
    wu_out,
    wd_out,
    gain_out,
    normed_one_out,
    q_out,
    kv_out,
    attn_out,
    residual_out,
    normed_two_out,
    g_out,
    x_all,
    normed,
    wqkv,
    wo,
    gains,
    gain_rows,
    cos,
    sin,
    q,
    kv,
    attn,
    low_attn,
    send_core,
    recv_core,
    send_block,
    recv_block,
    relay,
    both,
    residual,
    normed_two,
    send_sem,
    recv_sem,
    local_sem,
):
    rows, local, model, high_size = sizes
    own = rows * local
    tokens = SQUARE * own
    half = model // 2
    block = qkv_in.shape[1]
    heads = q.shape[2] // HD
    span = SQUARE * local
    keys = high_size * span
    l = Links(send_sem, recv_sem, local_sem, high_size)
    near = [dict(dl=dl) for dl in range(1, SQUARE)]
    far = [dict(dh=1, dl=dl) for dl in range(SQUARE)]
    l.greet(near + far + [dict(dx=1), dict(dc=1)])

    def row_spot(ref):
        def spot(x, h, low, n):
            start = ((x * high_size + h) * SQUARE + low) * block
            return ref.at[pl.ds(pl.multiple_of(start, block), n * block)]

        return spot

    def block_spot(ref):
        return lambda x, h, low, n: ref.at[pl.ds((x * high_size + h) * SQUARE + low, n)]

    def half_spot(ref):
        def spot(x, h, low, n):
            start = pl.multiple_of((h * SQUARE + low) * block, block)
            return ref.at[x, :, pl.ds(start, n * block)]

        return spot

    def column_spot(ref):
        def spot(x, h, low, n):
            start = ((x * high_size + h) * SQUARE + low) * block
            return ref.at[:, pl.ds(pl.multiple_of(start, block), n * block)]

        return spot

    def columns(ref, width):
        return lambda j: ref.at[:, pl.ds(pl.multiple_of(j * width, width), width)]

    def lines(ref, width):
        return lambda j: ref.at[pl.ds(pl.multiple_of(j * width, width), width)]

    def part_at(low, part):
        if part is None:
            return pl.ds(pl.multiple_of(low * own, own), own)
        return pl.ds(pl.multiple_of(low * own + part * (own // 2), own // 2), own // 2)

    def x_spot(side, low, part=None):
        return x_all.at[side, part_at(low, part)]

    def g_spot(side, low, part=None):
        return g_out.at[part_at(low, part), pl.ds(pl.multiple_of(side * half, half), half)]

    def normed_two_spot(side, low, part=None):
        return normed_two.at[side, part_at(low, part)]

    def own_part_of(ref):
        return lambda part: ref.at[
            pl.ds(part * (own // 2), own // 2), pl.ds(pl.multiple_of(l.core * half, half), half)
        ]

    def side_of(ref, side):
        return ref.at[:, pl.ds(pl.multiple_of(side * half, half), half)]

    loads = [l.local(side_of(x_in, side), x_spot(side, l.low)) for side in range(2)]
    loads += [l.local(cos_in, cos), l.local(sin_in, sin)]
    w_gain = Weight(l, lambda j: gain_in.at[pl.ds(0, 1)], block_spot(gains))
    w_qkv = Weight(l, lambda j: qkv_in.at[j], row_spot(wqkv))
    x_pushed = gather_push(l, x_spot, own_part_of(x_in))
    w_o = Weight(l, lines(wo_in, wo.shape[1]), half_spot(wo))
    w_gate = Weight(l, columns(wg_in, wg_out.shape[1]), row_spot(wg_out))

    w_gain.pass_near()
    w_qkv.pass_near()
    x_handed, _ = gather_across(l, x_spot, x_pushed)
    w_gain.pass_far()
    w_qkv.pass_far()
    w_o.pass_near()
    w_o.pass_far()
    for made in loads:
        made.wait()
    w_gain.wait()
    for b in range(gains.shape[0]):
        tile = gains[b].astype(jnp.float32)
        gain_rows[0:1, b * block : (b + 1) * block] = tile[0:1]
        gain_rows[1:2, b * block : (b + 1) * block] = tile[1:2]
    arrived(x_handed)

    step = 128

    def norm_step(i, carry):
        at = pl.ds(pl.multiple_of(i * step, step), step)
        first, second = x_all[0, at].astype(jnp.float32), x_all[1, at].astype(jnp.float32)
        total = jnp.sum(first * first, axis=1, keepdims=True)
        total = total + jnp.sum(second * second, axis=1, keepdims=True)
        scale = lax.rsqrt(total / model + EPSILON)
        normed[at, :half] = (first * scale * gain_rows[0:1, :half]).astype(jnp.bfloat16)
        normed[at, half:] = (second * scale * gain_rows[0:1, half:]).astype(jnp.bfloat16)
        return carry

    lax.fori_loop(0, tokens // step, norm_step, 0)
    stores = [l.local(normed, normed_one_out)]
    w_qkv.wait()
    stores += [l.local(wqkv, qkv_out), l.local(gain_rows, gain_out)]

    def project_step(i, carry):
        at = pl.ds(pl.multiple_of(i * local, local), local)
        pre = dot(normed[at], wqkv[...])
        times = heads // 2
        cos_all = jnp.concatenate([cos[at, : 2 * HD]] * times + [cos[at, 2 * HD :]], axis=1)
        sin_all = jnp.concatenate([sin[at, : 2 * HD]] * times + [sin[at, 2 * HD :]], axis=1)
        turned = pre * cos_all + roll_heads(pre) * sin_all
        spot = pl.ds(pl.multiple_of((i // rows) * local, local), local)
        q[i % rows, spot] = (turned[:, : heads * HD].astype(jnp.bfloat16) * HD ** (-0.5)).astype(
            jnp.bfloat16
        )
        kv[l.high, i % rows, spot] = turned[:, heads * HD :].astype(jnp.bfloat16)
        return carry

    lax.fori_loop(0, SQUARE * rows, project_step, 0)
    kv_copy = l.copy(kv.at[l.high], kv.at[l.high], dh=1)
    stores.append(l.local(q, q_out))
    w_gate.pass_near()
    w_up = Weight(l, columns(wu_in, wu_out.shape[1]), row_spot(wu_out))
    kv_copy.wait_recv()
    stores.append(l.local(kv, kv_out))

    def attend_row(r, carry):
        allowed = allowed_keys(l, ends, r, span, keys)
        kv_row = kv[:, r].reshape(keys, 2 * HD)
        k, v = kv_row[:, :HD], kv_row[:, HD:]
        q_row = q[r]
        outs = []
        for head in range(heads):
            score = dot(q_row[:, head * HD : (head + 1) * HD], k, ((1,), (1,)))
            score = jnp.where(allowed, score, MASKED)
            top = jnp.max(score, axis=1, keepdims=True)
            grown = jnp.exp(score - top)
            total = jnp.sum(grown, axis=1, keepdims=True)
            probs = (grown * (1.0 / total)).astype(jnp.bfloat16)
            outs.append(dot(probs, v))
        out = jnp.concatenate(outs, axis=1)
        for j in range(SQUARE):
            at = pl.ds(pl.multiple_of(j * own + r * local, local), local)
            part = out[j * local : (j + 1) * local]
            attn[at] = part
            low_attn[at] = part.astype(jnp.bfloat16)
        return carry

    lax.fori_loop(0, rows, attend_row, 0)
    stores.append(l.local(attn, attn_out))
    w_gate.pass_far()
    w_o.wait()
    stores.append(l.local(wo, wo_out))

    def project_out(j, side):
        at = pl.ds(pl.multiple_of(j * own, own), own)
        return dot(low_attn[at], wo[side])

    handed = []
    for j in range(SQUARE):
        send_core[j] = project_out(j, 1 - l.core).astype(jnp.bfloat16)
        handed.append(l.copy(send_core.at[j], recv_core.at[j], dc=1))
    arrived(handed)

    def total_out(j):
        return project_out(j, l.core) + recv_core[j].astype(jnp.float32)

    pushed = square_push(l, total_out, send_block, relay, recv_block)
    w_up.pass_near()
    w_down = Weight(l, lines(wd_in, wd_out.shape[0]), column_spot(wd_out))
    square_settle(l, total_out, pushed, recv_block, both).wait_recv()
    at_own = pl.ds(pl.multiple_of(l.low * own, own), own)
    total = jnp.zeros((own, 1), jnp.float32)
    for side in range(2):
        value = x_all[side, at_own].astype(jnp.float32) + both[side].astype(jnp.float32)
        residual[:, side * half : (side + 1) * half] = value
        total = total + jnp.sum(value * value, axis=1, keepdims=True)
    scale = lax.rsqrt(total / model + EPSILON)
    for side in range(2):
        at = slice(side * half, (side + 1) * half)
        normed_two[side, at_own] = (residual[:, at] * scale * gain_rows[1:2, at]).astype(
            jnp.bfloat16
        )
    stores.append(l.local(residual, residual_out))
    pushed = gather_push(
        l, normed_two_spot, lambda part: normed_two_spot(l.core, l.low, part)
    )
    loads = [l.local(side_of(g_in, side), g_spot(side, l.low)) for side in range(2)]
    g_pushed = gather_push(l, g_spot, own_part_of(g_in))
    w_up.pass_far()
    handed, _ = gather_across(l, normed_two_spot, pushed)
    w_down.pass_near()
    arrived(handed)
    for side in range(2):
        stores.append(l.local(normed_two.at[side], side_of(normed_two_out, side)))
    g_handed, _ = gather_across(l, g_spot, g_pushed)
    w_down.pass_far()
    arrived(g_handed)
    for weight in (w_gate, w_up, w_down):
        weight.wait()
    for made in loads + stores:
        made.wait()
    l.finish()


def front(sizes, ends, x, g, qkv, gain, wo, wg, wu, wd, cos, sin):
    rows, local, model, high_size = sizes
    own = rows * local
    tokens = SQUARE * own
    half = model // 2
    heads = wo.shape[0] // SQUARE // HD
    width = qkv.shape[2]
    ff = wg.shape[1] // SQUARE
    blocks = model // qkv.shape[1]
    span = SQUARE * local
    low, f32 = jnp.bfloat16, jnp.float32
    shape = jax.ShapeDtypeStruct
    outs = (
        shape((model, width), low),
        shape((2, heads * HD, half), low),
        shape((model, ff), low),
        shape((model, ff), low),
        shape((ff, model), low),
        shape((8, model), f32),
        shape((tokens, model), low),
        shape((rows, span, heads * HD), low),
        shape((high_size, rows, span, 2 * HD), low),
        shape((tokens, heads * HD), f32),
        shape((own, model), f32),
        shape((tokens, model), low),
        shape((tokens, model), low),
    )
    anywhere = pl.BlockSpec(memory_space=pl.ANY)
    vmem = pltpu.VMEM
    return pl.pallas_call(
        functools.partial(front_kernel, sizes),
        out_shape=outs,
        in_specs=[pl.BlockSpec(memory_space=pltpu.SMEM)] + [anywhere] * 10,
        out_specs=[anywhere] * len(outs),
        scratch_shapes=[
            vmem((2, tokens, half), low),
            vmem((tokens, model), low),
            vmem((model, width), low),
            vmem((2, heads * HD, half), low),
            vmem((blocks,) + gain.shape[1:], low),
            vmem((8, model), f32),
            vmem((tokens, 4 * HD), f32),
            vmem((tokens, 4 * HD), f32),
            vmem((rows, span, heads * HD), low),
            vmem((high_size, rows, span, 2 * HD), low),
            vmem((tokens, heads * HD), f32),
            vmem((tokens, heads * HD), low),
            vmem((SQUARE, own, half), low),
            vmem((SQUARE, own, half), low),
            vmem((SQUARE, own, half), low),
            vmem((2, own, half), low),
            vmem((2, own // 2, half), low),
            vmem((2, own, half), low),
            vmem((own, model), f32),
            vmem((2, tokens, half), low),
            pltpu.SemaphoreType.DMA((128,)),
            pltpu.SemaphoreType.DMA((128,)),
            pltpu.SemaphoreType.DMA((32,)),
        ],
        compiler_params=pltpu.CompilerParams(
            collective_id=0, has_side_effects=True, vmem_limit_bytes=VMEM
        ),
        name="front",
    )(ends, x, g, qkv, gain, wo, wg, wu, wd, cos, sin)


class Grad:
    def __init__(self, links, half_of, kept, crossed, block_of, landed):
        self.links, self.kept, self.crossed = links, kept, crossed
        self.block_of, self.landed = block_of, landed
        l = links
        self.own = l.local(half_of(l.x), kept) if half_of else None
        if half_of:
            self.cross = l.copy(half_of(1 - l.x), crossed, dx=1)

    def deal(self):
        l = self.links
        if self.own is not None:
            self.own.wait()
        self.cross.wait_recv()
        kept, crossed = self.kept, self.crossed
        lines = kept.shape[0]
        step = min(128, lines)

        def add(i, carry):
            at = pl.ds(pl.multiple_of(i * step, step), step)
            kept[at] = (kept[at].astype(jnp.float32) + crossed[at].astype(jnp.float32)).astype(
                jnp.bfloat16
            )
            return carry

        lax.fori_loop(0, lines // step, add, 0)
        self.dealt = []
        for dh in range(2):
            for dl in range(SQUARE):
                if dh or dl:
                    block = self.block_of((l.high + dh) % 2, (l.low + dl) % SQUARE)
                    self.dealt.append(
                        l.copy(block, self.landed(l.high, l.low), dh=dh, dl=dl)
                    )
        self.mine = l.local(self.block_of(l.high, l.low), self.landed(l.high, l.low))


def back_kernel(
    sizes,
    ends,
    x_in,
    g_in,
    residual_in,
    gain_in,
    normed_two_part,
    layer_part,
    dwg_in,
    dwu_in,
    dwd_in,
    qkv_in,
    wo_in,
    normed_one_in,
    q_in,
    kv_in,
    attn_in,
    cos_in,
    sin_in,
    layer_out,
    input_out,
    land_q,
    land_o,
    land_g,
    land_u,
    land_d,
    gains_out,
    kept_g,
    kept_u,
    kept_d,
    cross_g,
    cross_u,
    cross_d,
    kept_q,
    cross_q,
    kept_o,
    cross_o,
    send_q,
    send_o,
    own_a,
    recv_core,
    recv_block,
    relay,
    recv_block_b,
    relay_b,
    both,
    both_b,
    x_own,
    g_own,
    residual,
    gain_rows,
    low_all,
    wqkv,
    wo,
    q,
    kv,
    attn,
    attn_grad,
    dkv,
    dkv_send,
    dkv_recv,
    dqkv,
    cos,
    sin,
    gain_send,
    gain_recv,
    out_low,
    gain_sum,
    send_sem,
    recv_sem,
    local_sem,
):
    rows, local, model, high_size = sizes
    own = rows * local
    tokens = SQUARE * own
    half = model // 2
    block = x_own.shape[1] // 16
    heads = q.shape[2] // HD
    span = SQUARE * local
    keys = high_size * span
    f32, b16 = jnp.float32, jnp.bfloat16
    l = Links(send_sem, recv_sem, local_sem, high_size)
    steps = [
        dict(dx=dx, dh=dh, dl=dl)
        for dx in range(2)
        for dh in range(2)
        for dl in range(SQUARE)
        if dx or dh or dl
    ]
    l.greet(steps + [dict(dc=1)])

    def side_of(ref, side):
        return ref.at[:, pl.ds(pl.multiple_of(side * half, half), half)]

    def row_half(ref):
        return lambda x: ref.at[pl.ds(pl.multiple_of(x * half, half), half)]

    def row_block(ref):
        def at(h, low):
            start = pl.multiple_of((h * SQUARE + low) * block, block)
            return ref.at[pl.ds(start, block)]

        return at

    def column_block(ref):
        def at(h, low):
            start = pl.multiple_of((h * SQUARE + low) * block, block)
            return ref.at[:, pl.ds(start, block)]

        return at

    def tall(ref):
        lines = ref.shape[1] // SQUARE
        return lambda h, low: ref.at[h, pl.ds(pl.multiple_of(low * lines, lines), lines)]

    def broad(ref):
        wide = ref.shape[2] // SQUARE
        return lambda h, low: ref.at[h, :, pl.ds(pl.multiple_of(low * wide, wide), wide)]

    def block_at(j):
        return pl.ds(pl.multiple_of(j * own, own), own)

    def part_at(ref, j, side):
        return ref.at[block_at(j), pl.ds(pl.multiple_of(side * half, half), half)]

    handed = [
        l.copy(part_at(normed_two_part, j, 1 - l.core), recv_core.at[j], dc=1)
        for j in range(SQUARE)
    ]
    owned = [l.local(part_at(normed_two_part, j, l.core), own_a.at[j]) for j in range(SQUARE)]
    loads = [
        l.local(residual_in, residual),
        l.local(gain_in, gain_rows),
        l.local(g_in, g_own),
    ]
    grad_d = Grad(
        l, lambda x: side_of(dwd_in, x), kept_d, cross_d, column_block(kept_d), tall(land_d)
    )
    later = [
        l.local(x_in, x_own),
        l.local(wo_in, wo),
        l.local(attn_in, attn),
        l.local(q_in, q),
        l.local(kv_in, kv),
        l.local(qkv_in, wqkv),
        l.local(cos_in, cos),
        l.local(sin_in, sin),
    ]

    def own_total(j):
        return own_a[j].astype(f32) + recv_core[j].astype(f32)

    def norm_back(value_of, gain_row, grads):
        squares = jnp.zeros((own, 1), f32)
        inner = jnp.zeros((own, 1), f32)
        for side in range(2):
            at = slice(side * half, (side + 1) * half)
            value = value_of(side)
            squares = squares + jnp.sum(value * value, axis=1, keepdims=True)
            weighted = grads[side].astype(f32) * gain_rows[gain_row : gain_row + 1, at]
            inner = inner + jnp.sum(weighted * value, axis=1, keepdims=True)
        scale = lax.rsqrt(squares / model + EPSILON)
        pull = scale * scale * scale * (inner / model)
        outs = []
        for side in range(2):
            at = slice(side * half, (side + 1) * half)
            value = value_of(side)
            grad = grads[side].astype(f32)
            summed = jnp.sum(grad * (value * scale), axis=0, keepdims=True)
            for b in range(half // block):
                gain_send[gain_row, side * (half // block) + b, 0:1] = summed[
                    :, b * block : (b + 1) * block
                ]
            weighted = grad * gain_rows[gain_row : gain_row + 1, at]
            outs.append(weighted * scale - value * pull)
        return outs

    def push_gains(gain_row):
        me = (l.x * 2 + l.high) * SQUARE + l.low
        made = []
        for step in steps:
            to = ((l.x + step["dx"]) % 2 * 2 + (l.high + step["dh"]) % 2) * SQUARE + (
                l.low + step["dl"]
            ) % SQUARE
            made.append(l.copy(gain_send.at[gain_row, to], gain_recv.at[gain_row, me], **step))
        return made, l.local(gain_send.at[gain_row, me], gain_recv.at[gain_row, me])

    for made in owned:
        made.wait()
    arrived(handed)

    pushed = square_push(l, own_total, own_a, relay, recv_block)
    for made in loads:
        made.wait()
    swapped = square_settle(l, own_total, pushed, recv_block, both)
    swapped.wait_recv()
    l.left(pushed + [swapped])
    outs = norm_back(
        lambda side: residual[:, side * half : (side + 1) * half], 1, [both[0], both[1]]
    )
    for side in range(2):
        at = slice(side * half, (side + 1) * half)
        value = g_own[:, at].astype(f32) + outs[side]
        residual[:, at] = value
        low_all[side, block_at(l.low)] = value.astype(b16)

    def low_spot(side, low, part):
        start = pl.multiple_of(low * own + part * (own // 2), own // 2)
        return low_all.at[side, pl.ds(start, own // 2)]

    low_pushed = gather_push(l, low_spot, lambda part: low_spot(l.core, l.low, part))
    grad_g = Grad(l, row_half(dwg_in), kept_g, cross_g, row_block(kept_g), broad(land_g))
    ffn_gains = push_gains(1)
    handed_b = [
        l.copy(part_at(layer_part, j, 1 - l.core), recv_core.at[j], dc=1) for j in range(SQUARE)
    ]
    owned = [l.local(part_at(layer_part, j, l.core), own_a.at[j]) for j in range(SQUARE)]
    for made in later:
        made.wait()
    low_handed, low_corner = gather_across(l, low_spot, low_pushed)
    grad_d.deal()
    arrived(low_handed)
    grad_u = Grad(l, row_half(dwu_in), kept_u, cross_u, row_block(kept_u), broad(land_u))

    def out_grad_step(j, carry):
        at = block_at(j)
        rows_at = attn[at].astype(b16)
        low_out = dot(low_all[0, at], wo[0], ((1,), (1,)))
        low_out = (low_out + dot(low_all[1, at], wo[1], ((1,), (1,)))).astype(b16)
        for r in range(rows):
            spot = pl.ds(pl.multiple_of(j * local, local), local)
            attn_grad[r, spot] = low_out[r * local : (r + 1) * local]
        out_low[at] = rows_at
        return carry

    lax.fori_loop(0, SQUARE, out_grad_step, 0)
    send_o[...] = dot(out_low[...], low_all[1 - l.x], ((0,), (0,))).astype(b16)
    grad_o = Grad(l, None, kept_o, cross_o, column_block(kept_o), tall(land_o))
    grad_o.cross = l.copy(send_o, cross_o, dx=1)
    kept_o[...] = dot(out_low[...], low_all[l.x], ((0,), (0,))).astype(b16)

    for made in owned:
        made.wait()
    arrived(handed_b)
    pushed_b = square_push(l, own_total, own_a, relay_b, recv_block_b)

    def attend_row(r, carry):
        allowed = allowed_keys(l, ends, r, span, keys)
        kv_row = kv[:, r].reshape(keys, 2 * HD)
        k, v = kv_row[:, :HD], kv_row[:, HD:]
        q_row, go_row = q[r], attn_grad[r]
        out_row = jnp.concatenate(
            [
                attn[pl.ds(pl.multiple_of(j * own + r * local, local), local)]
                for j in range(SQUARE)
            ],
            axis=0,
        )
        grads = []
        dk = jnp.zeros((keys, HD), f32)
        dv = jnp.zeros((keys, HD), f32)
        for head in range(heads):
            at = slice(head * HD, (head + 1) * HD)
            qh, go = q_row[:, at], go_row[:, at]
            delta = jnp.sum(go.astype(f32) * out_row[:, at], axis=1, keepdims=True)
            score = jnp.where(allowed, dot(qh, k, ((1,), (1,))), MASKED)
            top = jnp.max(score, axis=1, keepdims=True)
            grown = jnp.exp(score - top)
            probs = grown * (1.0 / jnp.sum(grown, axis=1, keepdims=True))
            dv = dv + dot(probs.astype(b16), go, ((0,), (0,)))
            pull = dot(go, v, ((1,), (1,)))
            score_grad = (probs * (pull - delta)).astype(b16)
            grads.append(dot(score_grad, k) * HD ** (-0.5))
            dk = dk + dot(score_grad, qh, ((0,), (0,)))
        turned = jnp.concatenate(grads, axis=1)
        for j in range(SQUARE):
            at = pl.ds(pl.multiple_of(j * own + r * local, local), local)
            value = turned[j * local : (j + 1) * local]
            cos_q = jnp.concatenate([cos[at, : 2 * HD]] * (heads // 2), axis=1)
            sin_q = jnp.concatenate([sin[at, : 2 * HD]] * (heads // 2), axis=1)
            dqkv[at, : heads * HD] = (value * cos_q - roll_heads(value) * sin_q).astype(b16)
        both_kv = jnp.concatenate([dk, dv], axis=1)
        for part in range(high_size):
            dkv[part, r] = both_kv[part * span : (part + 1) * span]
        return carry

    lax.fori_loop(0, 1, attend_row, 0)
    grad_g.deal()
    lax.fori_loop(1, rows, attend_row, 0)
    dkv_send[...] = dkv[1 - l.high].astype(b16)
    dkv_copy = l.copy(dkv_send, dkv_recv, dh=1)
    l.left(low_pushed + low_handed + low_corner)
    normed = l.local(normed_one_in.at[:, pl.ds(0, half)], low_all.at[0])
    normed_2 = l.local(normed_one_in.at[:, pl.ds(half, half)], low_all.at[1])
    grad_o.deal()
    both_b_copy = square_settle(l, own_total, pushed_b, recv_block_b, both_b)
    dkv_copy.wait_recv()

    def unrotate_step(i, carry):
        at = pl.ds(pl.multiple_of(i * local, local), local)
        spot = pl.ds(pl.multiple_of((i // rows) * local, local), local)
        kv_sum = dkv[l.high, i % rows, spot] + dkv_recv[i % rows, spot].astype(f32)
        turned = kv_sum * cos[at, 2 * HD :] - roll_heads(kv_sum) * sin[at, 2 * HD :]
        dqkv[at, heads * HD :] = turned.astype(b16)
        return carry

    lax.fori_loop(0, SQUARE * rows, unrotate_step, 0)

    def project_back(j, side):
        weight = wqkv[pl.ds(pl.multiple_of(side * half, half), half)]
        return dot(dqkv[block_at(j)], weight, ((1,), (1,)))

    both_b_copy.wait_recv()
    l.left(pushed_b)
    handed = []
    for j in range(SQUARE):
        own_a[j] = project_back(j, 1 - l.core).astype(b16)
        handed.append(l.copy(own_a.at[j], recv_core.at[j], dc=1))
    normed.wait()
    normed_2.wait()
    send_q[...] = dot(low_all[1 - l.x], dqkv[...], ((0,), (0,))).astype(b16)
    arrived(handed)

    def own_total_c(j):
        return project_back(j, l.core) + recv_core[j].astype(f32)

    l.left(handed)
    pushed = square_push(l, own_total_c, own_a, relay, recv_block)
    grad_q = Grad(l, None, kept_q, cross_q, row_block(kept_q), lambda h, low: land_q.at[h, low])
    grad_q.cross = l.copy(send_q, cross_q, dx=1)
    kept_q[...] = dot(low_all[l.x], dqkv[...], ((0,), (0,))).astype(b16)
    grad_u.deal()
    square_settle(l, own_total_c, pushed, recv_block, both).wait_recv()
    outs = norm_back(
        lambda side: x_own[:, side * half : (side + 1) * half].astype(f32),
        0,
        [both[0], both[1]],
    )
    attn_gains = push_gains(0)
    for side in range(2):
        at = slice(side * half, (side + 1) * half)
        x_own[:, at] = (residual[:, at] + outs[side]).astype(b16)
    stores = [l.local(x_own, input_out)]
    residual_load = l.local(residual_in, residual)
    grad_q.deal()
    residual_load.wait()
    for side in range(2):
        at = slice(side * half, (side + 1) * half)
        g_own[:, at] = (residual[:, at] + both_b[side].astype(f32)).astype(b16)
    stores.append(l.local(g_own, layer_out))
    for made, kept in (ffn_gains, attn_gains):
        arrived(made)
        kept.wait()
    for row in range(2):
        total = jnp.zeros((8, block), f32)
        for b in range(16):
            total = total + gain_recv[row, b]
        gain_sum[row : row + 1] = total[0:1]
    stores.append(l.local(gain_sum, gains_out))
    for grad in (grad_d, grad_o, grad_g, grad_u, grad_q):
        grad.mine.wait()
        arrived(grad.dealt)
    for made in stores:
        made.wait()
    l.finish()


def back(sizes, ends, *arrays):
    rows, local, model, high_size = sizes
    own = rows * local
    tokens = SQUARE * own
    half = model // 2
    block = model // 16
    ff = arrays[6].shape[1]
    width = arrays[9].shape[1]
    wide = width - 2 * HD
    span = SQUARE * local
    b16, f32 = jnp.bfloat16, jnp.float32
    shape = jax.ShapeDtypeStruct
    vmem = pltpu.VMEM
    outs = (
        shape((own, model), b16),
        shape((own, model), b16),
        shape((2, SQUARE, block, width), b16),
        shape((2, SQUARE * wide, block), b16),
        shape((2, block, SQUARE * ff), b16),
        shape((2, block, SQUARE * ff), b16),
        shape((2, SQUARE * ff, block), b16),
        shape((8, block), f32),
    )
    anywhere = pl.BlockSpec(memory_space=pl.ANY)
    scratch = [
        vmem((half, ff), b16),
        vmem((half, ff), b16),
        vmem((ff, half), b16),
        vmem((half, ff), b16),
        vmem((half, ff), b16),
        vmem((ff, half), b16),
        vmem((half, width), b16),
        vmem((half, width), b16),
        vmem((wide, half), b16),
        vmem((wide, half), b16),
        vmem((half, width), b16),
        vmem((wide, half), b16),
        vmem((SQUARE, own, half), b16),
        vmem((SQUARE, own, half), b16),
        vmem((2, own, half), b16),
        vmem((2, own // 2, half), b16),
        vmem((2, own, half), b16),
        vmem((2, own // 2, half), b16),
        vmem((2, own, half), b16),
        vmem((2, own, half), b16),
        vmem((own, model), b16),
        vmem((own, model), b16),
        vmem((own, model), f32),
        vmem((8, model), f32),
        vmem((2, tokens, half), b16),
        vmem((model, width), b16),
        vmem((2, wide, half), b16),
        vmem((rows, span, wide), b16),
        vmem((high_size, rows, span, 2 * HD), b16),
        vmem((tokens, wide), f32),
        vmem((rows, span, wide), b16),
        vmem((high_size, rows, span, 2 * HD), f32),
        vmem((rows, span, 2 * HD), b16),
        vmem((rows, span, 2 * HD), b16),
        vmem((tokens, width), b16),
        vmem((tokens, 4 * HD), f32),
        vmem((tokens, 4 * HD), f32),
        vmem((2, 16, 8, block), f32),
        vmem((2, 16, 8, block), f32),
        vmem((tokens, wide), b16),
        vmem((8, block), f32),
        pltpu.SemaphoreType.DMA((128,)),
        pltpu.SemaphoreType.DMA((128,)),
        pltpu.SemaphoreType.DMA((64,)),
    ]
    return pl.pallas_call(
        functools.partial(back_kernel, sizes),
        out_shape=outs,
        in_specs=[pl.BlockSpec(memory_space=pltpu.SMEM)] + [anywhere] * len(arrays),
        out_specs=[anywhere] * len(outs),
        scratch_shapes=scratch,
        compiler_params=pltpu.CompilerParams(
            collective_id=1, has_side_effects=True, vmem_limit_bytes=VMEM
        ),
        name="back",
    )(ends, *arrays)


def norm_back(values, scale, gain, grad):
    weighted = grad * gain
    gain_grad = jnp.sum(grad * values * scale, axis=0)
    inner = jnp.mean(weighted * values, axis=-1, keepdims=True)
    return (weighted * scale - values * scale**3 * inner, gain_grad)


def shards_exchanged(
    hidden_in,
    doc_lengths,
    attn_gain,
    query_weight,
    key_weight,
    value_weight,
    output_weight,
    ffn_gain,
    gate_weight,
    up_weight,
    down_weight,
    out_grad,
):
    rows, local, model = hidden_in.shape
    tokens = rows * local
    seq = lax.axis_index("seq")
    core = lax.axis_index("mp")
    low, high = seq % SQUARE, seq // SQUARE
    high_size = lax.axis_size("seq") // SQUARE
    place = (lax.axis_index("dp"), high, low, lax.axis_size("dp"), high_size)
    group = H // KVH
    span = SQUARE * local

    ends = jnp.cumsum(doc_lengths, axis=-1)
    info = jnp.concatenate([jnp.stack([low, high]), ends.reshape(-1)]).astype(jnp.int32)

    gains = lax.all_gather(jnp.stack([attn_gain, ffn_gain]), ("dp", "seq"), axis=1, tiled=True)
    gain_one, gain_two = gains[0].astype(jnp.float32), gains[1].astype(jnp.float32)

    own_in = hidden_in.reshape(tokens, model)
    all_in = gather_square(own_in, core).astype(jnp.float32)
    query_own = spread_weight(query_weight, 0, place)
    key_own = spread_weight(key_weight, 0, place)
    value_own = spread_weight(value_weight, 0, place)
    output_own = spread_weight(output_weight, 1, place)
    gate_own = spread_weight(gate_weight, 0, place)
    up_own = spread_weight(up_weight, 0, place)
    down_own = spread_weight(down_weight, 1, place)
    all_grad = gather_square(out_grad.reshape(tokens, model), core)

    blocks = low ^ jnp.arange(SQUARE, dtype=jnp.int32)
    spots = (high * span + blocks[:, None] * local + jnp.arange(local, dtype=jnp.int32)[None, :])
    reached = spots[:, None, :, None] >= ends[None, :, None, :]
    begin = jnp.max(jnp.where(reached, ends[None, :, None, :], 0), axis=-1)
    position = (spots[:, None, :] - begin).astype(jnp.float32)
    cosine, sine = rope_tables(position, HD)

    scale_one = lax.rsqrt(jnp.mean(all_in * all_in, axis=-1, keepdims=True) + EPSILON)
    normed_one = (all_in * scale_one * gain_one).astype(jnp.bfloat16)
    query_pre = dot(normed_one, query_own).reshape(SQUARE, rows, local, group, HD)
    key_pre = dot(normed_one, key_own).reshape(SQUARE, rows, local, 1, HD)
    value_pre = dot(normed_one, value_own).reshape(SQUARE, rows, local, HD)
    queries = rotate(query_pre, cosine, sine).astype(jnp.bfloat16)
    queries = queries.reshape(SQUARE, rows, local, group * HD)
    keys = rotate(key_pre, cosine, sine).astype(jnp.bfloat16).reshape(value_pre.shape)
    kv = jnp.concatenate([keys, value_pre.astype(jnp.bfloat16)], axis=-1)[None]
    for bit in bits_of(high_size):
        kv = jnp.concatenate([kv, swap(kv, "seq", SQUARE * bit)], axis=0)
    attn, lse = attend(info, queries, kv)
    attn_low = attn.reshape(SQUARE * tokens, group * HD).astype(jnp.bfloat16)
    residual = own_in.astype(jnp.float32) + scatter_square(dot(attn_low, output_own), core)

    scale_two = lax.rsqrt(jnp.mean(residual * residual, axis=-1, keepdims=True) + EPSILON)
    normed_two = (residual * scale_two * gain_two).astype(jnp.bfloat16)
    normed_two = gather_square(normed_two, core)
    gate_proj = dot(normed_two, gate_own)
    up_proj = dot(normed_two, up_own)
    sigmoid_gate = jax.nn.sigmoid(gate_proj)
    silu_gate = gate_proj * sigmoid_gate
    hidden_units = (silu_gate * up_proj).astype(jnp.bfloat16)
    hidden_grad = dot(all_grad, down_own, ((1,), (1,)))
    gate_act = (
        hidden_grad * up_proj * sigmoid_gate * (1.0 + gate_proj * (1.0 - sigmoid_gate))
    ).astype(jnp.bfloat16)
    up_act = (hidden_grad * silu_gate).astype(jnp.bfloat16)
    down_grad = settle_grad(dot(hidden_units, all_grad, ((0,), (0,))), 1, place)
    normed_two_grad = scatter_square(
        dot(gate_act, gate_own, ((1,), (1,))) + dot(up_act, up_own, ((1,), (1,))), core
    )
    layer_out = residual + scatter_square(dot(hidden_units, down_own), core)
    layer_out = layer_out.astype(jnp.bfloat16).reshape(hidden_in.shape)
    gate_grad = settle_grad(dot(normed_two, gate_act, ((0,), (0,))), 0, place)
    up_grad = settle_grad(dot(normed_two, up_act, ((0,), (0,))), 0, place)

    residual_part, ffn_gain_grad = norm_back(residual, scale_two, gain_two, normed_two_grad)
    residual_grad = out_grad.reshape(tokens, model).astype(jnp.float32) + residual_part
    residual_low = gather_square(residual_grad.astype(jnp.bfloat16), core)
    output_grad = settle_grad(dot(attn_low, residual_low, ((0,), (0,))), 1, place)
    attn_grad = dot(residual_low, output_own, ((1,), (1,))).astype(jnp.bfloat16)
    attn_grad = attn_grad.reshape(queries.shape)
    query_acc, kv_acc = attend_back(info, queries, kv, attn_grad, attn, lse)
    for bit in reversed(bits_of(high_size)):
        sent = kv_acc[bit:].astype(jnp.bfloat16)
        kv_acc = kv_acc[:bit] + swap(sent, "seq", SQUARE * bit).astype(jnp.float32)
    kv_acc = kv_acc[0]
    query_back = unrotate(query_acc.reshape(query_pre.shape), cosine, sine).astype(jnp.bfloat16)
    key_back = unrotate(kv_acc[..., :HD].reshape(key_pre.shape), cosine, sine)
    key_back = key_back.astype(jnp.bfloat16).reshape(SQUARE * tokens, HD)
    value_back = kv_acc[..., HD:].astype(jnp.bfloat16).reshape(SQUARE * tokens, HD)
    query_back = query_back.reshape(SQUARE * tokens, group * HD)
    normed_one_grad = scatter_square(
        dot(query_back, query_own, ((1,), (1,)))
        + dot(key_back, key_own, ((1,), (1,)))
        + dot(value_back, value_own, ((1,), (1,))),
        core,
    )
    query_grad = settle_grad(dot(normed_one, query_back, ((0,), (0,))), 0, place)
    key_grad = settle_grad(dot(normed_one, key_back, ((0,), (0,))), 0, place)
    value_grad = settle_grad(dot(normed_one, value_back, ((0,), (0,))), 0, place)
    own_32 = own_in.astype(jnp.float32)
    own_scale = lax.rsqrt(jnp.mean(own_32 * own_32, axis=-1, keepdims=True) + EPSILON)
    input_part, attn_gain_grad = norm_back(own_32, own_scale, gain_one, normed_one_grad)
    input_grad = (residual_grad + input_part).astype(jnp.bfloat16).reshape(hidden_in.shape)
    gain_grads = lax.psum_scatter(
        jnp.stack([attn_gain_grad, ffn_gain_grad]), ("dp", "seq"), scatter_dimension=1, tiled=True
    )
    return (
        layer_out,
        input_grad,
        gain_grads[0],
        query_grad,
        key_grad,
        value_grad,
        output_grad,
        gain_grads[1],
        gate_grad,
        up_grad,
        down_grad,
    )


def shards(
    hidden_in,
    doc_lengths,
    attn_gain,
    query_weight,
    key_weight,
    value_weight,
    output_weight,
    ffn_gain,
    gate_weight,
    up_weight,
    down_weight,
    out_grad,
):
    rows, local, model = hidden_in.shape
    tokens = rows * local
    seq = lax.axis_index("seq")
    high = seq // SQUARE
    high_size = lax.axis_size("seq") // SQUARE
    block = query_weight.shape[0]
    if block % 128 or high_size != 2 or lax.axis_size("dp") != 2:
        return shards_exchanged(
            hidden_in,
            doc_lengths,
            attn_gain,
            query_weight,
            key_weight,
            value_weight,
            output_weight,
            ffn_gain,
            gate_weight,
            up_weight,
            down_weight,
            out_grad,
        )
    group = H // KVH
    span = SQUARE * local
    width = (group + 2) * HD

    ends = jnp.cumsum(doc_lengths, axis=-1).astype(jnp.int32)
    spots = high * span + jnp.arange(span, dtype=jnp.int32).reshape(SQUARE, 1, local)
    reached = spots[..., None] >= ends[None, :, None, :]
    begin = jnp.max(jnp.where(reached, ends[None, :, None, :], 0), axis=-1)
    position = (spots - begin).astype(jnp.float32).reshape(SQUARE * tokens)
    angles = position[:, None] * inverse_freqs(HD)
    cos, sin = jnp.cos(angles), jnp.sin(angles)
    flat = jnp.zeros((SQUARE * tokens, HD), jnp.float32)
    cos = jnp.concatenate([cos] * 6 + [flat + 1.0], axis=1)
    sin = jnp.concatenate([-sin, sin] * 3 + [flat], axis=1)
    qkv_shard = jnp.concatenate(
        [
            query_weight.reshape(block, SQUARE, group * HD),
            key_weight.reshape(block, SQUARE, HD),
            value_weight.reshape(block, SQUARE, HD),
        ],
        axis=2,
    ).transpose(1, 0, 2)
    gain_shard = jnp.zeros((1, 16, block), jnp.bfloat16)
    gain_shard = gain_shard.at[0, 0].set(attn_gain).at[0, 1].set(ffn_gain)
    own_in = hidden_in.reshape(tokens, model)
    own_grad = out_grad.reshape(tokens, model)
    (
        qkv_own,
        output_own,
        gate_own,
        up_own,
        down_own,
        gains,
        normed_one,
        queries,
        kv,
        attn,
        residual,
        normed_two,
        all_grad,
    ) = front(
        (rows, local, model, high_size),
        ends.reshape(-1),
        own_in,
        own_grad,
        qkv_shard,
        gain_shard,
        output_weight,
        gate_weight,
        up_weight,
        down_weight,
        cos,
        sin,
    )
    gate_proj = dot(normed_two, gate_own)
    up_proj = dot(normed_two, up_own)
    sigmoid_gate = jax.nn.sigmoid(gate_proj)
    silu_gate = gate_proj * sigmoid_gate
    hidden_units = (silu_gate * up_proj).astype(jnp.bfloat16)
    hidden_grad = dot(all_grad, down_own, ((1,), (1,)))
    gate_act = (
        hidden_grad * up_proj * sigmoid_gate * (1.0 + gate_proj * (1.0 - sigmoid_gate))
    ).astype(jnp.bfloat16)
    up_act = (hidden_grad * silu_gate).astype(jnp.bfloat16)
    down_part = dot(hidden_units, all_grad, ((0,), (0,))).astype(jnp.bfloat16)
    gate_part = dot(normed_two, gate_act, ((0,), (0,))).astype(jnp.bfloat16)
    up_part = dot(normed_two, up_act, ((0,), (0,))).astype(jnp.bfloat16)
    normed_two_part = dot(gate_act, gate_own, ((1,), (1,))) + dot(up_act, up_own, ((1,), (1,)))
    layer_part = dot(hidden_units, down_own).astype(jnp.bfloat16)
    (
        layer_out,
        input_grad,
        *landed,
        gain_grads,
    ) = back(
        (rows, local, model, high_size),
        ends.reshape(-1),
        own_in,
        own_grad,
        residual,
        gains,
        normed_two_part.astype(jnp.bfloat16),
        layer_part,
        gate_part,
        up_part,
        down_part,
        qkv_own,
        output_own,
        normed_one,
        queries,
        kv,
        attn,
        cos,
        sin,
    )
    qkv_grad, output_grad, gate_grad, up_grad, down_grad = (
        part[0].astype(jnp.float32) + part[1].astype(jnp.float32) for part in landed
    )
    query_grad = qkv_grad[..., : group * HD].transpose(1, 0, 2).reshape(block, -1)
    key_grad = qkv_grad[..., group * HD : (group + 1) * HD].transpose(1, 0, 2).reshape(block, -1)
    value_grad = qkv_grad[..., (group + 1) * HD :].transpose(1, 0, 2).reshape(block, -1)
    return (
        layer_out.reshape(hidden_in.shape),
        input_grad.reshape(hidden_in.shape),
        gain_grads[0],
        query_grad,
        key_grad,
        value_grad,
        output_grad,
        gain_grads[1],
        gate_grad,
        up_grad,
        down_grad,
    )


def solution(mesh):
    return jax.shard_map(
        shards,
        mesh=mesh,
        in_specs=(
            P("dp", "seq", None),
            P("dp", None),
            P(("dp", "seq")),
            P(("dp", "seq"), "mp"),
            P(("dp", "seq"), "mp"),
            P(("dp", "seq"), "mp"),
            P("mp", ("dp", "seq")),
            P(("dp", "seq")),
            P(("dp", "seq"), "mp"),
            P(("dp", "seq"), "mp"),
            P("mp", ("dp", "seq")),
            P("dp", "seq", None),
        ),
        out_specs=(
            P("dp", "seq", None),
            P("dp", "seq", None),
            P(("dp", "seq")),
            P(("dp", "seq"), "mp"),
            P(("dp", "seq"), "mp"),
            P(("dp", "seq"), "mp"),
            P("mp", ("dp", "seq")),
            P(("dp", "seq")),
            P(("dp", "seq"), "mp"),
            P(("dp", "seq"), "mp"),
            P("mp", ("dp", "seq")),
        ),
        check_vma=False,
    )
```

```python
import functools
import math

import jax
import jax.numpy as jnp
from jax import lax
from jax.experimental import pallas as pl
from jax.experimental.pallas import tpu as pltpu
from jax.sharding import PartitionSpec as P

H = 32
KVH = 8
HD = 64
SQUARE = 4

EPSILON = 1e-05
MASKED = -1e30
ROPE_THETA = 500000.0
ROPE_FACTOR = 32.0
LOW_FACTOR = 1.0
HIGH_FACTOR = 4.0
PRIOR_CONTEXT = 8192.0
VMEM = 62 * 1024 * 1024


def inverse_freqs(head_dim):
    ladder = jnp.arange(head_dim // 2, dtype=jnp.float32)
    base = ROPE_THETA ** (-2.0 * ladder / head_dim)
    wavelen = 2.0 * math.pi / base
    smooth = (PRIOR_CONTEXT / wavelen - LOW_FACTOR) / (HIGH_FACTOR - LOW_FACTOR)
    blended = (1.0 - smooth) * base / ROPE_FACTOR + smooth * base
    low_limit = PRIOR_CONTEXT / LOW_FACTOR
    high_limit = PRIOR_CONTEXT / HIGH_FACTOR
    return jnp.where(
        wavelen < high_limit, base, jnp.where(wavelen > low_limit, base / ROPE_FACTOR, blended)
    )


def rope_tables(position, head_dim):
    angles = position[..., None] * inverse_freqs(head_dim)
    angles = jnp.concatenate([angles, angles], axis=-1)
    return (jnp.cos(angles)[..., None, :], jnp.sin(angles)[..., None, :])


def rotate(values, cosine, sine):
    middle = values.shape[-1] // 2
    turned = jnp.concatenate([-values[..., middle:], values[..., :middle]], axis=-1)
    return values * cosine + turned * sine


def unrotate(grads, cosine, sine):
    middle = grads.shape[-1] // 2
    scaled = grads * sine
    turned = jnp.concatenate([scaled[..., middle:], -scaled[..., :middle]], axis=-1)
    return grads * cosine + turned


def dot(left, right, dims=((1,), (0,))):
    return lax.dot_general(left, right, (dims, ((), ())), preferred_element_type=jnp.float32)


def swap(value, axis, mask):
    size = lax.axis_size(axis)
    return lax.ppermute(value, axis, [(i, i ^ mask) for i in range(size)])


def cut(value, start, length, axis):
    return lax.dynamic_slice_in_dim(value, start, length, axis)


def put(whole, part, start, axis):
    return lax.dynamic_update_slice_in_dim(whole, part, start, axis)


def mask_of(info, row, row_count, local, keys):
    span = SQUARE * local
    low, high = info[0], info[1]

    def place_of(index):
        block = (index // local) % SQUARE
        part = index // span
        return (high ^ part) * span + (low ^ block) * local + index % local

    def segment_of(place):
        total = jnp.zeros_like(place)
        for doc in range(4):
            total = total + (place >= info[2 + row * 4 + doc]).astype(jnp.int32)
        return total

    query = place_of(lax.broadcasted_iota(jnp.int32, (span, 1), 0))
    key = place_of(lax.broadcasted_iota(jnp.int32, (1, keys), 1))
    return (segment_of(query) == segment_of(key)) & (query >= key)


def attend_kernel(local, keys, group, info, q_ref, kv_ref, out_ref, lse_ref):
    row = pl.program_id(0)
    span = SQUARE * local
    allowed = mask_of(info, row, None, local, keys)
    kv = kv_ref[...].reshape(keys, 2 * HD)
    k, v = kv[:, :HD], kv[:, HD:]
    q_all = q_ref[...].reshape(span, group * HD)
    outs, sums = [], []
    for head in range(group):
        q = q_all[:, head * HD : (head + 1) * HD]
        score = dot(q, k, ((1,), (1,))) * HD ** (-0.5)
        score = jnp.where(allowed, score, MASKED)
        top = jnp.max(score, axis=1, keepdims=True)
        grown = jnp.exp(score - top)
        total = jnp.sum(grown, axis=1, keepdims=True)
        lse = top + jnp.log(total)
        probs = (grown * (1.0 / total)).astype(jnp.bfloat16)
        outs.append(dot(probs, v))
        sums.append(lse)
    out_ref[...] = jnp.concatenate(outs, axis=1).reshape(out_ref.shape)
    lse_ref[...] = jnp.concatenate(sums, axis=1).reshape(lse_ref.shape)


def attend(info, queries, kv):
    blocks, rows, local, width = queries.shape
    parts = kv.shape[0]
    keys = parts * blocks * local
    group = width // HD
    return pl.pallas_call(
        functools.partial(attend_kernel, local, keys, group),
        grid=(rows,),
        out_shape=(
            jax.ShapeDtypeStruct((blocks, rows, local, width), jnp.float32),
            jax.ShapeDtypeStruct((blocks, rows, local, group), jnp.float32),
        ),
        in_specs=[
            pl.BlockSpec(memory_space=pltpu.SMEM),
            pl.BlockSpec((blocks, 1, local, width), lambda r: (0, r, 0, 0)),
            pl.BlockSpec((parts, blocks, 1, local, 2 * HD), lambda r: (0, 0, r, 0, 0)),
        ],
        out_specs=(
            pl.BlockSpec((blocks, 1, local, width), lambda r: (0, r, 0, 0)),
            pl.BlockSpec((blocks, 1, local, group), lambda r: (0, r, 0, 0)),
        ),
        compiler_params=pltpu.CompilerParams(vmem_limit_bytes=VMEM),
        cost_estimate=pl.CostEstimate(
            flops=8 * rows * blocks * local * keys * width,
            bytes_accessed=rows * blocks * local * width * 8,
            transcendentals=rows * blocks * local * keys * group,
        ),
        name="attend",
    )(info, queries, kv)


def attend_back_kernel(
    local, keys, group, info, q_ref, kv_ref, go_ref, out_ref, lse_ref, dq_ref, dkv_ref
):
    row = pl.program_id(0)
    span = SQUARE * local
    allowed = mask_of(info, row, None, local, keys)
    kv = kv_ref[...].reshape(keys, 2 * HD)
    k, v = kv[:, :HD], kv[:, HD:]
    q_all = q_ref[...].reshape(span, group * HD)
    go_all = go_ref[...].reshape(span, group * HD)
    out_all = out_ref[...].reshape(span, group * HD)
    lse_all = lse_ref[...].reshape(span, group)
    dq = []
    dk = jnp.zeros((keys, HD), jnp.float32)
    dv = jnp.zeros((keys, HD), jnp.float32)
    scale = HD ** (-0.5)
    for head in range(group):
        q = q_all[:, head * HD : (head + 1) * HD]
        go = go_all[:, head * HD : (head + 1) * HD]
        out = out_all[:, head * HD : (head + 1) * HD]
        delta = jnp.sum(go.astype(jnp.float32) * out, axis=1, keepdims=True)
        score = dot(q, k, ((1,), (1,))) * scale
        probs = jnp.exp(jnp.where(allowed, score, MASKED) - lse_all[:, head : head + 1])
        dv = dv + dot(probs.astype(jnp.bfloat16), go, ((0,), (0,)))
        prob_grad = dot(go, v, ((1,), (1,)))
        score_grad = (probs * (prob_grad - delta)).astype(jnp.bfloat16)
        dq.append(dot(score_grad, k) * scale)
        dk = dk + dot(score_grad, q, ((0,), (0,)))
    dq_ref[...] = jnp.concatenate(dq, axis=1).reshape(dq_ref.shape)
    dkv_ref[...] = jnp.concatenate([dk * scale, dv], axis=1).reshape(dkv_ref.shape)


def attend_back(info, queries, kv, out_grads, out, lse):
    blocks, rows, local, width = queries.shape
    parts = kv.shape[0]
    keys = parts * blocks * local
    group = width // HD
    wide = pl.BlockSpec((blocks, 1, local, width), lambda r: (0, r, 0, 0))
    kv_spec = pl.BlockSpec((parts, blocks, 1, local, 2 * HD), lambda r: (0, 0, r, 0, 0))
    return pl.pallas_call(
        functools.partial(attend_back_kernel, local, keys, group),
        grid=(rows,),
        out_shape=(
            jax.ShapeDtypeStruct(queries.shape, jnp.float32),
            jax.ShapeDtypeStruct(kv.shape, jnp.float32),
        ),
        in_specs=[
            pl.BlockSpec(memory_space=pltpu.SMEM),
            wide,
            kv_spec,
            wide,
            wide,
            pl.BlockSpec((blocks, 1, local, group), lambda r: (0, r, 0, 0)),
        ],
        out_specs=(wide, kv_spec),
        compiler_params=pltpu.CompilerParams(vmem_limit_bytes=VMEM),
        cost_estimate=pl.CostEstimate(
            flops=20 * rows * blocks * local * keys * width,
            bytes_accessed=rows * blocks * local * width * 16,
            transcendentals=rows * blocks * local * keys * group,
        ),
        name="attend_back",
    )(info, queries, kv, out_grads, out, lse)


def bits_of(size):
    return [1 << b for b in range(size.bit_length() - 1)]


def spread_weight(shard, axis, place):
    dp, high, low, dp_size, high_size = place
    other = 1 - axis
    block = shard.shape[axis]
    width = shard.shape[other] // SQUARE
    pieces = [cut(shard, low * width, width, other)]
    for mask in range(1, SQUARE):
        pieces.append(swap(cut(shard, (low ^ mask) * width, width, other), "seq", mask))
    shape = [0, 0]
    shape[axis], shape[other] = SQUARE * block, width
    square = jnp.zeros(shape, shard.dtype)
    for mask in range(SQUARE):
        square = put(square, pieces[mask], (low ^ mask) * block, axis)
    parts = {(0, 0): square}
    for bit in bits_of(high_size):
        for (a, b) in list(parts):
            parts[a, b ^ bit] = swap(parts[a, b], "seq", SQUARE * bit)
    for bit in bits_of(dp_size):
        for (a, b) in list(parts):
            parts[a ^ bit, b] = swap(parts[a, b], "dp", bit)
    shape[axis] = SQUARE * block * high_size * dp_size
    whole = jnp.zeros(shape, shard.dtype)
    for (a, b), part in parts.items():
        index = (dp ^ a) * high_size + (high ^ b)
        whole = put(whole, part, index * SQUARE * block, axis)
    return whole


def settle_grad(grad, axis, place):
    dp, high, low, dp_size, high_size = place
    other = 1 - axis
    width = grad.shape[other]
    kept = grad
    for index, size, name, unit in ((dp, dp_size, "dp", 1), (high, high_size, "seq", SQUARE)):
        for bit in reversed(bits_of(size)):
            half = kept.shape[axis] // 2
            mine = (index // bit) % 2
            sent = cut(kept, (1 - mine) * half, half, axis).astype(jnp.bfloat16)
            kept = cut(kept, mine * half, half, axis) + swap(sent, name, unit * bit).astype(
                jnp.float32
            )
    block = kept.shape[axis] // SQUARE
    shape = [0, 0]
    shape[axis], shape[other] = block, SQUARE * width
    whole = jnp.zeros(shape, jnp.float32)
    whole = put(whole, cut(kept, low * block, block, axis), low * width, other)
    for mask in range(1, SQUARE):
        sent = cut(kept, (low ^ mask) * block, block, axis).astype(jnp.bfloat16)
        got = swap(sent, "seq", mask).astype(jnp.float32)
        whole = put(whole, got, (low ^ mask) * width, other)
    return whole


def gather_square(own, core):
    tokens, width = own.shape
    half = width // 2
    mine = cut(own, core * half, half, 1)
    got = jnp.concatenate([swap(mine, "seq", mask) for mask in range(1, SQUARE)], axis=0)
    across = swap(got, "mp", 1)
    first = jnp.where(core == 0, got, across)
    second = jnp.where(core == 0, across, got)
    return jnp.concatenate([own, jnp.concatenate([first, second], axis=1)], axis=0)


def scatter_square(partial, core):
    tokens, width = partial.shape[0] // SQUARE, partial.shape[1]
    half = width // 2
    kept = cut(partial, core * half, half, 1)
    sent = cut(partial, (1 - core) * half, half, 1).astype(jnp.bfloat16)
    kept = kept + swap(sent, "mp", 1).astype(jnp.float32)
    total = kept[:tokens]
    for mask in range(1, SQUARE):
        part = kept[mask * tokens : (mask + 1) * tokens].astype(jnp.bfloat16)
        total = total + swap(part, "seq", mask).astype(jnp.float32)
    mine = total.astype(jnp.bfloat16)
    across = swap(mine, "mp", 1)
    return jnp.concatenate(
        [jnp.where(core == 0, mine, across), jnp.where(core == 0, across, mine)], axis=1
    ).astype(jnp.float32)


MESH = pl.DeviceIdType.MESH


class Links:
    def __init__(self, send_sem, recv_sem, local_sem, high_size):
        self.send_sem, self.recv_sem, self.local_sem = send_sem, recv_sem, local_sem
        self.x, self.seq, self.core = (lax.axis_index(a) for a in ("dp", "seq", "mp"))
        self.high_size = high_size
        self.low, self.high = self.seq % SQUARE, self.seq // SQUARE
        self.count = self.local_count = 0
        self.sent = []

    def beside(self, flip):
        if flip == 1:
            return self.low + 1 - 2 * (self.low % 2)
        return (self.low + 2) % SQUARE if flip == 2 else SQUARE - 1 - self.low

    def to(self, dx=0, dh=0, dl=0, dc=0, flip=0):
        low = self.beside(flip) if flip else (self.low + dl) % SQUARE
        seq = ((self.high + dh) % self.high_size) * SQUARE + low
        return ((self.x + dx) % 2, seq, (self.core + dc) % 2)

    def copy(self, src, dst, **step):
        k = self.count
        self.count += 1
        made = pltpu.make_async_remote_copy(
            src_ref=src,
            dst_ref=dst,
            send_sem=self.send_sem.at[k],
            recv_sem=self.recv_sem.at[k],
            device_id=self.to(**step),
            device_id_type=MESH,
        )
        made.start()
        self.sent.append(made)
        return made

    def local(self, src, dst):
        k = self.local_count
        self.local_count += 1
        made = pltpu.make_async_copy(src, dst, self.local_sem.at[k])
        made.start()
        return made

    def greet(self, steps):
        barrier = pltpu.get_barrier_semaphore()
        for step in steps:
            pl.semaphore_signal(barrier, inc=1, device_id=self.to(**step), device_id_type=MESH)
        pl.semaphore_wait(barrier, len(steps))

    def left(self, copies):
        for made in copies:
            made.wait_send()
            self.sent = [one for one in self.sent if one is not made]

    def finish(self):
        for made in self.sent:
            made.wait_send()


def arrived(copies):
    for made in copies:
        made.wait_recv()


class Weight:
    def __init__(self, links, slice_of, spot):
        self.links, self.spot = links, spot
        l = links
        self.own = l.local(slice_of(l.low), spot(l.x, l.high, l.low, 1))
        self.near, self.far = [], []
        for dh in range(2):
            for dl in range(SQUARE):
                if dh or dl:
                    made = l.copy(
                        slice_of((l.low + dl) % SQUARE),
                        spot(l.x, l.high, l.low, 1),
                        dh=dh,
                        dl=dl,
                    )
                    (self.far if dh else self.near).append(made)

    def pass_near(self):
        self.own.wait()
        arrived(self.near)
        l = self.links
        part = self.spot(l.x, l.high, 0, SQUARE)
        self.across = [l.copy(part, part, dx=1)]

    def pass_far(self):
        arrived(self.far)
        l = self.links
        part = self.spot(l.x, 1 - l.high, 0, SQUARE)
        self.across.append(l.copy(part, part, dx=1))

    def wait(self):
        arrived(self.across)


def gather_push(l, everyone, source):
    return [
        l.copy(source(part), everyone(l.core, l.low, part), flip=flip)
        for flip, part in ((1, 0), (2, 1), (1, 1), (2, 0))
    ]


def gather_across(l, everyone, pushed):
    handed, corner = [], []
    for k, (flip, part) in enumerate(((1, 0), (2, 1), (1, 1), (2, 0))):
        pushed[k].wait_recv()
        block = everyone(l.core, l.beside(flip), part)
        if k < 2:
            corner.append(l.copy(block, block, flip=3 - flip))
        handed.append(l.copy(block, block, dc=1))
    for part in range(2):
        corner[part].wait_recv()
        block = everyone(l.core, l.beside(3), part)
        handed.append(l.copy(block, block, dc=1))
    return handed, corner


def square_push(l, total_of, send, relay, landed):
    lines = send.shape[1]
    first, second = pl.ds(0, lines // 2), pl.ds(lines // 2, lines // 2)
    one, two, corner = (l.beside(flip) for flip in (1, 2, 3))
    send[corner] = total_of(corner).astype(jnp.bfloat16)
    made = [
        l.copy(send.at[corner, first], relay.at[0], flip=1),
        l.copy(send.at[corner, second], relay.at[1], flip=2),
    ]
    send[one] = total_of(one).astype(jnp.bfloat16)
    made.append(l.copy(send.at[one, first], landed.at[0, first], flip=1))
    send[two] = total_of(two).astype(jnp.bfloat16)
    made.append(l.copy(send.at[two, second], landed.at[1, second], flip=2))
    made[0].wait_recv()
    value = send[two, first].astype(jnp.float32) + relay[0].astype(jnp.float32)
    send[two, first] = value.astype(jnp.bfloat16)
    made.append(l.copy(send.at[two, first], landed.at[1, first], flip=2))
    made[1].wait_recv()
    value = send[one, second].astype(jnp.float32) + relay[1].astype(jnp.float32)
    send[one, second] = value.astype(jnp.bfloat16)
    made.append(l.copy(send.at[one, second], landed.at[0, second], flip=1))
    return made


def square_settle(l, total_of, made, landed, both):
    total = total_of(l.low)
    arrived(made[2:])
    total = total + landed[0].astype(jnp.float32) + landed[1].astype(jnp.float32)
    both[l.core] = total.astype(jnp.bfloat16)
    return l.copy(both.at[l.core], both.at[l.core], dc=1)


def roll_heads(value):
    width = value.shape[1]
    lane = lax.broadcasted_iota(jnp.int32, value.shape, 1)
    left = pltpu.roll(value, width - HD // 2, 1)
    right = pltpu.roll(value, HD // 2, 1)
    return jnp.where(lane % HD < HD // 2, left, right)


def rope_rows(cos, sin, at, copies):
    return (
        jnp.concatenate([cos[at]] * copies, axis=1),
        jnp.concatenate([sin[at]] * copies, axis=1),
    )


def rope_key_rows(cos, sin, at):
    lane = lax.broadcasted_iota(jnp.int32, (1, 2 * HD), 1)
    return (jnp.where(lane < HD, cos[at], 1.0), jnp.where(lane < HD, sin[at], 0.0))


def allowed_keys(l, lengths, row, span, keys):
    def segment_of(place):
        total = jnp.zeros_like(place)
        end = lengths[row * 4]
        for doc in range(4):
            if doc:
                end = end + lengths[row * 4 + doc]
            total = total + (place >= end).astype(jnp.int32)
        return total

    query = l.high * span + lax.broadcasted_iota(jnp.int32, (span, 1), 0)
    key = lax.broadcasted_iota(jnp.int32, (1, keys), 1)
    return (segment_of(query) == segment_of(key)) & (query >= key)


def front_kernel(
    sizes,
    lengths,
    x_in,
    g_in,
    qkv_in,
    gain_in,
    wo_in,
    wg_in,
    wu_in,
    wd_in,
    cos_in,
    sin_in,
    qkv_out,
    wo_out,
    gain_out,
    normed_one_out,
    q_out,
    kv_out,
    attn_out,
    residual_out,
    dwg_out,
    dwu_out,
    dwd_out,
    normed_two_part,
    layer_part,
    x_all,
    normed,
    wqkv,
    wo,
    gains,
    gain_rows,
    cos,
    sin,
    q,
    kv,
    attn,
    low_attn,
    send_core,
    recv_core,
    send_block,
    recv_block,
    relay,
    both,
    residual,
    normed_two,
    g_all,
    wg,
    wu,
    wd,
    hidden,
    gate_act,
    up_act,
    send_sem,
    recv_sem,
    local_sem,
):
    rows, local, model, high_size = sizes
    own = rows * local
    tokens = SQUARE * own
    half = model // 2
    block = qkv_in.shape[0]
    heads = q.shape[2] // HD
    span = SQUARE * local
    keys = high_size * span
    l = Links(send_sem, recv_sem, local_sem, high_size)
    near = [dict(dl=dl) for dl in range(1, SQUARE)]
    far = [dict(dh=1, dl=dl) for dl in range(SQUARE)]
    l.greet(near + far + [dict(dx=1), dict(dc=1)])

    def row_spot(ref):
        def spot(x, h, low, n):
            start = ((x * high_size + h) * SQUARE + low) * block
            return ref.at[pl.ds(pl.multiple_of(start, block), n * block)]

        return spot

    def block_spot(ref):
        return lambda x, h, low, n: ref.at[pl.ds((x * high_size + h) * SQUARE + low, n)]

    def half_spot(ref):
        def spot(x, h, low, n):
            start = pl.multiple_of((h * SQUARE + low) * block, block)
            return ref.at[x, :, pl.ds(start, n * block)]

        return spot

    def row_half_spot(ref):
        def spot(x, h, low, n):
            start = pl.multiple_of((h * SQUARE + low) * block, block)
            return ref.at[x, pl.ds(start, n * block)]

        return spot

    def columns(ref, width):
        return lambda j: ref.at[:, pl.ds(pl.multiple_of(j * width, width), width)]

    def lines(ref, width):
        return lambda j: ref.at[pl.ds(pl.multiple_of(j * width, width), width)]

    def part_at(low, part):
        if part is None:
            return pl.ds(pl.multiple_of(low * own, own), own)
        return pl.ds(pl.multiple_of(low * own + part * (own // 2), own // 2), own // 2)

    def x_spot(side, low, part=None):
        return x_all.at[side, part_at(low, part)]

    def g_spot(side, low, part=None):
        return g_all.at[side, part_at(low, part)]

    def normed_two_spot(side, low, part=None):
        return normed_two.at[side, part_at(low, part)]

    def own_part_of(ref):
        return lambda part: ref.at[
            pl.ds(part * (own // 2), own // 2), pl.ds(pl.multiple_of(l.core * half, half), half)
        ]

    def side_of(ref, side):
        return ref.at[:, pl.ds(pl.multiple_of(side * half, half), half)]

    loads = [l.local(side_of(x_in, side), x_spot(side, l.low)) for side in range(2)]
    loads += [l.local(cos_in, cos), l.local(sin_in, sin)]
    w_gain = Weight(l, lambda j: gain_in.at[pl.ds(0, 1)], block_spot(gains))
    w_qkv = Weight(l, columns(qkv_in, wqkv.shape[1]), row_spot(wqkv))
    x_pushed = gather_push(l, x_spot, own_part_of(x_in))
    w_o = Weight(l, lines(wo_in, wo.shape[1]), half_spot(wo))
    w_gate = Weight(l, columns(wg_in, wg.shape[2]), row_half_spot(wg))

    w_gain.pass_near()
    w_qkv.pass_near()
    x_handed, _ = gather_across(l, x_spot, x_pushed)
    w_gain.pass_far()
    w_qkv.pass_far()
    w_o.pass_near()
    w_o.pass_far()
    for made in loads:
        made.wait()
    w_gain.wait()
    for b in range(gains.shape[0]):
        tile = gains[b].astype(jnp.float32)
        gain_rows[0:1, b * block : (b + 1) * block] = tile[0:1]
        gain_rows[1:2, b * block : (b + 1) * block] = tile[1:2]
    arrived(x_handed)

    step = 128

    def norm_step(i, carry):
        at = pl.ds(pl.multiple_of(i * step, step), step)
        first, second = x_all[0, at].astype(jnp.float32), x_all[1, at].astype(jnp.float32)
        total = jnp.sum(first * first, axis=1, keepdims=True)
        total = total + jnp.sum(second * second, axis=1, keepdims=True)
        scale = lax.rsqrt(total / model + EPSILON)
        normed[0, at] = (first * scale * gain_rows[0:1, :half]).astype(jnp.bfloat16)
        normed[1, at] = (second * scale * gain_rows[0:1, half:]).astype(jnp.bfloat16)
        return carry

    lax.fori_loop(0, tokens // step, norm_step, 0)
    normed_store = l.local(normed, normed_one_out)
    stores = []
    w_qkv.wait()
    stores += [l.local(wqkv, qkv_out), l.local(gain_rows, gain_out)]

    def project_step(i, carry):
        at = pl.ds(pl.multiple_of(i * local, local), local)
        pre = dot(normed[0, at], wqkv[:half]) + dot(normed[1, at], wqkv[half:])
        cos_q, sin_q = rope_rows(cos, sin, at, heads // 2)
        cos_k, sin_k = rope_key_rows(cos, sin, at)
        cos_all = jnp.concatenate([cos_q, cos_k], axis=1)
        sin_all = jnp.concatenate([sin_q, sin_k], axis=1)
        turned = pre * cos_all + roll_heads(pre) * sin_all
        spot = pl.ds(pl.multiple_of((i // rows) * local, local), local)
        q[i % rows, spot] = (turned[:, : heads * HD].astype(jnp.bfloat16) * HD ** (-0.5)).astype(
            jnp.bfloat16
        )
        kv[l.high, i % rows, spot] = turned[:, heads * HD :].astype(jnp.bfloat16)
        return carry

    lax.fori_loop(0, SQUARE * rows, project_step, 0)
    kv_copy = l.copy(kv.at[l.high], kv.at[l.high], dh=1)
    stores.append(l.local(q, q_out))
    w_gate.pass_near()
    w_up = Weight(l, columns(wu_in, wu.shape[2]), row_half_spot(wu))
    kv_copy.wait_recv()
    stores.append(l.local(kv, kv_out))

    def attend_row(r, carry):
        allowed = allowed_keys(l, lengths, r, span, keys)
        kv_row = kv[:, r].reshape(keys, 2 * HD)
        k, v = kv_row[:, :HD], kv_row[:, HD:]
        q_row = q[r]
        outs = []
        for head in range(heads):
            score = dot(q_row[:, head * HD : (head + 1) * HD], k, ((1,), (1,)))
            score = jnp.where(allowed, score, MASKED)
            top = jnp.max(score, axis=1, keepdims=True)
            grown = jnp.exp(score - top)
            total = jnp.sum(grown, axis=1, keepdims=True)
            probs = (grown * (1.0 / total)).astype(jnp.bfloat16)
            outs.append(dot(probs, v))
        out = jnp.concatenate(outs, axis=1)
        for j in range(SQUARE):
            at = pl.ds(pl.multiple_of(j * own + r * local, local), local)
            part = out[j * local : (j + 1) * local]
            attn[at] = part
            low_attn[at] = part.astype(jnp.bfloat16)
        return carry

    lax.fori_loop(0, rows, attend_row, 0)
    stores.append(l.local(attn, attn_out))
    w_gate.pass_far()
    w_o.wait()
    stores.append(l.local(wo, wo_out))

    def project_out(j, side):
        at = pl.ds(pl.multiple_of(j * own, own), own)
        return dot(low_attn[at], wo[side])

    handed = []
    for j in range(SQUARE):
        send_core[j] = project_out(j, 1 - l.core).astype(jnp.bfloat16)
        handed.append(l.copy(send_core.at[j], recv_core.at[j], dc=1))
    arrived(handed)

    def total_out(j):
        return project_out(j, l.core) + recv_core[j].astype(jnp.float32)

    pushed = square_push(l, total_out, send_block, relay, recv_block)
    w_up.pass_near()
    square_settle(l, total_out, pushed, recv_block, both).wait_recv()
    at_own = pl.ds(pl.multiple_of(l.low * own, own), own)
    total = jnp.zeros((own, 1), jnp.float32)
    for side in range(2):
        value = x_all[side, at_own].astype(jnp.float32) + both[side].astype(jnp.float32)
        residual[:, side * half : (side + 1) * half] = value
        total = total + jnp.sum(value * value, axis=1, keepdims=True)
    scale = lax.rsqrt(total / model + EPSILON)
    for side in range(2):
        at = slice(side * half, (side + 1) * half)
        normed_two[side, at_own] = (residual[:, at] * scale * gain_rows[1:2, at]).astype(
            jnp.bfloat16
        )
    stores.append(l.local(residual, residual_out))
    pushed = gather_push(
        l, normed_two_spot, lambda part: normed_two_spot(l.core, l.low, part)
    )
    w_up.pass_far()
    w_down = Weight(l, lines(wd_in, wd.shape[1]), half_spot(wd))
    handed, _ = gather_across(l, normed_two_spot, pushed)
    loads = [l.local(side_of(g_in, side), g_spot(side, l.low)) for side in range(2)]
    g_pushed = gather_push(l, g_spot, own_part_of(g_in))
    w_down.pass_near()
    arrived(handed)
    normed_store.wait()
    w_gate.wait()
    w_up.wait()

    def unit_step(j, carry):
        at = part_at(j, None)
        first, second = normed_two[0, at], normed_two[1, at]
        gate = dot(first, wg[0]) + dot(second, wg[1])
        up = dot(first, wu[0]) + dot(second, wu[1])
        sigmoid = jax.nn.sigmoid(gate)
        silu = gate * sigmoid
        hidden[at] = (silu * up).astype(jnp.bfloat16)
        gate_act[at] = (up * sigmoid * (1.0 + gate * (1.0 - sigmoid))).astype(jnp.bfloat16)
        up_act[at] = silu.astype(jnp.bfloat16)
        return carry

    lax.fori_loop(0, SQUARE, unit_step, 0)
    g_handed, _ = gather_across(l, g_spot, g_pushed)
    w_down.pass_far()
    for made in loads:
        made.wait()
    arrived(g_handed)
    busy = [(0, None), (1, None)]

    def fill(product, out):
        k, made = busy.pop(0)
        if made is not None:
            made.wait()
        buffer = normed.at[k]

        def step(i, carry):
            at = pl.ds(pl.multiple_of(i * own, own), own)
            buffer[at] = product(at).astype(jnp.bfloat16)
            return carry

        lax.fori_loop(0, half // own, step, 0)
        busy.append((k, l.local(buffer, out)))

    for side in range(2):
        fill(
            lambda at, side=side: dot(hidden[:, at], g_all[side], ((0,), (0,))),
            dwd_out.at[side],
        )
    w_down.wait()

    def act_step(j, carry):
        at = part_at(j, None)
        grad = dot(g_all[0, at], wd[0], ((1,), (1,))) + dot(g_all[1, at], wd[1], ((1,), (1,)))
        gate_act[at] = (grad * gate_act[at].astype(jnp.float32)).astype(jnp.bfloat16)
        up_act[at] = (grad * up_act[at].astype(jnp.float32)).astype(jnp.bfloat16)
        return carry

    lax.fori_loop(0, SQUARE, act_step, 0)
    for side in range(2):
        fill(
            lambda at, side=side: dot(gate_act[at], wg[side], ((1,), (1,)))
            + dot(up_act[at], wu[side], ((1,), (1,))),
            normed_two_part.at[side],
        )
    for side in range(2):
        fill(lambda at, side=side: dot(hidden[at], wd[side]), layer_part.at[side])
    for act, out in ((gate_act, dwg_out), (up_act, dwu_out)):
        for side in range(2):
            fill(
                lambda at, side=side, act=act: dot(
                    normed_two[side, :, at], act[...], ((0,), (0,))
                ),
                out.at[side],
            )
    for _, made in busy:
        made.wait()
    for made in stores:
        made.wait()
    l.finish()


def front(sizes, lengths, x, g, qkv, gain, wo, wg, wu, wd, cos, sin):
    rows, local, model, high_size = sizes
    own = rows * local
    tokens = SQUARE * own
    half = model // 2
    heads = wo.shape[0] // SQUARE // HD
    width = qkv.shape[1] // SQUARE
    ff = wg.shape[1] // SQUARE
    blocks = model // qkv.shape[0]
    span = SQUARE * local
    low, f32 = jnp.bfloat16, jnp.float32
    shape = jax.ShapeDtypeStruct
    outs = (
        shape((model, width), low),
        shape((2, heads * HD, half), low),
        shape((8, model), f32),
        shape((2, tokens, half), low),
        shape((rows, span, heads * HD), low),
        shape((high_size, rows, span, 2 * HD), low),
        shape((tokens, heads * HD), f32),
        shape((own, model), f32),
        shape((2, half, ff), low),
        shape((2, half, ff), low),
        shape((2, ff, half), low),
        shape((2, tokens, half), low),
        shape((2, tokens, half), low),
    )
    anywhere = pl.BlockSpec(memory_space=pl.ANY)
    vmem = pltpu.VMEM
    return pl.pallas_call(
        functools.partial(front_kernel, sizes),
        out_shape=outs,
        in_specs=[pl.BlockSpec(memory_space=pltpu.SMEM)] + [anywhere] * 10,
        out_specs=[anywhere] * len(outs),
        scratch_shapes=[
            vmem((2, tokens, half), low),
            vmem((2, tokens, half), low),
            vmem((model, width), low),
            vmem((2, heads * HD, half), low),
            vmem((blocks,) + gain.shape[1:], low),
            vmem((8, model), f32),
            vmem((tokens, 2 * HD), f32),
            vmem((tokens, 2 * HD), f32),
            vmem((rows, span, heads * HD), low),
            vmem((high_size, rows, span, 2 * HD), low),
            vmem((tokens, heads * HD), f32),
            vmem((tokens, heads * HD), low),
            vmem((SQUARE, own, half), low),
            vmem((SQUARE, own, half), low),
            vmem((SQUARE, own, half), low),
            vmem((2, own, half), low),
            vmem((2, own // 2, half), low),
            vmem((2, own, half), low),
            vmem((own, model), f32),
            vmem((2, tokens, half), low),
            vmem((2, tokens, half), low),
            vmem((2, half, ff), low),
            vmem((2, half, ff), low),
            vmem((2, ff, half), low),
            vmem((tokens, ff), low),
            vmem((tokens, ff), low),
            vmem((tokens, ff), low),
            pltpu.SemaphoreType.DMA((128,)),
            pltpu.SemaphoreType.DMA((128,)),
            pltpu.SemaphoreType.DMA((32,)),
        ],
        compiler_params=pltpu.CompilerParams(
            collective_id=0, has_side_effects=True, vmem_limit_bytes=VMEM
        ),
        name="front",
    )(lengths, x, g, qkv, gain, wo, wg, wu, wd, cos, sin)


class Grad:
    def __init__(self, links, half_of, kept, crossed, block_of, landed):
        self.links, self.kept, self.crossed = links, kept, crossed
        self.block_of, self.landed = block_of, landed
        l = links
        self.own = l.local(half_of(l.x), kept) if half_of else None
        if half_of:
            self.cross = l.copy(half_of(1 - l.x), crossed, dx=1)

    def deal(self):
        l = self.links
        if self.own is not None:
            self.own.wait()
        self.cross.wait_recv()
        kept, crossed = self.kept, self.crossed
        lines = kept.shape[0]
        step = min(128, lines)

        def add(i, carry):
            at = pl.ds(pl.multiple_of(i * step, step), step)
            kept[at] = (kept[at].astype(jnp.float32) + crossed[at].astype(jnp.float32)).astype(
                jnp.bfloat16
            )
            return carry

        lax.fori_loop(0, lines // step, add, 0)
        self.dealt = []
        for dh in range(2):
            for dl in range(SQUARE):
                if dh or dl:
                    block = self.block_of((l.high + dh) % 2, (l.low + dl) % SQUARE)
                    self.dealt.append(
                        l.copy(block, self.landed(l.high, l.low), dh=dh, dl=dl)
                    )
        self.mine = l.local(self.block_of(l.high, l.low), self.landed(l.high, l.low))


def back_kernel(
    sizes,
    lengths,
    x_in,
    g_in,
    residual_in,
    gain_in,
    normed_two_part,
    layer_part,
    dwg_in,
    dwu_in,
    dwd_in,
    qkv_in,
    wo_in,
    normed_one_in,
    q_in,
    kv_in,
    attn_in,
    cos_in,
    sin_in,
    layer_out,
    input_out,
    land_q,
    land_o,
    land_g,
    land_u,
    land_d,
    gains_out,
    kept_g,
    kept_u,
    kept_d,
    cross_g,
    cross_u,
    cross_d,
    kept_q,
    cross_q,
    kept_o,
    cross_o,
    send_q,
    send_o,
    own_a,
    recv_core,
    recv_block,
    relay,
    recv_block_b,
    relay_b,
    both,
    both_b,
    x_own,
    g_own,
    residual,
    gain_rows,
    low_all,
    wqkv,
    wo,
    q,
    kv,
    attn,
    attn_grad,
    dkv,
    dkv_send,
    dkv_recv,
    dqkv,
    cos,
    sin,
    gain_send,
    gain_recv,
    out_low,
    gain_sum,
    send_sem,
    recv_sem,
    local_sem,
):
    rows, local, model, high_size = sizes
    own = rows * local
    tokens = SQUARE * own
    half = model // 2
    block = x_own.shape[1] // 16
    heads = q.shape[2] // HD
    span = SQUARE * local
    keys = high_size * span
    f32, b16 = jnp.float32, jnp.bfloat16
    l = Links(send_sem, recv_sem, local_sem, high_size)
    steps = [
        dict(dx=dx, dh=dh, dl=dl)
        for dx in range(2)
        for dh in range(2)
        for dl in range(SQUARE)
        if dx or dh or dl
    ]
    l.greet(steps + [dict(dc=1)])

    def row_block(ref):
        def at(h, low):
            start = pl.multiple_of((h * SQUARE + low) * block, block)
            return ref.at[pl.ds(start, block)]

        return at

    def column_block(ref):
        def at(h, low):
            start = pl.multiple_of((h * SQUARE + low) * block, block)
            return ref.at[:, pl.ds(start, block)]

        return at

    def tall(ref):
        lines = ref.shape[1] // SQUARE
        return lambda h, low: ref.at[h, pl.ds(pl.multiple_of(low * lines, lines), lines)]

    def broad(ref):
        wide = ref.shape[2] // SQUARE
        return lambda h, low: ref.at[h, :, pl.ds(pl.multiple_of(low * wide, wide), wide)]

    def block_at(j):
        return pl.ds(pl.multiple_of(j * own, own), own)

    def part_at(ref, j, side):
        return ref.at[side, block_at(j)]

    handed = [
        l.copy(part_at(normed_two_part, j, 1 - l.core), recv_core.at[j], dc=1)
        for j in range(SQUARE)
    ]
    owned = [l.local(part_at(normed_two_part, j, l.core), own_a.at[j]) for j in range(SQUARE)]
    loads = [
        l.local(residual_in, residual),
        l.local(gain_in, gain_rows),
        l.local(g_in, g_own),
    ]
    grad_d = Grad(
        l, lambda x: dwd_in.at[x], kept_d, cross_d, column_block(kept_d), tall(land_d)
    )
    later = [
        l.local(x_in, x_own),
        l.local(wo_in, wo),
        l.local(attn_in, attn),
        l.local(q_in, q),
        l.local(kv_in, kv),
        l.local(qkv_in, wqkv),
        l.local(cos_in, cos),
        l.local(sin_in, sin),
    ]

    def own_total(j):
        return own_a[j].astype(f32) + recv_core[j].astype(f32)

    def norm_back(value_of, gain_row, grads):
        squares = jnp.zeros((own, 1), f32)
        inner = jnp.zeros((own, 1), f32)
        for side in range(2):
            at = slice(side * half, (side + 1) * half)
            value = value_of(side)
            squares = squares + jnp.sum(value * value, axis=1, keepdims=True)
            weighted = grads[side].astype(f32) * gain_rows[gain_row : gain_row + 1, at]
            inner = inner + jnp.sum(weighted * value, axis=1, keepdims=True)
        scale = lax.rsqrt(squares / model + EPSILON)
        pull = scale * scale * scale * (inner / model)
        outs = []
        for side in range(2):
            at = slice(side * half, (side + 1) * half)
            value = value_of(side)
            grad = grads[side].astype(f32)
            summed = jnp.sum(grad * (value * scale), axis=0, keepdims=True)
            for b in range(half // block):
                gain_send[gain_row, side * (half // block) + b, 0:1] = summed[
                    :, b * block : (b + 1) * block
                ]
            weighted = grad * gain_rows[gain_row : gain_row + 1, at]
            outs.append(weighted * scale - value * pull)
        return outs

    def push_gains(gain_row):
        me = (l.x * 2 + l.high) * SQUARE + l.low
        made = []
        for step in steps:
            to = ((l.x + step["dx"]) % 2 * 2 + (l.high + step["dh"]) % 2) * SQUARE + (
                l.low + step["dl"]
            ) % SQUARE
            made.append(l.copy(gain_send.at[gain_row, to], gain_recv.at[gain_row, me], **step))
        return made, l.local(gain_send.at[gain_row, me], gain_recv.at[gain_row, me])

    for made in owned:
        made.wait()
    arrived(handed)

    pushed = square_push(l, own_total, own_a, relay, recv_block)
    for made in loads:
        made.wait()
    swapped = square_settle(l, own_total, pushed, recv_block, both)
    swapped.wait_recv()
    l.left(pushed + [swapped])
    outs = norm_back(
        lambda side: residual[:, side * half : (side + 1) * half], 1, [both[0], both[1]]
    )
    for side in range(2):
        at = slice(side * half, (side + 1) * half)
        value = g_own[:, at].astype(f32) + outs[side]
        residual[:, at] = value
        low_all[side, block_at(l.low)] = value.astype(b16)

    def low_spot(side, low, part):
        start = pl.multiple_of(low * own + part * (own // 2), own // 2)
        return low_all.at[side, pl.ds(start, own // 2)]

    low_pushed = gather_push(l, low_spot, lambda part: low_spot(l.core, l.low, part))
    grad_g = Grad(l, lambda x: dwg_in.at[x], kept_g, cross_g, row_block(kept_g), broad(land_g))
    ffn_gains = push_gains(1)
    handed_b = [
        l.copy(part_at(layer_part, j, 1 - l.core), recv_core.at[j], dc=1) for j in range(SQUARE)
    ]
    owned = [l.local(part_at(layer_part, j, l.core), own_a.at[j]) for j in range(SQUARE)]
    for made in later:
        made.wait()
    low_handed, low_corner = gather_across(l, low_spot, low_pushed)
    grad_d.deal()
    arrived(low_handed)
    grad_u = Grad(l, lambda x: dwu_in.at[x], kept_u, cross_u, row_block(kept_u), broad(land_u))

    def out_grad_step(j, carry):
        at = block_at(j)
        rows_at = attn[at].astype(b16)
        low_out = dot(low_all[0, at], wo[0], ((1,), (1,)))
        low_out = (low_out + dot(low_all[1, at], wo[1], ((1,), (1,)))).astype(b16)
        for r in range(rows):
            spot = pl.ds(pl.multiple_of(j * local, local), local)
            attn_grad[r, spot] = low_out[r * local : (r + 1) * local]
        out_low[at] = rows_at
        return carry

    lax.fori_loop(0, SQUARE, out_grad_step, 0)
    send_o[...] = dot(out_low[...], low_all[1 - l.x], ((0,), (0,))).astype(b16)
    grad_o = Grad(l, None, kept_o, cross_o, column_block(kept_o), tall(land_o))
    grad_o.cross = l.copy(send_o, cross_o, dx=1)
    kept_o[...] = dot(out_low[...], low_all[l.x], ((0,), (0,))).astype(b16)

    for made in owned:
        made.wait()
    arrived(handed_b)
    pushed_b = square_push(l, own_total, own_a, relay_b, recv_block_b)

    def attend_row(r, carry):
        allowed = allowed_keys(l, lengths, r, span, keys)
        kv_row = kv[:, r].reshape(keys, 2 * HD)
        k, v = kv_row[:, :HD], kv_row[:, HD:]
        q_row, go_row = q[r], attn_grad[r]
        out_row = jnp.concatenate(
            [
                attn[pl.ds(pl.multiple_of(j * own + r * local, local), local)]
                for j in range(SQUARE)
            ],
            axis=0,
        )
        grads = []
        dk = jnp.zeros((keys, HD), f32)
        dv = jnp.zeros((keys, HD), f32)
        for head in range(heads):
            at = slice(head * HD, (head + 1) * HD)
            qh, go = q_row[:, at], go_row[:, at]
            delta = jnp.sum(go.astype(f32) * out_row[:, at], axis=1, keepdims=True)
            score = jnp.where(allowed, dot(qh, k, ((1,), (1,))), MASKED)
            top = jnp.max(score, axis=1, keepdims=True)
            grown = jnp.exp(score - top)
            probs = grown * (1.0 / jnp.sum(grown, axis=1, keepdims=True))
            dv = dv + dot(probs.astype(b16), go, ((0,), (0,)))
            pull = dot(go, v, ((1,), (1,)))
            score_grad = (probs * (pull - delta)).astype(b16)
            grads.append(dot(score_grad, k) * HD ** (-0.5))
            dk = dk + dot(score_grad, qh, ((0,), (0,)))
        turned = jnp.concatenate(grads, axis=1)
        for j in range(SQUARE):
            at = pl.ds(pl.multiple_of(j * own + r * local, local), local)
            value = turned[j * local : (j + 1) * local]
            cos_q, sin_q = rope_rows(cos, sin, at, heads // 2)
            dqkv[at, : heads * HD] = (value * cos_q - roll_heads(value) * sin_q).astype(b16)
        both_kv = jnp.concatenate([dk, dv], axis=1)
        for part in range(high_size):
            dkv[part, r] = both_kv[part * span : (part + 1) * span]
        return carry

    lax.fori_loop(0, 1, attend_row, 0)
    grad_g.deal()
    lax.fori_loop(1, rows, attend_row, 0)
    dkv_send[...] = dkv[1 - l.high].astype(b16)
    dkv_copy = l.copy(dkv_send, dkv_recv, dh=1)
    l.left(low_pushed + low_handed + low_corner)
    normed = l.local(normed_one_in, low_all)
    grad_o.deal()
    both_b_copy = square_settle(l, own_total, pushed_b, recv_block_b, both_b)
    dkv_copy.wait_recv()

    def unrotate_step(i, carry):
        at = pl.ds(pl.multiple_of(i * local, local), local)
        spot = pl.ds(pl.multiple_of((i // rows) * local, local), local)
        kv_sum = dkv[l.high, i % rows, spot] + dkv_recv[i % rows, spot].astype(f32)
        cos_k, sin_k = rope_key_rows(cos, sin, at)
        turned = kv_sum * cos_k - roll_heads(kv_sum) * sin_k
        dqkv[at, heads * HD :] = turned.astype(b16)
        return carry

    lax.fori_loop(0, SQUARE * rows, unrotate_step, 0)

    def project_back(j, side):
        weight = wqkv[pl.ds(pl.multiple_of(side * half, half), half)]
        return dot(dqkv[block_at(j)], weight, ((1,), (1,)))

    both_b_copy.wait_recv()
    l.left(pushed_b)
    handed = []
    for j in range(SQUARE):
        own_a[j] = project_back(j, 1 - l.core).astype(b16)
        handed.append(l.copy(own_a.at[j], recv_core.at[j], dc=1))
    normed.wait()
    send_q[...] = dot(low_all[1 - l.x], dqkv[...], ((0,), (0,))).astype(b16)
    arrived(handed)

    def own_total_c(j):
        return project_back(j, l.core) + recv_core[j].astype(f32)

    l.left(handed)
    pushed = square_push(l, own_total_c, own_a, relay, recv_block)
    grad_q = Grad(l, None, kept_q, cross_q, row_block(kept_q), lambda h, low: land_q.at[h, low])
    grad_q.cross = l.copy(send_q, cross_q, dx=1)
    kept_q[...] = dot(low_all[l.x], dqkv[...], ((0,), (0,))).astype(b16)
    grad_u.deal()
    square_settle(l, own_total_c, pushed, recv_block, both).wait_recv()
    outs = norm_back(
        lambda side: x_own[:, side * half : (side + 1) * half].astype(f32),
        0,
        [both[0], both[1]],
    )
    attn_gains = push_gains(0)
    for side in range(2):
        at = slice(side * half, (side + 1) * half)
        x_own[:, at] = (residual[:, at] + outs[side]).astype(b16)
    stores = [l.local(x_own, input_out)]
    residual_load = l.local(residual_in, residual)
    grad_q.deal()
    residual_load.wait()
    for side in range(2):
        at = slice(side * half, (side + 1) * half)
        g_own[:, at] = (residual[:, at] + both_b[side].astype(f32)).astype(b16)
    stores.append(l.local(g_own, layer_out))
    for made, kept in (ffn_gains, attn_gains):
        arrived(made)
        kept.wait()
    for row in range(2):
        total = jnp.zeros((8, block), f32)
        for b in range(16):
            total = total + gain_recv[row, b]
        gain_sum[row : row + 1] = total[0:1]
    stores.append(l.local(gain_sum, gains_out))
    for grad in (grad_d, grad_o, grad_g, grad_u, grad_q):
        grad.mine.wait()
        arrived(grad.dealt)
    for made in stores:
        made.wait()
    l.finish()


def back(sizes, lengths, *arrays):
    rows, local, model, high_size = sizes
    own = rows * local
    tokens = SQUARE * own
    half = model // 2
    block = model // 16
    ff = arrays[6].shape[2]
    width = arrays[9].shape[1]
    wide = width - 2 * HD
    span = SQUARE * local
    b16, f32 = jnp.bfloat16, jnp.float32
    shape = jax.ShapeDtypeStruct
    vmem = pltpu.VMEM
    outs = (
        shape((own, model), b16),
        shape((own, model), b16),
        shape((2, SQUARE, block, width), b16),
        shape((2, SQUARE * wide, block), b16),
        shape((2, block, SQUARE * ff), b16),
        shape((2, block, SQUARE * ff), b16),
        shape((2, SQUARE * ff, block), b16),
        shape((8, block), f32),
    )
    anywhere = pl.BlockSpec(memory_space=pl.ANY)
    scratch = [
        vmem((half, ff), b16),
        vmem((half, ff), b16),
        vmem((ff, half), b16),
        vmem((half, ff), b16),
        vmem((half, ff), b16),
        vmem((ff, half), b16),
        vmem((half, width), b16),
        vmem((half, width), b16),
        vmem((wide, half), b16),
        vmem((wide, half), b16),
        vmem((half, width), b16),
        vmem((wide, half), b16),
        vmem((SQUARE, own, half), b16),
        vmem((SQUARE, own, half), b16),
        vmem((2, own, half), b16),
        vmem((2, own // 2, half), b16),
        vmem((2, own, half), b16),
        vmem((2, own // 2, half), b16),
        vmem((2, own, half), b16),
        vmem((2, own, half), b16),
        vmem((own, model), b16),
        vmem((own, model), b16),
        vmem((own, model), f32),
        vmem((8, model), f32),
        vmem((2, tokens, half), b16),
        vmem((model, width), b16),
        vmem((2, wide, half), b16),
        vmem((rows, span, wide), b16),
        vmem((high_size, rows, span, 2 * HD), b16),
        vmem((tokens, wide), f32),
        vmem((rows, span, wide), b16),
        vmem((high_size, rows, span, 2 * HD), f32),
        vmem((rows, span, 2 * HD), b16),
        vmem((rows, span, 2 * HD), b16),
        vmem((tokens, width), b16),
        vmem((tokens, 2 * HD), f32),
        vmem((tokens, 2 * HD), f32),
        vmem((2, 16, 8, block), f32),
        vmem((2, 16, 8, block), f32),
        vmem((tokens, wide), b16),
        vmem((8, block), f32),
        pltpu.SemaphoreType.DMA((128,)),
        pltpu.SemaphoreType.DMA((128,)),
        pltpu.SemaphoreType.DMA((64,)),
    ]
    return pl.pallas_call(
        functools.partial(back_kernel, sizes),
        out_shape=outs,
        in_specs=[pl.BlockSpec(memory_space=pltpu.SMEM)] + [anywhere] * len(arrays),
        out_specs=[anywhere] * len(outs),
        scratch_shapes=scratch,
        compiler_params=pltpu.CompilerParams(
            collective_id=1, has_side_effects=True, vmem_limit_bytes=VMEM
        ),
        name="back",
    )(lengths, *arrays)


def norm_back(values, scale, gain, grad):
    weighted = grad * gain
    gain_grad = jnp.sum(grad * values * scale, axis=0)
    inner = jnp.mean(weighted * values, axis=-1, keepdims=True)
    return (weighted * scale - values * scale**3 * inner, gain_grad)


def shards_exchanged(
    hidden_in,
    doc_lengths,
    attn_gain,
    query_weight,
    key_weight,
    value_weight,
    output_weight,
    ffn_gain,
    gate_weight,
    up_weight,
    down_weight,
    out_grad,
):
    rows, local, model = hidden_in.shape
    tokens = rows * local
    seq = lax.axis_index("seq")
    core = lax.axis_index("mp")
    low, high = seq % SQUARE, seq // SQUARE
    high_size = lax.axis_size("seq") // SQUARE
    place = (lax.axis_index("dp"), high, low, lax.axis_size("dp"), high_size)
    group = H // KVH
    span = SQUARE * local

    ends = jnp.cumsum(doc_lengths, axis=-1)
    info = jnp.concatenate([jnp.stack([low, high]), ends.reshape(-1)]).astype(jnp.int32)

    gains = lax.all_gather(jnp.stack([attn_gain, ffn_gain]), ("dp", "seq"), axis=1, tiled=True)
    gain_one, gain_two = gains[0].astype(jnp.float32), gains[1].astype(jnp.float32)

    own_in = hidden_in.reshape(tokens, model)
    all_in = gather_square(own_in, core).astype(jnp.float32)
    query_own = spread_weight(query_weight, 0, place)
    key_own = spread_weight(key_weight, 0, place)
    value_own = spread_weight(value_weight, 0, place)
    output_own = spread_weight(output_weight, 1, place)
    gate_own = spread_weight(gate_weight, 0, place)
    up_own = spread_weight(up_weight, 0, place)
    down_own = spread_weight(down_weight, 1, place)
    all_grad = gather_square(out_grad.reshape(tokens, model), core)

    blocks = low ^ jnp.arange(SQUARE, dtype=jnp.int32)
    spots = (high * span + blocks[:, None] * local + jnp.arange(local, dtype=jnp.int32)[None, :])
    reached = spots[:, None, :, None] >= ends[None, :, None, :]
    begin = jnp.max(jnp.where(reached, ends[None, :, None, :], 0), axis=-1)
    position = (spots[:, None, :] - begin).astype(jnp.float32)
    cosine, sine = rope_tables(position, HD)

    scale_one = lax.rsqrt(jnp.mean(all_in * all_in, axis=-1, keepdims=True) + EPSILON)
    normed_one = (all_in * scale_one * gain_one).astype(jnp.bfloat16)
    query_pre = dot(normed_one, query_own).reshape(SQUARE, rows, local, group, HD)
    key_pre = dot(normed_one, key_own).reshape(SQUARE, rows, local, 1, HD)
    value_pre = dot(normed_one, value_own).reshape(SQUARE, rows, local, HD)
    queries = rotate(query_pre, cosine, sine).astype(jnp.bfloat16)
    queries = queries.reshape(SQUARE, rows, local, group * HD)
    keys = rotate(key_pre, cosine, sine).astype(jnp.bfloat16).reshape(value_pre.shape)
    kv = jnp.concatenate([keys, value_pre.astype(jnp.bfloat16)], axis=-1)[None]
    for bit in bits_of(high_size):
        kv = jnp.concatenate([kv, swap(kv, "seq", SQUARE * bit)], axis=0)
    attn, lse = attend(info, queries, kv)
    attn_low = attn.reshape(SQUARE * tokens, group * HD).astype(jnp.bfloat16)
    residual = own_in.astype(jnp.float32) + scatter_square(dot(attn_low, output_own), core)

    scale_two = lax.rsqrt(jnp.mean(residual * residual, axis=-1, keepdims=True) + EPSILON)
    normed_two = (residual * scale_two * gain_two).astype(jnp.bfloat16)
    normed_two = gather_square(normed_two, core)
    gate_proj = dot(normed_two, gate_own)
    up_proj = dot(normed_two, up_own)
    sigmoid_gate = jax.nn.sigmoid(gate_proj)
    silu_gate = gate_proj * sigmoid_gate
    hidden_units = (silu_gate * up_proj).astype(jnp.bfloat16)
    hidden_grad = dot(all_grad, down_own, ((1,), (1,)))
    gate_act = (
        hidden_grad * up_proj * sigmoid_gate * (1.0 + gate_proj * (1.0 - sigmoid_gate))
    ).astype(jnp.bfloat16)
    up_act = (hidden_grad * silu_gate).astype(jnp.bfloat16)
    down_grad = settle_grad(dot(hidden_units, all_grad, ((0,), (0,))), 1, place)
    normed_two_grad = scatter_square(
        dot(gate_act, gate_own, ((1,), (1,))) + dot(up_act, up_own, ((1,), (1,))), core
    )
    layer_out = residual + scatter_square(dot(hidden_units, down_own), core)
    layer_out = layer_out.astype(jnp.bfloat16).reshape(hidden_in.shape)
    gate_grad = settle_grad(dot(normed_two, gate_act, ((0,), (0,))), 0, place)
    up_grad = settle_grad(dot(normed_two, up_act, ((0,), (0,))), 0, place)

    residual_part, ffn_gain_grad = norm_back(residual, scale_two, gain_two, normed_two_grad)
    residual_grad = out_grad.reshape(tokens, model).astype(jnp.float32) + residual_part
    residual_low = gather_square(residual_grad.astype(jnp.bfloat16), core)
    output_grad = settle_grad(dot(attn_low, residual_low, ((0,), (0,))), 1, place)
    attn_grad = dot(residual_low, output_own, ((1,), (1,))).astype(jnp.bfloat16)
    attn_grad = attn_grad.reshape(queries.shape)
    query_acc, kv_acc = attend_back(info, queries, kv, attn_grad, attn, lse)
    for bit in reversed(bits_of(high_size)):
        sent = kv_acc[bit:].astype(jnp.bfloat16)
        kv_acc = kv_acc[:bit] + swap(sent, "seq", SQUARE * bit).astype(jnp.float32)
    kv_acc = kv_acc[0]
    query_back = unrotate(query_acc.reshape(query_pre.shape), cosine, sine).astype(jnp.bfloat16)
    key_back = unrotate(kv_acc[..., :HD].reshape(key_pre.shape), cosine, sine)
    key_back = key_back.astype(jnp.bfloat16).reshape(SQUARE * tokens, HD)
    value_back = kv_acc[..., HD:].astype(jnp.bfloat16).reshape(SQUARE * tokens, HD)
    query_back = query_back.reshape(SQUARE * tokens, group * HD)
    normed_one_grad = scatter_square(
        dot(query_back, query_own, ((1,), (1,)))
        + dot(key_back, key_own, ((1,), (1,)))
        + dot(value_back, value_own, ((1,), (1,))),
        core,
    )
    query_grad = settle_grad(dot(normed_one, query_back, ((0,), (0,))), 0, place)
    key_grad = settle_grad(dot(normed_one, key_back, ((0,), (0,))), 0, place)
    value_grad = settle_grad(dot(normed_one, value_back, ((0,), (0,))), 0, place)
    own_32 = own_in.astype(jnp.float32)
    own_scale = lax.rsqrt(jnp.mean(own_32 * own_32, axis=-1, keepdims=True) + EPSILON)
    input_part, attn_gain_grad = norm_back(own_32, own_scale, gain_one, normed_one_grad)
    input_grad = (residual_grad + input_part).astype(jnp.bfloat16).reshape(hidden_in.shape)
    gain_grads = lax.psum_scatter(
        jnp.stack([attn_gain_grad, ffn_gain_grad]), ("dp", "seq"), scatter_dimension=1, tiled=True
    )
    return (
        layer_out,
        input_grad,
        gain_grads[0],
        query_grad,
        key_grad,
        value_grad,
        output_grad,
        gain_grads[1],
        gate_grad,
        up_grad,
        down_grad,
    )


def shards(
    hidden_in,
    doc_lengths,
    attn_gain,
    query_weight,
    key_weight,
    value_weight,
    output_weight,
    ffn_gain,
    gate_weight,
    up_weight,
    down_weight,
    out_grad,
):
    rows, local, model = hidden_in.shape
    tokens = rows * local
    seq = lax.axis_index("seq")
    high = seq // SQUARE
    high_size = lax.axis_size("seq") // SQUARE
    block = query_weight.shape[0]
    if block % 128 or high_size != 2 or lax.axis_size("dp") != 2:
        return shards_exchanged(
            hidden_in,
            doc_lengths,
            attn_gain,
            query_weight,
            key_weight,
            value_weight,
            output_weight,
            ffn_gain,
            gate_weight,
            up_weight,
            down_weight,
            out_grad,
        )
    group = H // KVH
    span = SQUARE * local
    width = (group + 2) * HD

    spots = high * span + jnp.arange(span, dtype=jnp.int32).reshape(SQUARE, 1, local)
    begin, end = jnp.zeros((1, rows, 1), jnp.int32), jnp.zeros((1, rows, 1), jnp.int32)
    for doc in range(doc_lengths.shape[1]):
        end = end + doc_lengths[:, doc].reshape(1, rows, 1)
        begin = jnp.where(spots >= end, end, begin)
    position = (spots - begin).astype(jnp.float32).reshape(SQUARE * tokens, 1)
    angles = position * jnp.tile(inverse_freqs(HD), 4)[None, :]
    sign = jnp.where(jnp.arange(2 * HD) % HD < HD // 2, -1.0, 1.0)[None, :]
    cos, sin = jnp.cos(angles), jnp.sin(angles) * sign
    qkv_shard = jnp.concatenate(
        [
            query_weight.reshape(block, SQUARE, group * HD),
            key_weight.reshape(block, SQUARE, HD),
            value_weight.reshape(block, SQUARE, HD),
        ],
        axis=2,
    ).reshape(block, SQUARE * width)
    gain_shard = jnp.concatenate(
        [attn_gain[None, None], ffn_gain[None, None], jnp.zeros((1, 14, block), jnp.bfloat16)],
        axis=1,
    )
    lengths = doc_lengths.reshape(-1)
    own_in = hidden_in.reshape(tokens, model)
    own_grad = out_grad.reshape(tokens, model)
    (
        qkv_own,
        output_own,
        gains,
        normed_one,
        queries,
        kv,
        attn,
        residual,
        gate_part,
        up_part,
        down_part,
        normed_two_part,
        layer_part,
    ) = front(
        (rows, local, model, high_size),
        lengths,
        own_in,
        own_grad,
        qkv_shard,
        gain_shard,
        output_weight,
        gate_weight,
        up_weight,
        down_weight,
        cos,
        sin,
    )
    (
        layer_out,
        input_grad,
        *landed,
        gain_grads,
    ) = back(
        (rows, local, model, high_size),
        lengths,
        own_in,
        own_grad,
        residual,
        gains,
        normed_two_part,
        layer_part,
        gate_part,
        up_part,
        down_part,
        qkv_own,
        output_own,
        normed_one,
        queries,
        kv,
        attn,
        cos,
        sin,
    )
    qkv_grad, output_grad, gate_grad, up_grad, down_grad = (
        part[0].astype(jnp.float32) + part[1].astype(jnp.float32) for part in landed
    )
    query_grad = qkv_grad[..., : group * HD].transpose(1, 0, 2).reshape(block, -1)
    key_grad = qkv_grad[..., group * HD : (group + 1) * HD].transpose(1, 0, 2).reshape(block, -1)
    value_grad = qkv_grad[..., (group + 1) * HD :].transpose(1, 0, 2).reshape(block, -1)
    return (
        layer_out.reshape(hidden_in.shape),
        input_grad.reshape(hidden_in.shape),
        gain_grads[0],
        query_grad,
        key_grad,
        value_grad,
        output_grad,
        gain_grads[1],
        gate_grad,
        up_grad,
        down_grad,
    )


def solution(mesh):
    return jax.shard_map(
        shards,
        mesh=mesh,
        in_specs=(
            P("dp", "seq", None),
            P("dp", None),
            P(("dp", "seq")),
            P(("dp", "seq"), "mp"),
            P(("dp", "seq"), "mp"),
            P(("dp", "seq"), "mp"),
            P("mp", ("dp", "seq")),
            P(("dp", "seq")),
            P(("dp", "seq"), "mp"),
            P(("dp", "seq"), "mp"),
            P("mp", ("dp", "seq")),
            P("dp", "seq", None),
        ),
        out_specs=(
            P("dp", "seq", None),
            P("dp", "seq", None),
            P(("dp", "seq")),
            P(("dp", "seq"), "mp"),
            P(("dp", "seq"), "mp"),
            P(("dp", "seq"), "mp"),
            P("mp", ("dp", "seq")),
            P(("dp", "seq")),
            P(("dp", "seq"), "mp"),
            P(("dp", "seq"), "mp"),
            P("mp", ("dp", "seq")),
        ),
        check_vma=False,
    )
```

```python
import functools
import math

import jax
import jax.numpy as jnp
from jax import lax
from jax.experimental import pallas as pl
from jax.experimental.pallas import tpu as pltpu
from jax.sharding import PartitionSpec as P

H = 32
KVH = 8
HD = 64
SQUARE = 4

EPSILON = 1e-05
MASKED = -1e30
ROPE_THETA = 500000.0
ROPE_FACTOR = 32.0
LOW_FACTOR = 1.0
HIGH_FACTOR = 4.0
PRIOR_CONTEXT = 8192.0
VMEM = 62 * 1024 * 1024


def inverse_freqs(head_dim):
    ladder = jnp.arange(head_dim // 2, dtype=jnp.float32)
    base = ROPE_THETA ** (-2.0 * ladder / head_dim)
    wavelen = 2.0 * math.pi / base
    smooth = (PRIOR_CONTEXT / wavelen - LOW_FACTOR) / (HIGH_FACTOR - LOW_FACTOR)
    blended = (1.0 - smooth) * base / ROPE_FACTOR + smooth * base
    low_limit = PRIOR_CONTEXT / LOW_FACTOR
    high_limit = PRIOR_CONTEXT / HIGH_FACTOR
    return jnp.where(
        wavelen < high_limit, base, jnp.where(wavelen > low_limit, base / ROPE_FACTOR, blended)
    )


def rope_tables(position, head_dim):
    angles = position[..., None] * inverse_freqs(head_dim)
    angles = jnp.concatenate([angles, angles], axis=-1)
    return (jnp.cos(angles)[..., None, :], jnp.sin(angles)[..., None, :])


def rotate(values, cosine, sine):
    middle = values.shape[-1] // 2
    turned = jnp.concatenate([-values[..., middle:], values[..., :middle]], axis=-1)
    return values * cosine + turned * sine


def unrotate(grads, cosine, sine):
    middle = grads.shape[-1] // 2
    scaled = grads * sine
    turned = jnp.concatenate([scaled[..., middle:], -scaled[..., :middle]], axis=-1)
    return grads * cosine + turned


def dot(left, right, dims=((1,), (0,))):
    return lax.dot_general(left, right, (dims, ((), ())), preferred_element_type=jnp.float32)


def swap(value, axis, mask):
    size = lax.axis_size(axis)
    return lax.ppermute(value, axis, [(i, i ^ mask) for i in range(size)])


def cut(value, start, length, axis):
    return lax.dynamic_slice_in_dim(value, start, length, axis)


def put(whole, part, start, axis):
    return lax.dynamic_update_slice_in_dim(whole, part, start, axis)


def mask_of(info, row, row_count, local, keys):
    span = SQUARE * local
    low, high = info[0], info[1]

    def place_of(index):
        block = (index // local) % SQUARE
        part = index // span
        return (high ^ part) * span + (low ^ block) * local + index % local

    def segment_of(place):
        total = jnp.zeros_like(place)
        for doc in range(4):
            total = total + (place >= info[2 + row * 4 + doc]).astype(jnp.int32)
        return total

    query = place_of(lax.broadcasted_iota(jnp.int32, (span, 1), 0))
    key = place_of(lax.broadcasted_iota(jnp.int32, (1, keys), 1))
    return (segment_of(query) == segment_of(key)) & (query >= key)


def attend_kernel(local, keys, group, info, q_ref, kv_ref, out_ref, lse_ref):
    row = pl.program_id(0)
    span = SQUARE * local
    allowed = mask_of(info, row, None, local, keys)
    kv = kv_ref[...].reshape(keys, 2 * HD)
    k, v = kv[:, :HD], kv[:, HD:]
    q_all = q_ref[...].reshape(span, group * HD)
    outs, sums = [], []
    for head in range(group):
        q = q_all[:, head * HD : (head + 1) * HD]
        score = dot(q, k, ((1,), (1,))) * HD ** (-0.5)
        score = jnp.where(allowed, score, MASKED)
        top = jnp.max(score, axis=1, keepdims=True)
        grown = jnp.exp(score - top)
        total = jnp.sum(grown, axis=1, keepdims=True)
        lse = top + jnp.log(total)
        probs = (grown * (1.0 / total)).astype(jnp.bfloat16)
        outs.append(dot(probs, v))
        sums.append(lse)
    out_ref[...] = jnp.concatenate(outs, axis=1).reshape(out_ref.shape)
    lse_ref[...] = jnp.concatenate(sums, axis=1).reshape(lse_ref.shape)


def attend(info, queries, kv):
    blocks, rows, local, width = queries.shape
    parts = kv.shape[0]
    keys = parts * blocks * local
    group = width // HD
    return pl.pallas_call(
        functools.partial(attend_kernel, local, keys, group),
        grid=(rows,),
        out_shape=(
            jax.ShapeDtypeStruct((blocks, rows, local, width), jnp.float32),
            jax.ShapeDtypeStruct((blocks, rows, local, group), jnp.float32),
        ),
        in_specs=[
            pl.BlockSpec(memory_space=pltpu.SMEM),
            pl.BlockSpec((blocks, 1, local, width), lambda r: (0, r, 0, 0)),
            pl.BlockSpec((parts, blocks, 1, local, 2 * HD), lambda r: (0, 0, r, 0, 0)),
        ],
        out_specs=(
            pl.BlockSpec((blocks, 1, local, width), lambda r: (0, r, 0, 0)),
            pl.BlockSpec((blocks, 1, local, group), lambda r: (0, r, 0, 0)),
        ),
        compiler_params=pltpu.CompilerParams(vmem_limit_bytes=VMEM),
        cost_estimate=pl.CostEstimate(
            flops=8 * rows * blocks * local * keys * width,
            bytes_accessed=rows * blocks * local * width * 8,
            transcendentals=rows * blocks * local * keys * group,
        ),
        name="attend",
    )(info, queries, kv)


def attend_back_kernel(
    local, keys, group, info, q_ref, kv_ref, go_ref, out_ref, lse_ref, dq_ref, dkv_ref
):
    row = pl.program_id(0)
    span = SQUARE * local
    allowed = mask_of(info, row, None, local, keys)
    kv = kv_ref[...].reshape(keys, 2 * HD)
    k, v = kv[:, :HD], kv[:, HD:]
    q_all = q_ref[...].reshape(span, group * HD)
    go_all = go_ref[...].reshape(span, group * HD)
    out_all = out_ref[...].reshape(span, group * HD)
    lse_all = lse_ref[...].reshape(span, group)
    dq = []
    dk = jnp.zeros((keys, HD), jnp.float32)
    dv = jnp.zeros((keys, HD), jnp.float32)
    scale = HD ** (-0.5)
    for head in range(group):
        q = q_all[:, head * HD : (head + 1) * HD]
        go = go_all[:, head * HD : (head + 1) * HD]
        out = out_all[:, head * HD : (head + 1) * HD]
        delta = jnp.sum(go.astype(jnp.float32) * out, axis=1, keepdims=True)
        score = dot(q, k, ((1,), (1,))) * scale
        probs = jnp.exp(jnp.where(allowed, score, MASKED) - lse_all[:, head : head + 1])
        dv = dv + dot(probs.astype(jnp.bfloat16), go, ((0,), (0,)))
        prob_grad = dot(go, v, ((1,), (1,)))
        score_grad = (probs * (prob_grad - delta)).astype(jnp.bfloat16)
        dq.append(dot(score_grad, k) * scale)
        dk = dk + dot(score_grad, q, ((0,), (0,)))
    dq_ref[...] = jnp.concatenate(dq, axis=1).reshape(dq_ref.shape)
    dkv_ref[...] = jnp.concatenate([dk * scale, dv], axis=1).reshape(dkv_ref.shape)


def attend_back(info, queries, kv, out_grads, out, lse):
    blocks, rows, local, width = queries.shape
    parts = kv.shape[0]
    keys = parts * blocks * local
    group = width // HD
    wide = pl.BlockSpec((blocks, 1, local, width), lambda r: (0, r, 0, 0))
    kv_spec = pl.BlockSpec((parts, blocks, 1, local, 2 * HD), lambda r: (0, 0, r, 0, 0))
    return pl.pallas_call(
        functools.partial(attend_back_kernel, local, keys, group),
        grid=(rows,),
        out_shape=(
            jax.ShapeDtypeStruct(queries.shape, jnp.float32),
            jax.ShapeDtypeStruct(kv.shape, jnp.float32),
        ),
        in_specs=[
            pl.BlockSpec(memory_space=pltpu.SMEM),
            wide,
            kv_spec,
            wide,
            wide,
            pl.BlockSpec((blocks, 1, local, group), lambda r: (0, r, 0, 0)),
        ],
        out_specs=(wide, kv_spec),
        compiler_params=pltpu.CompilerParams(vmem_limit_bytes=VMEM),
        cost_estimate=pl.CostEstimate(
            flops=20 * rows * blocks * local * keys * width,
            bytes_accessed=rows * blocks * local * width * 16,
            transcendentals=rows * blocks * local * keys * group,
        ),
        name="attend_back",
    )(info, queries, kv, out_grads, out, lse)


def bits_of(size):
    return [1 << b for b in range(size.bit_length() - 1)]


def spread_weight(shard, axis, place):
    dp, high, low, dp_size, high_size = place
    other = 1 - axis
    block = shard.shape[axis]
    width = shard.shape[other] // SQUARE
    pieces = [cut(shard, low * width, width, other)]
    for mask in range(1, SQUARE):
        pieces.append(swap(cut(shard, (low ^ mask) * width, width, other), "seq", mask))
    shape = [0, 0]
    shape[axis], shape[other] = SQUARE * block, width
    square = jnp.zeros(shape, shard.dtype)
    for mask in range(SQUARE):
        square = put(square, pieces[mask], (low ^ mask) * block, axis)
    parts = {(0, 0): square}
    for bit in bits_of(high_size):
        for (a, b) in list(parts):
            parts[a, b ^ bit] = swap(parts[a, b], "seq", SQUARE * bit)
    for bit in bits_of(dp_size):
        for (a, b) in list(parts):
            parts[a ^ bit, b] = swap(parts[a, b], "dp", bit)
    shape[axis] = SQUARE * block * high_size * dp_size
    whole = jnp.zeros(shape, shard.dtype)
    for (a, b), part in parts.items():
        index = (dp ^ a) * high_size + (high ^ b)
        whole = put(whole, part, index * SQUARE * block, axis)
    return whole


def settle_grad(grad, axis, place):
    dp, high, low, dp_size, high_size = place
    other = 1 - axis
    width = grad.shape[other]
    kept = grad
    for index, size, name, unit in ((dp, dp_size, "dp", 1), (high, high_size, "seq", SQUARE)):
        for bit in reversed(bits_of(size)):
            half = kept.shape[axis] // 2
            mine = (index // bit) % 2
            sent = cut(kept, (1 - mine) * half, half, axis).astype(jnp.bfloat16)
            kept = cut(kept, mine * half, half, axis) + swap(sent, name, unit * bit).astype(
                jnp.float32
            )
    block = kept.shape[axis] // SQUARE
    shape = [0, 0]
    shape[axis], shape[other] = block, SQUARE * width
    whole = jnp.zeros(shape, jnp.float32)
    whole = put(whole, cut(kept, low * block, block, axis), low * width, other)
    for mask in range(1, SQUARE):
        sent = cut(kept, (low ^ mask) * block, block, axis).astype(jnp.bfloat16)
        got = swap(sent, "seq", mask).astype(jnp.float32)
        whole = put(whole, got, (low ^ mask) * width, other)
    return whole


def gather_square(own, core):
    tokens, width = own.shape
    half = width // 2
    mine = cut(own, core * half, half, 1)
    got = jnp.concatenate([swap(mine, "seq", mask) for mask in range(1, SQUARE)], axis=0)
    across = swap(got, "mp", 1)
    first = jnp.where(core == 0, got, across)
    second = jnp.where(core == 0, across, got)
    return jnp.concatenate([own, jnp.concatenate([first, second], axis=1)], axis=0)


def scatter_square(partial, core):
    tokens, width = partial.shape[0] // SQUARE, partial.shape[1]
    half = width // 2
    kept = cut(partial, core * half, half, 1)
    sent = cut(partial, (1 - core) * half, half, 1).astype(jnp.bfloat16)
    kept = kept + swap(sent, "mp", 1).astype(jnp.float32)
    total = kept[:tokens]
    for mask in range(1, SQUARE):
        part = kept[mask * tokens : (mask + 1) * tokens].astype(jnp.bfloat16)
        total = total + swap(part, "seq", mask).astype(jnp.float32)
    mine = total.astype(jnp.bfloat16)
    across = swap(mine, "mp", 1)
    return jnp.concatenate(
        [jnp.where(core == 0, mine, across), jnp.where(core == 0, across, mine)], axis=1
    ).astype(jnp.float32)


MESH = pl.DeviceIdType.MESH


class Links:
    def __init__(self, send_sem, recv_sem, local_sem, high_size):
        self.send_sem, self.recv_sem, self.local_sem = send_sem, recv_sem, local_sem
        self.x, self.seq, self.core = (lax.axis_index(a) for a in ("dp", "seq", "mp"))
        self.high_size = high_size
        self.low, self.high = self.seq % SQUARE, self.seq // SQUARE
        self.count = self.local_count = 0
        self.sent = []

    def beside(self, flip):
        if flip == 1:
            return self.low + 1 - 2 * (self.low % 2)
        return (self.low + 2) % SQUARE if flip == 2 else SQUARE - 1 - self.low

    def to(self, dx=0, dh=0, dl=0, dc=0, flip=0):
        low = self.beside(flip) if flip else (self.low + dl) % SQUARE
        seq = ((self.high + dh) % self.high_size) * SQUARE + low
        return ((self.x + dx) % 2, seq, (self.core + dc) % 2)

    def copy(self, src, dst, **step):
        k = self.count
        self.count += 1
        made = pltpu.make_async_remote_copy(
            src_ref=src,
            dst_ref=dst,
            send_sem=self.send_sem.at[k],
            recv_sem=self.recv_sem.at[k],
            device_id=self.to(**step),
            device_id_type=MESH,
        )
        made.start()
        self.sent.append(made)
        return made

    def local(self, src, dst):
        k = self.local_count
        self.local_count += 1
        made = pltpu.make_async_copy(src, dst, self.local_sem.at[k])
        made.start()
        return made

    def greet(self, steps):
        barrier = pltpu.get_barrier_semaphore()
        for step in steps:
            pl.semaphore_signal(barrier, inc=1, device_id=self.to(**step), device_id_type=MESH)
        pl.semaphore_wait(barrier, len(steps))

    def left(self, copies):
        for made in copies:
            made.wait_send()
            self.sent = [one for one in self.sent if one is not made]

    def finish(self):
        for made in self.sent:
            made.wait_send()


def arrived(copies):
    for made in copies:
        made.wait_recv()


class Weight:
    def __init__(self, links, slice_of, spot):
        self.links, self.spot = links, spot
        l = links
        self.own = l.local(slice_of(l.low), spot(l.x, l.high, l.low, 1))
        self.near, self.far = [], []
        for dh in range(2):
            for dl in range(SQUARE):
                if dh or dl:
                    made = l.copy(
                        slice_of((l.low + dl) % SQUARE),
                        spot(l.x, l.high, l.low, 1),
                        dh=dh,
                        dl=dl,
                    )
                    (self.far if dh else self.near).append(made)

    def pass_near(self):
        self.own.wait()
        arrived(self.near)
        l = self.links
        part = self.spot(l.x, l.high, 0, SQUARE)
        self.across = [l.copy(part, part, dx=1)]

    def pass_far(self):
        arrived(self.far)
        l = self.links
        part = self.spot(l.x, 1 - l.high, 0, SQUARE)
        self.across.append(l.copy(part, part, dx=1))

    def wait(self):
        arrived(self.across)


def gather_push(l, everyone, source):
    return [
        l.copy(source(part), everyone(l.core, l.low, part), flip=flip)
        for flip, part in ((1, 0), (2, 1), (1, 1), (2, 0))
    ]


def gather_across(l, everyone, pushed):
    handed, corner = [], []
    for k, (flip, part) in enumerate(((1, 0), (2, 1), (1, 1), (2, 0))):
        pushed[k].wait_recv()
        block = everyone(l.core, l.beside(flip), part)
        if k < 2:
            corner.append(l.copy(block, block, flip=3 - flip))
        handed.append(l.copy(block, block, dc=1))
    for part in range(2):
        corner[part].wait_recv()
        block = everyone(l.core, l.beside(3), part)
        handed.append(l.copy(block, block, dc=1))
    return handed, corner


def square_push(l, total_of, send, relay, landed, split=False):
    lines = send.shape[1]
    first, second = pl.ds(0, lines // 2), pl.ds(lines // 2, lines // 2)
    one, two, corner = (l.beside(flip) for flip in (1, 2, 3))
    send[corner] = total_of(corner).astype(jnp.bfloat16)
    made = [
        l.copy(send.at[corner, first], relay.at[0], flip=1),
        l.copy(send.at[corner, second], relay.at[1], flip=2),
    ]
    send[one] = total_of(one).astype(jnp.bfloat16)
    made.append(l.copy(send.at[one, first], landed.at[0, first], flip=1))
    send[two] = total_of(two).astype(jnp.bfloat16)
    made.append(l.copy(send.at[two, second], landed.at[1, second], flip=2))
    if not split:
        square_relay(l, made, send, relay, landed)
    return made


def square_relay(l, made, send, relay, landed):
    lines = send.shape[1]
    first, second = pl.ds(0, lines // 2), pl.ds(lines // 2, lines // 2)
    one, two = l.beside(1), l.beside(2)
    made[0].wait_recv()
    value = send[two, first].astype(jnp.float32) + relay[0].astype(jnp.float32)
    send[two, first] = value.astype(jnp.bfloat16)
    made.append(l.copy(send.at[two, first], landed.at[1, first], flip=2))
    made[1].wait_recv()
    value = send[one, second].astype(jnp.float32) + relay[1].astype(jnp.float32)
    send[one, second] = value.astype(jnp.bfloat16)
    made.append(l.copy(send.at[one, second], landed.at[0, second], flip=1))


def square_settle(l, total_of, made, landed, both):
    total = total_of(l.low)
    arrived(made[2:])
    total = total + landed[0].astype(jnp.float32) + landed[1].astype(jnp.float32)
    both[l.core] = total.astype(jnp.bfloat16)
    return l.copy(both.at[l.core], both.at[l.core], dc=1)


def roll_heads(value):
    width = value.shape[1]
    lane = lax.broadcasted_iota(jnp.int32, value.shape, 1)
    left = pltpu.roll(value, width - HD // 2, 1)
    right = pltpu.roll(value, HD // 2, 1)
    return jnp.where(lane % HD < HD // 2, left, right)


def rope_rows(cos, sin, at, copies):
    return (
        jnp.concatenate([cos[at]] * copies, axis=1),
        jnp.concatenate([sin[at]] * copies, axis=1),
    )


def rope_key_rows(cos, sin, at):
    lane = lax.broadcasted_iota(jnp.int32, (1, 2 * HD), 1)
    return (jnp.where(lane < HD, cos[at], 1.0), jnp.where(lane < HD, sin[at], 0.0))


def allowed_keys(l, lengths, row, span, keys):
    def segment_of(place):
        total = jnp.zeros_like(place)
        end = lengths[row, 0]
        for doc in range(4):
            if doc:
                end = end + lengths[row, doc]
            total = total + (place >= end).astype(jnp.int32)
        return total

    query = l.high * span + lax.broadcasted_iota(jnp.int32, (span, 1), 0)
    key = lax.broadcasted_iota(jnp.int32, (1, keys), 1)
    return (segment_of(query) == segment_of(key)) & (query >= key)


def front_kernel(
    sizes,
    lengths,
    x_in,
    g_in,
    qkv_in,
    gain_in,
    wo_in,
    wg_in,
    wu_in,
    wd_in,
    cos_in,
    sin_in,
    qkv_out,
    wo_out,
    gain_out,
    normed_one_out,
    q_out,
    kv_out,
    attn_out,
    residual_out,
    dwg_out,
    dwu_out,
    dwd_out,
    normed_two_part,
    layer_part,
    x_all,
    normed,
    wqkv,
    wo,
    gains,
    gain_rows,
    cos,
    sin,
    q,
    kv,
    attn,
    low_attn,
    send_core,
    recv_core,
    send_block,
    recv_block,
    relay,
    both,
    residual,
    normed_two,
    g_all,
    wg,
    wu,
    wd,
    hidden,
    gate_act,
    up_act,
    send_sem,
    recv_sem,
    local_sem,
):
    rows, local, model, high_size = sizes
    own = rows * local
    tokens = SQUARE * own
    half = model // 2
    block = qkv_in.shape[0]
    heads = q.shape[2] // HD
    span = SQUARE * local
    keys = high_size * span
    l = Links(send_sem, recv_sem, local_sem, high_size)
    near = [dict(dl=dl) for dl in range(1, SQUARE)]
    far = [dict(dh=1, dl=dl) for dl in range(SQUARE)]
    l.greet(near + far + [dict(dx=1), dict(dc=1)])

    def row_spot(ref):
        def spot(x, h, low, n):
            start = ((x * high_size + h) * SQUARE + low) * block
            return ref.at[pl.ds(pl.multiple_of(start, block), n * block)]

        return spot

    def block_spot(ref):
        return lambda x, h, low, n: ref.at[pl.ds((x * high_size + h) * SQUARE + low, n)]

    def half_spot(ref):
        def spot(x, h, low, n):
            start = pl.multiple_of((h * SQUARE + low) * block, block)
            return ref.at[x, :, pl.ds(start, n * block)]

        return spot

    def row_half_spot(ref):
        def spot(x, h, low, n):
            start = pl.multiple_of((h * SQUARE + low) * block, block)
            return ref.at[x, pl.ds(start, n * block)]

        return spot

    def columns(ref, width):
        return lambda j: ref.at[:, pl.ds(pl.multiple_of(j * width, width), width)]

    def lines(ref, width):
        return lambda j: ref.at[pl.ds(pl.multiple_of(j * width, width), width)]

    def part_at(low, part):
        if part is None:
            return pl.ds(pl.multiple_of(low * own, own), own)
        return pl.ds(pl.multiple_of(low * own + part * (own // 2), own // 2), own // 2)

    def x_spot(side, low, part=None):
        return x_all.at[side, part_at(low, part)]

    def g_spot(side, low, part=None):
        return g_all.at[side, part_at(low, part)]

    def normed_two_spot(side, low, part=None):
        return normed_two.at[side, part_at(low, part)]

    def own_part_of(ref):
        return lambda part: ref.at[
            pl.ds(part * (own // 2), own // 2), pl.ds(pl.multiple_of(l.core * half, half), half)
        ]

    def side_of(ref, side):
        return ref.at[:, pl.ds(pl.multiple_of(side * half, half), half)]

    loads = [l.local(side_of(x_in, side), x_spot(side, l.low)) for side in range(2)]
    loads += [l.local(cos_in, cos), l.local(sin_in, sin)]
    w_gain = Weight(l, lambda j: gain_in.at[pl.ds(0, 1)], block_spot(gains))
    w_qkv = Weight(l, columns(qkv_in, wqkv.shape[1]), row_spot(wqkv))
    x_pushed = gather_push(l, x_spot, own_part_of(x_in))
    w_o = Weight(l, lines(wo_in, wo.shape[1]), half_spot(wo))
    w_gate = Weight(l, columns(wg_in, wg.shape[2]), row_half_spot(wg))

    w_gain.pass_near()
    w_qkv.pass_near()
    x_handed, _ = gather_across(l, x_spot, x_pushed)
    w_gain.pass_far()
    w_qkv.pass_far()
    w_o.pass_near()
    w_o.pass_far()
    for made in loads:
        made.wait()
    w_gain.wait()
    for b in range(gains.shape[0]):
        tile = gains[b].astype(jnp.float32)
        gain_rows[0:1, b * block : (b + 1) * block] = tile[0:1]
        gain_rows[1:2, b * block : (b + 1) * block] = tile[1:2]
    arrived(x_handed)

    step = 128

    def norm_step(i, carry):
        at = pl.ds(pl.multiple_of(i * step, step), step)
        first, second = x_all[0, at].astype(jnp.float32), x_all[1, at].astype(jnp.float32)
        total = jnp.sum(first * first, axis=1, keepdims=True)
        total = total + jnp.sum(second * second, axis=1, keepdims=True)
        scale = lax.rsqrt(total / model + EPSILON)
        normed[0, at] = (first * scale * gain_rows[0:1, :half]).astype(jnp.bfloat16)
        normed[1, at] = (second * scale * gain_rows[0:1, half:]).astype(jnp.bfloat16)
        return carry

    lax.fori_loop(0, tokens // step, norm_step, 0)
    normed_store = l.local(normed, normed_one_out)
    stores = []
    w_qkv.wait()
    stores += [l.local(wqkv, qkv_out), l.local(gain_rows, gain_out)]

    def project_step(i, carry):
        at = pl.ds(pl.multiple_of(i * local, local), local)
        pre = dot(normed[0, at], wqkv[:half]) + dot(normed[1, at], wqkv[half:])
        cos_q, sin_q = rope_rows(cos, sin, at, heads // 2)
        cos_k, sin_k = rope_key_rows(cos, sin, at)
        cos_all = jnp.concatenate([cos_q, cos_k], axis=1)
        sin_all = jnp.concatenate([sin_q, sin_k], axis=1)
        turned = pre * cos_all + roll_heads(pre) * sin_all
        spot = pl.ds(pl.multiple_of((i // rows) * local, local), local)
        q[i % rows, spot] = (turned[:, : heads * HD].astype(jnp.bfloat16) * HD ** (-0.5)).astype(
            jnp.bfloat16
        )
        kv[l.high, i % rows, spot] = turned[:, heads * HD :].astype(jnp.bfloat16)
        return carry

    lax.fori_loop(0, SQUARE * rows, project_step, 0)
    kv_copy = l.copy(kv.at[l.high], kv.at[l.high], dh=1)
    stores.append(l.local(q, q_out))
    w_gate.pass_near()
    w_up = Weight(l, columns(wu_in, wu.shape[2]), row_half_spot(wu))
    kv_copy.wait_recv()
    stores.append(l.local(kv, kv_out))

    def attend_row(r, carry):
        allowed = allowed_keys(l, lengths, r, span, keys)
        kv_row = kv[:, r].reshape(keys, 2 * HD)
        k, v = kv_row[:, :HD], kv_row[:, HD:]
        q_row = q[r]
        outs = []
        for head in range(heads):
            score = dot(q_row[:, head * HD : (head + 1) * HD], k, ((1,), (1,)))
            score = jnp.where(allowed, score, MASKED)
            top = jnp.max(score, axis=1, keepdims=True)
            grown = jnp.exp(score - top)
            total = jnp.sum(grown, axis=1, keepdims=True)
            probs = (grown * (1.0 / total)).astype(jnp.bfloat16)
            outs.append(dot(probs, v))
        out = jnp.concatenate(outs, axis=1)
        for j in range(SQUARE):
            at = pl.ds(pl.multiple_of(j * own + r * local, local), local)
            part = out[j * local : (j + 1) * local]
            attn[at] = part
            low_attn[at] = part.astype(jnp.bfloat16)
        return carry

    lax.fori_loop(0, rows, attend_row, 0)
    stores.append(l.local(attn, attn_out))
    w_gate.pass_far()
    w_o.wait()
    stores.append(l.local(wo, wo_out))

    def project_out(j, side):
        at = pl.ds(pl.multiple_of(j * own, own), own)
        return dot(low_attn[at], wo[side])

    handed = []
    for j in range(SQUARE):
        send_core[j] = project_out(j, 1 - l.core).astype(jnp.bfloat16)
        handed.append(l.copy(send_core.at[j], recv_core.at[j], dc=1))
    arrived(handed)

    def total_out(j):
        return project_out(j, l.core) + recv_core[j].astype(jnp.float32)

    pushed = square_push(l, total_out, send_block, relay, recv_block)
    w_up.pass_near()
    square_settle(l, total_out, pushed, recv_block, both).wait_recv()
    at_own = pl.ds(pl.multiple_of(l.low * own, own), own)
    total = jnp.zeros((own, 1), jnp.float32)
    for side in range(2):
        value = x_all[side, at_own].astype(jnp.float32) + both[side].astype(jnp.float32)
        residual[:, side * half : (side + 1) * half] = value
        total = total + jnp.sum(value * value, axis=1, keepdims=True)
    scale = lax.rsqrt(total / model + EPSILON)
    for side in range(2):
        at = slice(side * half, (side + 1) * half)
        normed_two[side, at_own] = (residual[:, at] * scale * gain_rows[1:2, at]).astype(
            jnp.bfloat16
        )
    stores.append(l.local(residual, residual_out))
    pushed = gather_push(
        l, normed_two_spot, lambda part: normed_two_spot(l.core, l.low, part)
    )
    w_up.pass_far()
    w_down = Weight(l, lines(wd_in, wd.shape[1]), half_spot(wd))
    handed, _ = gather_across(l, normed_two_spot, pushed)
    loads = [l.local(side_of(g_in, side), g_spot(side, l.low)) for side in range(2)]
    g_pushed = gather_push(l, g_spot, own_part_of(g_in))
    w_down.pass_near()
    arrived(handed)
    normed_store.wait()
    w_gate.wait()
    w_up.wait()

    def unit_step(j, carry):
        at = part_at(j, None)
        first, second = normed_two[0, at], normed_two[1, at]
        gate = dot(first, wg[0]) + dot(second, wg[1])
        up = dot(first, wu[0]) + dot(second, wu[1])
        sigmoid = jax.nn.sigmoid(gate)
        silu = gate * sigmoid
        hidden[at] = (silu * up).astype(jnp.bfloat16)
        gate_act[at] = (up * sigmoid * (1.0 + gate * (1.0 - sigmoid))).astype(jnp.bfloat16)
        up_act[at] = silu.astype(jnp.bfloat16)
        return carry

    lax.fori_loop(0, SQUARE, unit_step, 0)
    g_handed, _ = gather_across(l, g_spot, g_pushed)
    w_down.pass_far()
    for made in loads:
        made.wait()
    arrived(g_handed)
    busy = [(0, None), (1, None)]

    def fill(product, out):
        k, made = busy.pop(0)
        if made is not None:
            made.wait()
        buffer = normed.at[k]

        def step(i, carry):
            at = pl.ds(pl.multiple_of(i * own, own), own)
            buffer[at] = product(at).astype(jnp.bfloat16)
            return carry

        lax.fori_loop(0, half // own, step, 0)
        busy.append((k, l.local(buffer, out)))

    for side in range(2):
        fill(
            lambda at, side=side: dot(hidden[:, at], g_all[side], ((0,), (0,))),
            dwd_out.at[side],
        )
    w_down.wait()

    def act_step(j, carry):
        at = part_at(j, None)
        grad = dot(g_all[0, at], wd[0], ((1,), (1,))) + dot(g_all[1, at], wd[1], ((1,), (1,)))
        gate_act[at] = (grad * gate_act[at].astype(jnp.float32)).astype(jnp.bfloat16)
        up_act[at] = (grad * up_act[at].astype(jnp.float32)).astype(jnp.bfloat16)
        return carry

    lax.fori_loop(0, SQUARE, act_step, 0)
    for side in range(2):
        fill(
            lambda at, side=side: dot(gate_act[at], wg[side], ((1,), (1,)))
            + dot(up_act[at], wu[side], ((1,), (1,))),
            normed_two_part.at[side],
        )
    for side in range(2):
        fill(lambda at, side=side: dot(hidden[at], wd[side]), layer_part.at[side])
    for act, out in ((gate_act, dwg_out), (up_act, dwu_out)):
        for side in range(2):
            fill(
                lambda at, side=side, act=act: dot(
                    normed_two[side, :, at], act[...], ((0,), (0,))
                ),
                out.at[side],
            )
    for _, made in busy:
        made.wait()
    for made in stores:
        made.wait()
    l.finish()


def front(sizes, lengths, x, g, qkv, gain, wo, wg, wu, wd, cos, sin):
    rows, local, model, high_size = sizes
    own = rows * local
    tokens = SQUARE * own
    half = model // 2
    heads = wo.shape[0] // SQUARE // HD
    width = qkv.shape[1] // SQUARE
    ff = wg.shape[1] // SQUARE
    blocks = model // qkv.shape[0]
    span = SQUARE * local
    low, f32 = jnp.bfloat16, jnp.float32
    shape = jax.ShapeDtypeStruct
    outs = (
        shape((model, width), low),
        shape((2, heads * HD, half), low),
        shape((8, model), f32),
        shape((2, tokens, half), low),
        shape((rows, span, heads * HD), low),
        shape((high_size, rows, span, 2 * HD), low),
        shape((tokens, heads * HD), f32),
        shape((own, model), f32),
        shape((2, half, ff), low),
        shape((2, half, ff), low),
        shape((2, ff, half), low),
        shape((2, tokens, half), low),
        shape((2, tokens, half), low),
    )
    anywhere = pl.BlockSpec(memory_space=pl.ANY)
    vmem = pltpu.VMEM
    return pl.pallas_call(
        functools.partial(front_kernel, sizes),
        out_shape=outs,
        in_specs=[pl.BlockSpec(memory_space=pltpu.SMEM)] + [anywhere] * 10,
        out_specs=[anywhere] * len(outs),
        scratch_shapes=[
            vmem((2, tokens, half), low),
            vmem((2, tokens, half), low),
            vmem((model, width), low),
            vmem((2, heads * HD, half), low),
            vmem((blocks,) + gain.shape[1:], low),
            vmem((8, model), f32),
            vmem((tokens, 2 * HD), f32),
            vmem((tokens, 2 * HD), f32),
            vmem((rows, span, heads * HD), low),
            vmem((high_size, rows, span, 2 * HD), low),
            vmem((tokens, heads * HD), f32),
            vmem((tokens, heads * HD), low),
            vmem((SQUARE, own, half), low),
            vmem((SQUARE, own, half), low),
            vmem((SQUARE, own, half), low),
            vmem((2, own, half), low),
            vmem((2, own // 2, half), low),
            vmem((2, own, half), low),
            vmem((own, model), f32),
            vmem((2, tokens, half), low),
            vmem((2, tokens, half), low),
            vmem((2, half, ff), low),
            vmem((2, half, ff), low),
            vmem((2, ff, half), low),
            vmem((tokens, ff), low),
            vmem((tokens, ff), low),
            vmem((tokens, ff), low),
            pltpu.SemaphoreType.DMA((128,)),
            pltpu.SemaphoreType.DMA((128,)),
            pltpu.SemaphoreType.DMA((32,)),
        ],
        compiler_params=pltpu.CompilerParams(
            collective_id=0, has_side_effects=True, vmem_limit_bytes=VMEM
        ),
        name="front",
    )(lengths, x, g, qkv, gain, wo, wg, wu, wd, cos, sin)


class Grad:
    def __init__(self, links, half_of, kept, crossed, block_of, landed):
        self.links, self.kept, self.crossed = links, kept, crossed
        self.block_of, self.landed = block_of, landed
        l = links
        self.own = l.local(half_of(l.x), kept) if half_of else None
        if half_of:
            self.cross = l.copy(half_of(1 - l.x), crossed, dx=1)

    def deal(self):
        l = self.links
        if self.own is not None:
            self.own.wait()
        self.cross.wait_recv()
        kept, crossed = self.kept, self.crossed
        lines = kept.shape[0]
        step = min(128, lines)

        def add(i, carry):
            at = pl.ds(pl.multiple_of(i * step, step), step)
            kept[at] = (kept[at].astype(jnp.float32) + crossed[at].astype(jnp.float32)).astype(
                jnp.bfloat16
            )
            return carry

        lax.fori_loop(0, lines // step, add, 0)
        self.dealt = []
        for dh in range(2):
            for dl in range(SQUARE):
                if dh or dl:
                    block = self.block_of((l.high + dh) % 2, (l.low + dl) % SQUARE)
                    self.dealt.append(
                        l.copy(block, self.landed(l.high, l.low), dh=dh, dl=dl)
                    )
        self.mine = l.local(self.block_of(l.high, l.low), self.landed(l.high, l.low))


def back_kernel(
    sizes,
    lengths,
    x_in,
    g_in,
    residual_in,
    gain_in,
    normed_two_part,
    layer_part,
    dwg_in,
    dwu_in,
    dwd_in,
    qkv_in,
    wo_in,
    normed_one_in,
    q_in,
    kv_in,
    attn_in,
    cos_in,
    sin_in,
    layer_out,
    input_out,
    land_q,
    land_o,
    land_g,
    land_u,
    land_d,
    gains_out,
    kept_g,
    kept_u,
    kept_d,
    cross_g,
    cross_u,
    cross_d,
    kept_q,
    cross_q,
    kept_o,
    cross_o,
    send_q,
    send_o,
    own_a,
    recv_core,
    recv_block,
    relay,
    recv_block_b,
    relay_b,
    both,
    both_b,
    x_own,
    g_own,
    residual,
    gain_rows,
    low_all,
    wqkv,
    wo,
    q,
    kv,
    attn,
    attn_grad,
    dkv,
    dkv_send,
    dkv_recv,
    dqkv,
    cos,
    sin,
    gain_send,
    gain_recv,
    out_low,
    gain_sum,
    send_sem,
    recv_sem,
    local_sem,
):
    rows, local, model, high_size = sizes
    own = rows * local
    tokens = SQUARE * own
    half = model // 2
    block = x_own.shape[1] // 16
    heads = q.shape[2] // HD
    span = SQUARE * local
    keys = high_size * span
    f32, b16 = jnp.float32, jnp.bfloat16
    l = Links(send_sem, recv_sem, local_sem, high_size)
    steps = [
        dict(dx=dx, dh=dh, dl=dl)
        for dx in range(2)
        for dh in range(2)
        for dl in range(SQUARE)
        if dx or dh or dl
    ]
    l.greet(steps + [dict(dc=1)])

    def row_block(ref):
        def at(h, low):
            start = pl.multiple_of((h * SQUARE + low) * block, block)
            return ref.at[pl.ds(start, block)]

        return at

    def column_block(ref):
        def at(h, low):
            start = pl.multiple_of((h * SQUARE + low) * block, block)
            return ref.at[:, pl.ds(start, block)]

        return at

    def tall(ref):
        lines = ref.shape[1] // SQUARE
        return lambda h, low: ref.at[h, pl.ds(pl.multiple_of(low * lines, lines), lines)]

    def broad(ref):
        wide = ref.shape[2] // SQUARE
        return lambda h, low: ref.at[h, :, pl.ds(pl.multiple_of(low * wide, wide), wide)]

    def block_at(j):
        return pl.ds(pl.multiple_of(j * own, own), own)

    def part_at(ref, j, side):
        return ref.at[side, block_at(j)]

    handed = [
        l.copy(part_at(normed_two_part, j, 1 - l.core), recv_core.at[j], dc=1)
        for j in range(SQUARE)
    ]
    owned = [l.local(part_at(normed_two_part, j, l.core), own_a.at[j]) for j in range(SQUARE)]
    loads = [
        l.local(residual_in, residual),
        l.local(gain_in, gain_rows),
        l.local(g_in, g_own),
    ]
    grad_d = Grad(
        l, lambda x: dwd_in.at[x], kept_d, cross_d, column_block(kept_d), tall(land_d)
    )
    later = [
        l.local(x_in, x_own),
        l.local(wo_in, wo),
        l.local(attn_in, attn),
        l.local(q_in, q),
        l.local(kv_in, kv),
        l.local(qkv_in, wqkv),
        l.local(cos_in, cos),
        l.local(sin_in, sin),
    ]

    def own_total(j):
        return own_a[j].astype(f32) + recv_core[j].astype(f32)

    def norm_back(value_of, gain_row, grads):
        squares = jnp.zeros((own, 1), f32)
        inner = jnp.zeros((own, 1), f32)
        for side in range(2):
            at = slice(side * half, (side + 1) * half)
            value = value_of(side)
            squares = squares + jnp.sum(value * value, axis=1, keepdims=True)
            weighted = grads[side].astype(f32) * gain_rows[gain_row : gain_row + 1, at]
            inner = inner + jnp.sum(weighted * value, axis=1, keepdims=True)
        scale = lax.rsqrt(squares / model + EPSILON)
        pull = scale * scale * scale * (inner / model)
        outs = []
        for side in range(2):
            at = slice(side * half, (side + 1) * half)
            value = value_of(side)
            grad = grads[side].astype(f32)
            summed = jnp.sum(grad * (value * scale), axis=0, keepdims=True)
            for b in range(half // block):
                gain_send[gain_row, side * (half // block) + b, 0:1] = summed[
                    :, b * block : (b + 1) * block
                ]
            weighted = grad * gain_rows[gain_row : gain_row + 1, at]
            outs.append(weighted * scale - value * pull)
        return outs

    def push_gains(gain_row):
        me = (l.x * 2 + l.high) * SQUARE + l.low
        made = []
        for step in steps:
            to = ((l.x + step["dx"]) % 2 * 2 + (l.high + step["dh"]) % 2) * SQUARE + (
                l.low + step["dl"]
            ) % SQUARE
            made.append(l.copy(gain_send.at[gain_row, to], gain_recv.at[gain_row, me], **step))
        return made, l.local(gain_send.at[gain_row, me], gain_recv.at[gain_row, me])

    for made in owned:
        made.wait()
    arrived(handed)

    pushed = square_push(l, own_total, own_a, relay, recv_block)
    for made in loads:
        made.wait()
    swapped = square_settle(l, own_total, pushed, recv_block, both)
    swapped.wait_recv()
    l.left(pushed + [swapped])
    outs = norm_back(
        lambda side: residual[:, side * half : (side + 1) * half], 1, [both[0], both[1]]
    )
    for side in range(2):
        at = slice(side * half, (side + 1) * half)
        value = g_own[:, at].astype(f32) + outs[side]
        residual[:, at] = value
        low_all[side, block_at(l.low)] = value.astype(b16)

    def low_spot(side, low, part):
        start = pl.multiple_of(low * own + part * (own // 2), own // 2)
        return low_all.at[side, pl.ds(start, own // 2)]

    low_pushed = gather_push(l, low_spot, lambda part: low_spot(l.core, l.low, part))
    grad_g = Grad(l, lambda x: dwg_in.at[x], kept_g, cross_g, row_block(kept_g), broad(land_g))
    ffn_gains = push_gains(1)
    handed_b = [
        l.copy(part_at(layer_part, j, 1 - l.core), recv_core.at[j], dc=1) for j in range(SQUARE)
    ]
    owned = [l.local(part_at(layer_part, j, l.core), own_a.at[j]) for j in range(SQUARE)]
    for made in later:
        made.wait()
    low_handed, low_corner = gather_across(l, low_spot, low_pushed)
    grad_d.deal()
    arrived(low_handed)
    grad_u = Grad(l, lambda x: dwu_in.at[x], kept_u, cross_u, row_block(kept_u), broad(land_u))

    def out_grad_step(j, carry):
        at = block_at(j)
        rows_at = attn[at].astype(b16)
        low_out = dot(low_all[0, at], wo[0], ((1,), (1,)))
        low_out = (low_out + dot(low_all[1, at], wo[1], ((1,), (1,)))).astype(b16)
        for r in range(rows):
            spot = pl.ds(pl.multiple_of(j * local, local), local)
            attn_grad[r, spot] = low_out[r * local : (r + 1) * local]
        out_low[at] = rows_at
        return carry

    lax.fori_loop(0, SQUARE, out_grad_step, 0)
    send_o[...] = dot(out_low[...], low_all[1 - l.x], ((0,), (0,))).astype(b16)
    grad_o = Grad(l, None, kept_o, cross_o, column_block(kept_o), tall(land_o))
    grad_o.cross = l.copy(send_o, cross_o, dx=1)
    kept_o[...] = dot(out_low[...], low_all[l.x], ((0,), (0,))).astype(b16)

    for made in owned:
        made.wait()
    arrived(handed_b)
    pushed_b = square_push(l, own_total, own_a, relay_b, recv_block_b, split=True)

    def attend_row(r, carry):
        allowed = allowed_keys(l, lengths, r, span, keys)
        kv_row = kv[:, r].reshape(keys, 2 * HD)
        k, v = kv_row[:, :HD], kv_row[:, HD:]
        q_row, go_row = q[r], attn_grad[r]
        out_row = jnp.concatenate(
            [
                attn[pl.ds(pl.multiple_of(j * own + r * local, local), local)]
                for j in range(SQUARE)
            ],
            axis=0,
        )
        grads = []
        dk = jnp.zeros((keys, HD), f32)
        dv = jnp.zeros((keys, HD), f32)
        for head in range(heads):
            at = slice(head * HD, (head + 1) * HD)
            qh, go = q_row[:, at], go_row[:, at]
            delta = jnp.sum(go.astype(f32) * out_row[:, at], axis=1, keepdims=True)
            score = jnp.where(allowed, dot(qh, k, ((1,), (1,))), MASKED)
            top = jnp.max(score, axis=1, keepdims=True)
            grown = jnp.exp(score - top)
            probs = grown * (1.0 / jnp.sum(grown, axis=1, keepdims=True))
            dv = dv + dot(probs.astype(b16), go, ((0,), (0,)))
            pull = dot(go, v, ((1,), (1,)))
            score_grad = (probs * (pull - delta)).astype(b16)
            grads.append(dot(score_grad, k) * HD ** (-0.5))
            dk = dk + dot(score_grad, qh, ((0,), (0,)))
        turned = jnp.concatenate(grads, axis=1)
        for j in range(SQUARE):
            at = pl.ds(pl.multiple_of(j * own + r * local, local), local)
            value = turned[j * local : (j + 1) * local]
            cos_q, sin_q = rope_rows(cos, sin, at, heads // 2)
            dqkv[at, : heads * HD] = (value * cos_q - roll_heads(value) * sin_q).astype(b16)
        both_kv = jnp.concatenate([dk, dv], axis=1)
        for part in range(high_size):
            dkv[part, r] = both_kv[part * span : (part + 1) * span]
        return carry

    dkv_copies = []
    for r in range(rows):
        lax.fori_loop(r, r + 1, attend_row, 0)
        dkv_send[r] = dkv[1 - l.high, r].astype(b16)
        dkv_copies.append(l.copy(dkv_send.at[r], dkv_recv.at[r], dh=1))
        if r == 0:
            square_relay(l, pushed_b, own_a, relay_b, recv_block_b)
            grad_g.deal()
    l.left(low_pushed + low_handed + low_corner)
    normed = l.local(normed_one_in, low_all)
    grad_o.deal()
    both_b_copy = square_settle(l, own_total, pushed_b, recv_block_b, both_b)
    arrived(dkv_copies)

    def unrotate_step(i, carry):
        at = pl.ds(pl.multiple_of(i * local, local), local)
        spot = pl.ds(pl.multiple_of((i // rows) * local, local), local)
        kv_sum = dkv[l.high, i % rows, spot] + dkv_recv[i % rows, spot].astype(f32)
        cos_k, sin_k = rope_key_rows(cos, sin, at)
        turned = kv_sum * cos_k - roll_heads(kv_sum) * sin_k
        dqkv[at, heads * HD :] = turned.astype(b16)
        return carry

    lax.fori_loop(0, SQUARE * rows, unrotate_step, 0)

    def project_back(j, side):
        weight = wqkv[pl.ds(pl.multiple_of(side * half, half), half)]
        return dot(dqkv[block_at(j)], weight, ((1,), (1,)))

    both_b_copy.wait_recv()
    l.left(pushed_b)
    handed = []
    for j in range(SQUARE):
        own_a[j] = project_back(j, 1 - l.core).astype(b16)
        handed.append(l.copy(own_a.at[j], recv_core.at[j], dc=1))
    normed.wait()
    send_q[...] = dot(low_all[1 - l.x], dqkv[...], ((0,), (0,))).astype(b16)
    arrived(handed)

    def own_total_c(j):
        return project_back(j, l.core) + recv_core[j].astype(f32)

    l.left(handed)
    pushed = square_push(l, own_total_c, own_a, relay, recv_block)
    grad_q = Grad(l, None, kept_q, cross_q, row_block(kept_q), lambda h, low: land_q.at[h, low])
    grad_q.cross = l.copy(send_q, cross_q, dx=1)
    kept_q[...] = dot(low_all[l.x], dqkv[...], ((0,), (0,))).astype(b16)
    grad_u.deal()
    square_settle(l, own_total_c, pushed, recv_block, both).wait_recv()
    outs = norm_back(
        lambda side: x_own[:, side * half : (side + 1) * half].astype(f32),
        0,
        [both[0], both[1]],
    )
    attn_gains = push_gains(0)
    for side in range(2):
        at = slice(side * half, (side + 1) * half)
        x_own[:, at] = (residual[:, at] + outs[side]).astype(b16)
    stores = [l.local(x_own, input_out)]
    residual_load = l.local(residual_in, residual)
    grad_q.deal()
    residual_load.wait()
    for side in range(2):
        at = slice(side * half, (side + 1) * half)
        g_own[:, at] = (residual[:, at] + both_b[side].astype(f32)).astype(b16)
    stores.append(l.local(g_own, layer_out))
    for made, kept in (ffn_gains, attn_gains):
        arrived(made)
        kept.wait()
    for row in range(2):
        total = jnp.zeros((8, block), f32)
        for b in range(16):
            total = total + gain_recv[row, b]
        gain_sum[row : row + 1] = total[0:1]
    stores.append(l.local(gain_sum, gains_out))
    for grad in (grad_d, grad_o, grad_g, grad_u, grad_q):
        grad.mine.wait()
        arrived(grad.dealt)
    for made in stores:
        made.wait()
    l.finish()


def back(sizes, lengths, *arrays):
    rows, local, model, high_size = sizes
    own = rows * local
    tokens = SQUARE * own
    half = model // 2
    block = model // 16
    ff = arrays[6].shape[2]
    width = arrays[9].shape[1]
    wide = width - 2 * HD
    span = SQUARE * local
    b16, f32 = jnp.bfloat16, jnp.float32
    shape = jax.ShapeDtypeStruct
    vmem = pltpu.VMEM
    outs = (
        shape((own, model), b16),
        shape((own, model), b16),
        shape((2, SQUARE, block, width), b16),
        shape((2, SQUARE * wide, block), b16),
        shape((2, block, SQUARE * ff), b16),
        shape((2, block, SQUARE * ff), b16),
        shape((2, SQUARE * ff, block), b16),
        shape((8, block), f32),
    )
    anywhere = pl.BlockSpec(memory_space=pl.ANY)
    scratch = [
        vmem((half, ff), b16),
        vmem((half, ff), b16),
        vmem((ff, half), b16),
        vmem((half, ff), b16),
        vmem((half, ff), b16),
        vmem((ff, half), b16),
        vmem((half, width), b16),
        vmem((half, width), b16),
        vmem((wide, half), b16),
        vmem((wide, half), b16),
        vmem((half, width), b16),
        vmem((wide, half), b16),
        vmem((SQUARE, own, half), b16),
        vmem((SQUARE, own, half), b16),
        vmem((2, own, half), b16),
        vmem((2, own // 2, half), b16),
        vmem((2, own, half), b16),
        vmem((2, own // 2, half), b16),
        vmem((2, own, half), b16),
        vmem((2, own, half), b16),
        vmem((own, model), b16),
        vmem((own, model), b16),
        vmem((own, model), f32),
        vmem((8, model), f32),
        vmem((2, tokens, half), b16),
        vmem((model, width), b16),
        vmem((2, wide, half), b16),
        vmem((rows, span, wide), b16),
        vmem((high_size, rows, span, 2 * HD), b16),
        vmem((tokens, wide), f32),
        vmem((rows, span, wide), b16),
        vmem((high_size, rows, span, 2 * HD), f32),
        vmem((rows, span, 2 * HD), b16),
        vmem((rows, span, 2 * HD), b16),
        vmem((tokens, width), b16),
        vmem((tokens, 2 * HD), f32),
        vmem((tokens, 2 * HD), f32),
        vmem((2, 16, 8, block), f32),
        vmem((2, 16, 8, block), f32),
        vmem((tokens, wide), b16),
        vmem((8, block), f32),
        pltpu.SemaphoreType.DMA((128,)),
        pltpu.SemaphoreType.DMA((128,)),
        pltpu.SemaphoreType.DMA((64,)),
    ]
    return pl.pallas_call(
        functools.partial(back_kernel, sizes),
        out_shape=outs,
        in_specs=[pl.BlockSpec(memory_space=pltpu.SMEM)] + [anywhere] * len(arrays),
        out_specs=[anywhere] * len(outs),
        scratch_shapes=scratch,
        compiler_params=pltpu.CompilerParams(
            collective_id=1, has_side_effects=True, vmem_limit_bytes=VMEM
        ),
        name="back",
    )(lengths, *arrays)


def norm_back(values, scale, gain, grad):
    weighted = grad * gain
    gain_grad = jnp.sum(grad * values * scale, axis=0)
    inner = jnp.mean(weighted * values, axis=-1, keepdims=True)
    return (weighted * scale - values * scale**3 * inner, gain_grad)


def shards_exchanged(
    hidden_in,
    doc_lengths,
    attn_gain,
    query_weight,
    key_weight,
    value_weight,
    output_weight,
    ffn_gain,
    gate_weight,
    up_weight,
    down_weight,
    out_grad,
):
    rows, local, model = hidden_in.shape
    tokens = rows * local
    seq = lax.axis_index("seq")
    core = lax.axis_index("mp")
    low, high = seq % SQUARE, seq // SQUARE
    high_size = lax.axis_size("seq") // SQUARE
    place = (lax.axis_index("dp"), high, low, lax.axis_size("dp"), high_size)
    group = H // KVH
    span = SQUARE * local

    ends = jnp.cumsum(doc_lengths, axis=-1)
    info = jnp.concatenate([jnp.stack([low, high]), ends.reshape(-1)]).astype(jnp.int32)

    gains = lax.all_gather(jnp.stack([attn_gain, ffn_gain]), ("dp", "seq"), axis=1, tiled=True)
    gain_one, gain_two = gains[0].astype(jnp.float32), gains[1].astype(jnp.float32)

    own_in = hidden_in.reshape(tokens, model)
    all_in = gather_square(own_in, core).astype(jnp.float32)
    query_own = spread_weight(query_weight, 0, place)
    key_own = spread_weight(key_weight, 0, place)
    value_own = spread_weight(value_weight, 0, place)
    output_own = spread_weight(output_weight, 1, place)
    gate_own = spread_weight(gate_weight, 0, place)
    up_own = spread_weight(up_weight, 0, place)
    down_own = spread_weight(down_weight, 1, place)
    all_grad = gather_square(out_grad.reshape(tokens, model), core)

    blocks = low ^ jnp.arange(SQUARE, dtype=jnp.int32)
    spots = (high * span + blocks[:, None] * local + jnp.arange(local, dtype=jnp.int32)[None, :])
    reached = spots[:, None, :, None] >= ends[None, :, None, :]
    begin = jnp.max(jnp.where(reached, ends[None, :, None, :], 0), axis=-1)
    position = (spots[:, None, :] - begin).astype(jnp.float32)
    cosine, sine = rope_tables(position, HD)

    scale_one = lax.rsqrt(jnp.mean(all_in * all_in, axis=-1, keepdims=True) + EPSILON)
    normed_one = (all_in * scale_one * gain_one).astype(jnp.bfloat16)
    query_pre = dot(normed_one, query_own).reshape(SQUARE, rows, local, group, HD)
    key_pre = dot(normed_one, key_own).reshape(SQUARE, rows, local, 1, HD)
    value_pre = dot(normed_one, value_own).reshape(SQUARE, rows, local, HD)
    queries = rotate(query_pre, cosine, sine).astype(jnp.bfloat16)
    queries = queries.reshape(SQUARE, rows, local, group * HD)
    keys = rotate(key_pre, cosine, sine).astype(jnp.bfloat16).reshape(value_pre.shape)
    kv = jnp.concatenate([keys, value_pre.astype(jnp.bfloat16)], axis=-1)[None]
    for bit in bits_of(high_size):
        kv = jnp.concatenate([kv, swap(kv, "seq", SQUARE * bit)], axis=0)
    attn, lse = attend(info, queries, kv)
    attn_low = attn.reshape(SQUARE * tokens, group * HD).astype(jnp.bfloat16)
    residual = own_in.astype(jnp.float32) + scatter_square(dot(attn_low, output_own), core)

    scale_two = lax.rsqrt(jnp.mean(residual * residual, axis=-1, keepdims=True) + EPSILON)
    normed_two = (residual * scale_two * gain_two).astype(jnp.bfloat16)
    normed_two = gather_square(normed_two, core)
    gate_proj = dot(normed_two, gate_own)
    up_proj = dot(normed_two, up_own)
    sigmoid_gate = jax.nn.sigmoid(gate_proj)
    silu_gate = gate_proj * sigmoid_gate
    hidden_units = (silu_gate * up_proj).astype(jnp.bfloat16)
    hidden_grad = dot(all_grad, down_own, ((1,), (1,)))
    gate_act = (
        hidden_grad * up_proj * sigmoid_gate * (1.0 + gate_proj * (1.0 - sigmoid_gate))
    ).astype(jnp.bfloat16)
    up_act = (hidden_grad * silu_gate).astype(jnp.bfloat16)
    down_grad = settle_grad(dot(hidden_units, all_grad, ((0,), (0,))), 1, place)
    normed_two_grad = scatter_square(
        dot(gate_act, gate_own, ((1,), (1,))) + dot(up_act, up_own, ((1,), (1,))), core
    )
    layer_out = residual + scatter_square(dot(hidden_units, down_own), core)
    layer_out = layer_out.astype(jnp.bfloat16).reshape(hidden_in.shape)
    gate_grad = settle_grad(dot(normed_two, gate_act, ((0,), (0,))), 0, place)
    up_grad = settle_grad(dot(normed_two, up_act, ((0,), (0,))), 0, place)

    residual_part, ffn_gain_grad = norm_back(residual, scale_two, gain_two, normed_two_grad)
    residual_grad = out_grad.reshape(tokens, model).astype(jnp.float32) + residual_part
    residual_low = gather_square(residual_grad.astype(jnp.bfloat16), core)
    output_grad = settle_grad(dot(attn_low, residual_low, ((0,), (0,))), 1, place)
    attn_grad = dot(residual_low, output_own, ((1,), (1,))).astype(jnp.bfloat16)
    attn_grad = attn_grad.reshape(queries.shape)
    query_acc, kv_acc = attend_back(info, queries, kv, attn_grad, attn, lse)
    for bit in reversed(bits_of(high_size)):
        sent = kv_acc[bit:].astype(jnp.bfloat16)
        kv_acc = kv_acc[:bit] + swap(sent, "seq", SQUARE * bit).astype(jnp.float32)
    kv_acc = kv_acc[0]
    query_back = unrotate(query_acc.reshape(query_pre.shape), cosine, sine).astype(jnp.bfloat16)
    key_back = unrotate(kv_acc[..., :HD].reshape(key_pre.shape), cosine, sine)
    key_back = key_back.astype(jnp.bfloat16).reshape(SQUARE * tokens, HD)
    value_back = kv_acc[..., HD:].astype(jnp.bfloat16).reshape(SQUARE * tokens, HD)
    query_back = query_back.reshape(SQUARE * tokens, group * HD)
    normed_one_grad = scatter_square(
        dot(query_back, query_own, ((1,), (1,)))
        + dot(key_back, key_own, ((1,), (1,)))
        + dot(value_back, value_own, ((1,), (1,))),
        core,
    )
    query_grad = settle_grad(dot(normed_one, query_back, ((0,), (0,))), 0, place)
    key_grad = settle_grad(dot(normed_one, key_back, ((0,), (0,))), 0, place)
    value_grad = settle_grad(dot(normed_one, value_back, ((0,), (0,))), 0, place)
    own_32 = own_in.astype(jnp.float32)
    own_scale = lax.rsqrt(jnp.mean(own_32 * own_32, axis=-1, keepdims=True) + EPSILON)
    input_part, attn_gain_grad = norm_back(own_32, own_scale, gain_one, normed_one_grad)
    input_grad = (residual_grad + input_part).astype(jnp.bfloat16).reshape(hidden_in.shape)
    gain_grads = lax.psum_scatter(
        jnp.stack([attn_gain_grad, ffn_gain_grad]), ("dp", "seq"), scatter_dimension=1, tiled=True
    )
    return (
        layer_out,
        input_grad,
        gain_grads[0],
        query_grad,
        key_grad,
        value_grad,
        output_grad,
        gain_grads[1],
        gate_grad,
        up_grad,
        down_grad,
    )


def shards(
    hidden_in,
    doc_lengths,
    attn_gain,
    query_weight,
    key_weight,
    value_weight,
    output_weight,
    ffn_gain,
    gate_weight,
    up_weight,
    down_weight,
    out_grad,
):
    rows, local, model = hidden_in.shape
    tokens = rows * local
    seq = lax.axis_index("seq")
    high = seq // SQUARE
    high_size = lax.axis_size("seq") // SQUARE
    block = query_weight.shape[0]
    if block % 128 or high_size != 2 or lax.axis_size("dp") != 2:
        return shards_exchanged(
            hidden_in,
            doc_lengths,
            attn_gain,
            query_weight,
            key_weight,
            value_weight,
            output_weight,
            ffn_gain,
            gate_weight,
            up_weight,
            down_weight,
            out_grad,
        )
    group = H // KVH
    span = SQUARE * local
    width = (group + 2) * HD

    spots = high * span + jnp.arange(span, dtype=jnp.int32).reshape(SQUARE, 1, local)
    begin, end = jnp.zeros((1, rows, 1), jnp.int32), jnp.zeros((1, rows, 1), jnp.int32)
    for doc in range(doc_lengths.shape[1]):
        end = end + doc_lengths[:, doc].reshape(1, rows, 1)
        begin = jnp.where(spots >= end, end, begin)
    position = (spots - begin).astype(jnp.float32).reshape(SQUARE * tokens, 1)
    angles = position * jnp.tile(inverse_freqs(HD), 4)[None, :]
    sign = jnp.where(jnp.arange(2 * HD) % HD < HD // 2, -1.0, 1.0)[None, :]
    cos, sin = jnp.cos(angles), jnp.sin(angles) * sign
    qkv_shard = jnp.concatenate(
        [
            query_weight.reshape(block, SQUARE, group * HD),
            key_weight.reshape(block, SQUARE, HD),
            value_weight.reshape(block, SQUARE, HD),
        ],
        axis=2,
    ).reshape(block, SQUARE * width)
    gain_shard = jnp.concatenate(
        [attn_gain[None, None], ffn_gain[None, None], jnp.zeros((1, 14, block), jnp.bfloat16)],
        axis=1,
    )
    lengths = doc_lengths
    own_in = hidden_in.reshape(tokens, model)
    own_grad = out_grad.reshape(tokens, model)
    (
        qkv_own,
        output_own,
        gains,
        normed_one,
        queries,
        kv,
        attn,
        residual,
        gate_part,
        up_part,
        down_part,
        normed_two_part,
        layer_part,
    ) = front(
        (rows, local, model, high_size),
        lengths,
        own_in,
        own_grad,
        qkv_shard,
        gain_shard,
        output_weight,
        gate_weight,
        up_weight,
        down_weight,
        cos,
        sin,
    )
    (
        layer_out,
        input_grad,
        *landed,
        gain_grads,
    ) = back(
        (rows, local, model, high_size),
        lengths,
        own_in,
        own_grad,
        residual,
        gains,
        normed_two_part,
        layer_part,
        gate_part,
        up_part,
        down_part,
        qkv_own,
        output_own,
        normed_one,
        queries,
        kv,
        attn,
        cos,
        sin,
    )
    qkv_grad, output_grad, gate_grad, up_grad, down_grad = (
        part[0].astype(jnp.float32) + part[1].astype(jnp.float32) for part in landed
    )
    query_grad = qkv_grad[..., : group * HD].transpose(1, 0, 2).reshape(block, -1)
    key_grad = qkv_grad[..., group * HD : (group + 1) * HD].transpose(1, 0, 2).reshape(block, -1)
    value_grad = qkv_grad[..., (group + 1) * HD :].transpose(1, 0, 2).reshape(block, -1)
    return (
        layer_out.reshape(hidden_in.shape),
        input_grad.reshape(hidden_in.shape),
        gain_grads[0],
        query_grad,
        key_grad,
        value_grad,
        output_grad,
        gain_grads[1],
        gate_grad,
        up_grad,
        down_grad,
    )


def solution(mesh):
    return jax.shard_map(
        shards,
        mesh=mesh,
        in_specs=(
            P("dp", "seq", None),
            P("dp", None),
            P(("dp", "seq")),
            P(("dp", "seq"), "mp"),
            P(("dp", "seq"), "mp"),
            P(("dp", "seq"), "mp"),
            P("mp", ("dp", "seq")),
            P(("dp", "seq")),
            P(("dp", "seq"), "mp"),
            P(("dp", "seq"), "mp"),
            P("mp", ("dp", "seq")),
            P("dp", "seq", None),
        ),
        out_specs=(
            P("dp", "seq", None),
            P("dp", "seq", None),
            P(("dp", "seq")),
            P(("dp", "seq"), "mp"),
            P(("dp", "seq"), "mp"),
            P(("dp", "seq"), "mp"),
            P("mp", ("dp", "seq")),
            P(("dp", "seq")),
            P(("dp", "seq"), "mp"),
            P(("dp", "seq"), "mp"),
            P("mp", ("dp", "seq")),
        ),
        check_vma=False,
    )
```

```python
import functools
import math

import jax
import jax.numpy as jnp
from jax import lax
from jax.experimental import pallas as pl
from jax.experimental.pallas import tpu as pltpu
from jax.sharding import PartitionSpec as P

H = 32
KVH = 8
HD = 64
SQUARE = 4

EPSILON = 1e-05
MASKED = -1e30
ROPE_THETA = 500000.0
ROPE_FACTOR = 32.0
LOW_FACTOR = 1.0
HIGH_FACTOR = 4.0
PRIOR_CONTEXT = 8192.0
VMEM = 62 * 1024 * 1024


def inverse_freqs(head_dim):
    ladder = jnp.arange(head_dim // 2, dtype=jnp.float32)
    base = ROPE_THETA ** (-2.0 * ladder / head_dim)
    wavelen = 2.0 * math.pi / base
    smooth = (PRIOR_CONTEXT / wavelen - LOW_FACTOR) / (HIGH_FACTOR - LOW_FACTOR)
    blended = (1.0 - smooth) * base / ROPE_FACTOR + smooth * base
    low_limit = PRIOR_CONTEXT / LOW_FACTOR
    high_limit = PRIOR_CONTEXT / HIGH_FACTOR
    return jnp.where(
        wavelen < high_limit, base, jnp.where(wavelen > low_limit, base / ROPE_FACTOR, blended)
    )


def rope_tables(position, head_dim):
    angles = position[..., None] * inverse_freqs(head_dim)
    angles = jnp.concatenate([angles, angles], axis=-1)
    return (jnp.cos(angles)[..., None, :], jnp.sin(angles)[..., None, :])


def rotate(values, cosine, sine):
    middle = values.shape[-1] // 2
    turned = jnp.concatenate([-values[..., middle:], values[..., :middle]], axis=-1)
    return values * cosine + turned * sine


def unrotate(grads, cosine, sine):
    middle = grads.shape[-1] // 2
    scaled = grads * sine
    turned = jnp.concatenate([scaled[..., middle:], -scaled[..., :middle]], axis=-1)
    return grads * cosine + turned


def dot(left, right, dims=((1,), (0,))):
    return lax.dot_general(left, right, (dims, ((), ())), preferred_element_type=jnp.float32)


def swap(value, axis, mask):
    size = lax.axis_size(axis)
    return lax.ppermute(value, axis, [(i, i ^ mask) for i in range(size)])


def cut(value, start, length, axis):
    return lax.dynamic_slice_in_dim(value, start, length, axis)


def put(whole, part, start, axis):
    return lax.dynamic_update_slice_in_dim(whole, part, start, axis)


def mask_of(info, row, row_count, local, keys):
    span = SQUARE * local
    low, high = info[0], info[1]

    def place_of(index):
        block = (index // local) % SQUARE
        part = index // span
        return (high ^ part) * span + (low ^ block) * local + index % local

    def segment_of(place):
        total = jnp.zeros_like(place)
        for doc in range(4):
            total = total + (place >= info[2 + row * 4 + doc]).astype(jnp.int32)
        return total

    query = place_of(lax.broadcasted_iota(jnp.int32, (span, 1), 0))
    key = place_of(lax.broadcasted_iota(jnp.int32, (1, keys), 1))
    return (segment_of(query) == segment_of(key)) & (query >= key)


def attend_kernel(local, keys, group, info, q_ref, kv_ref, out_ref, lse_ref):
    row = pl.program_id(0)
    span = SQUARE * local
    allowed = mask_of(info, row, None, local, keys)
    kv = kv_ref[...].reshape(keys, 2 * HD)
    k, v = kv[:, :HD], kv[:, HD:]
    q_all = q_ref[...].reshape(span, group * HD)
    outs, sums = [], []
    for head in range(group):
        q = q_all[:, head * HD : (head + 1) * HD]
        score = dot(q, k, ((1,), (1,))) * HD ** (-0.5)
        score = jnp.where(allowed, score, MASKED)
        top = jnp.max(score, axis=1, keepdims=True)
        grown = jnp.exp(score - top)
        total = jnp.sum(grown, axis=1, keepdims=True)
        lse = top + jnp.log(total)
        probs = (grown * (1.0 / total)).astype(jnp.bfloat16)
        outs.append(dot(probs, v))
        sums.append(lse)
    out_ref[...] = jnp.concatenate(outs, axis=1).reshape(out_ref.shape)
    lse_ref[...] = jnp.concatenate(sums, axis=1).reshape(lse_ref.shape)


def attend(info, queries, kv):
    blocks, rows, local, width = queries.shape
    parts = kv.shape[0]
    keys = parts * blocks * local
    group = width // HD
    return pl.pallas_call(
        functools.partial(attend_kernel, local, keys, group),
        grid=(rows,),
        out_shape=(
            jax.ShapeDtypeStruct((blocks, rows, local, width), jnp.float32),
            jax.ShapeDtypeStruct((blocks, rows, local, group), jnp.float32),
        ),
        in_specs=[
            pl.BlockSpec(memory_space=pltpu.SMEM),
            pl.BlockSpec((blocks, 1, local, width), lambda r: (0, r, 0, 0)),
            pl.BlockSpec((parts, blocks, 1, local, 2 * HD), lambda r: (0, 0, r, 0, 0)),
        ],
        out_specs=(
            pl.BlockSpec((blocks, 1, local, width), lambda r: (0, r, 0, 0)),
            pl.BlockSpec((blocks, 1, local, group), lambda r: (0, r, 0, 0)),
        ),
        compiler_params=pltpu.CompilerParams(vmem_limit_bytes=VMEM),
        cost_estimate=pl.CostEstimate(
            flops=8 * rows * blocks * local * keys * width,
            bytes_accessed=rows * blocks * local * width * 8,
            transcendentals=rows * blocks * local * keys * group,
        ),
        name="attend",
    )(info, queries, kv)


def attend_back_kernel(
    local, keys, group, info, q_ref, kv_ref, go_ref, out_ref, lse_ref, dq_ref, dkv_ref
):
    row = pl.program_id(0)
    span = SQUARE * local
    allowed = mask_of(info, row, None, local, keys)
    kv = kv_ref[...].reshape(keys, 2 * HD)
    k, v = kv[:, :HD], kv[:, HD:]
    q_all = q_ref[...].reshape(span, group * HD)
    go_all = go_ref[...].reshape(span, group * HD)
    out_all = out_ref[...].reshape(span, group * HD)
    lse_all = lse_ref[...].reshape(span, group)
    dq = []
    dk = jnp.zeros((keys, HD), jnp.float32)
    dv = jnp.zeros((keys, HD), jnp.float32)
    scale = HD ** (-0.5)
    for head in range(group):
        q = q_all[:, head * HD : (head + 1) * HD]
        go = go_all[:, head * HD : (head + 1) * HD]
        out = out_all[:, head * HD : (head + 1) * HD]
        delta = jnp.sum(go.astype(jnp.float32) * out, axis=1, keepdims=True)
        score = dot(q, k, ((1,), (1,))) * scale
        probs = jnp.exp(jnp.where(allowed, score, MASKED) - lse_all[:, head : head + 1])
        dv = dv + dot(probs.astype(jnp.bfloat16), go, ((0,), (0,)))
        prob_grad = dot(go, v, ((1,), (1,)))
        score_grad = (probs * (prob_grad - delta)).astype(jnp.bfloat16)
        dq.append(dot(score_grad, k) * scale)
        dk = dk + dot(score_grad, q, ((0,), (0,)))
    dq_ref[...] = jnp.concatenate(dq, axis=1).reshape(dq_ref.shape)
    dkv_ref[...] = jnp.concatenate([dk * scale, dv], axis=1).reshape(dkv_ref.shape)


def attend_back(info, queries, kv, out_grads, out, lse):
    blocks, rows, local, width = queries.shape
    parts = kv.shape[0]
    keys = parts * blocks * local
    group = width // HD
    wide = pl.BlockSpec((blocks, 1, local, width), lambda r: (0, r, 0, 0))
    kv_spec = pl.BlockSpec((parts, blocks, 1, local, 2 * HD), lambda r: (0, 0, r, 0, 0))
    return pl.pallas_call(
        functools.partial(attend_back_kernel, local, keys, group),
        grid=(rows,),
        out_shape=(
            jax.ShapeDtypeStruct(queries.shape, jnp.float32),
            jax.ShapeDtypeStruct(kv.shape, jnp.float32),
        ),
        in_specs=[
            pl.BlockSpec(memory_space=pltpu.SMEM),
            wide,
            kv_spec,
            wide,
            wide,
            pl.BlockSpec((blocks, 1, local, group), lambda r: (0, r, 0, 0)),
        ],
        out_specs=(wide, kv_spec),
        compiler_params=pltpu.CompilerParams(vmem_limit_bytes=VMEM),
        cost_estimate=pl.CostEstimate(
            flops=20 * rows * blocks * local * keys * width,
            bytes_accessed=rows * blocks * local * width * 16,
            transcendentals=rows * blocks * local * keys * group,
        ),
        name="attend_back",
    )(info, queries, kv, out_grads, out, lse)


def bits_of(size):
    return [1 << b for b in range(size.bit_length() - 1)]


def spread_weight(shard, axis, place):
    dp, high, low, dp_size, high_size = place
    other = 1 - axis
    block = shard.shape[axis]
    width = shard.shape[other] // SQUARE
    pieces = [cut(shard, low * width, width, other)]
    for mask in range(1, SQUARE):
        pieces.append(swap(cut(shard, (low ^ mask) * width, width, other), "seq", mask))
    shape = [0, 0]
    shape[axis], shape[other] = SQUARE * block, width
    square = jnp.zeros(shape, shard.dtype)
    for mask in range(SQUARE):
        square = put(square, pieces[mask], (low ^ mask) * block, axis)
    parts = {(0, 0): square}
    for bit in bits_of(high_size):
        for (a, b) in list(parts):
            parts[a, b ^ bit] = swap(parts[a, b], "seq", SQUARE * bit)
    for bit in bits_of(dp_size):
        for (a, b) in list(parts):
            parts[a ^ bit, b] = swap(parts[a, b], "dp", bit)
    shape[axis] = SQUARE * block * high_size * dp_size
    whole = jnp.zeros(shape, shard.dtype)
    for (a, b), part in parts.items():
        index = (dp ^ a) * high_size + (high ^ b)
        whole = put(whole, part, index * SQUARE * block, axis)
    return whole


def settle_grad(grad, axis, place):
    dp, high, low, dp_size, high_size = place
    other = 1 - axis
    width = grad.shape[other]
    kept = grad
    for index, size, name, unit in ((dp, dp_size, "dp", 1), (high, high_size, "seq", SQUARE)):
        for bit in reversed(bits_of(size)):
            half = kept.shape[axis] // 2
            mine = (index // bit) % 2
            sent = cut(kept, (1 - mine) * half, half, axis).astype(jnp.bfloat16)
            kept = cut(kept, mine * half, half, axis) + swap(sent, name, unit * bit).astype(
                jnp.float32
            )
    block = kept.shape[axis] // SQUARE
    shape = [0, 0]
    shape[axis], shape[other] = block, SQUARE * width
    whole = jnp.zeros(shape, jnp.float32)
    whole = put(whole, cut(kept, low * block, block, axis), low * width, other)
    for mask in range(1, SQUARE):
        sent = cut(kept, (low ^ mask) * block, block, axis).astype(jnp.bfloat16)
        got = swap(sent, "seq", mask).astype(jnp.float32)
        whole = put(whole, got, (low ^ mask) * width, other)
    return whole


def gather_square(own, core):
    tokens, width = own.shape
    half = width // 2
    mine = cut(own, core * half, half, 1)
    got = jnp.concatenate([swap(mine, "seq", mask) for mask in range(1, SQUARE)], axis=0)
    across = swap(got, "mp", 1)
    first = jnp.where(core == 0, got, across)
    second = jnp.where(core == 0, across, got)
    return jnp.concatenate([own, jnp.concatenate([first, second], axis=1)], axis=0)


def scatter_square(partial, core):
    tokens, width = partial.shape[0] // SQUARE, partial.shape[1]
    half = width // 2
    kept = cut(partial, core * half, half, 1)
    sent = cut(partial, (1 - core) * half, half, 1).astype(jnp.bfloat16)
    kept = kept + swap(sent, "mp", 1).astype(jnp.float32)
    total = kept[:tokens]
    for mask in range(1, SQUARE):
        part = kept[mask * tokens : (mask + 1) * tokens].astype(jnp.bfloat16)
        total = total + swap(part, "seq", mask).astype(jnp.float32)
    mine = total.astype(jnp.bfloat16)
    across = swap(mine, "mp", 1)
    return jnp.concatenate(
        [jnp.where(core == 0, mine, across), jnp.where(core == 0, across, mine)], axis=1
    ).astype(jnp.float32)


MESH = pl.DeviceIdType.MESH


class Links:
    def __init__(self, send_sem, recv_sem, local_sem, high_size):
        self.send_sem, self.recv_sem, self.local_sem = send_sem, recv_sem, local_sem
        self.x, self.seq, self.core = (lax.axis_index(a) for a in ("dp", "seq", "mp"))
        self.high_size = high_size
        self.low, self.high = self.seq % SQUARE, self.seq // SQUARE
        self.count = self.local_count = 0
        self.sent = []

    def beside(self, flip):
        if flip == 1:
            return self.low + 1 - 2 * (self.low % 2)
        return (self.low + 2) % SQUARE if flip == 2 else SQUARE - 1 - self.low

    def to(self, dx=0, dh=0, dl=0, dc=0, flip=0):
        low = self.beside(flip) if flip else (self.low + dl) % SQUARE
        seq = ((self.high + dh) % self.high_size) * SQUARE + low
        return ((self.x + dx) % 2, seq, (self.core + dc) % 2)

    def copy(self, src, dst, **step):
        k = self.count
        self.count += 1
        made = pltpu.make_async_remote_copy(
            src_ref=src,
            dst_ref=dst,
            send_sem=self.send_sem.at[k],
            recv_sem=self.recv_sem.at[k],
            device_id=self.to(**step),
            device_id_type=MESH,
        )
        made.start()
        self.sent.append(made)
        return made

    def local(self, src, dst):
        k = self.local_count
        self.local_count += 1
        made = pltpu.make_async_copy(src, dst, self.local_sem.at[k])
        made.start()
        return made

    def greet(self, steps):
        barrier = pltpu.get_barrier_semaphore()
        for step in steps:
            pl.semaphore_signal(barrier, inc=1, device_id=self.to(**step), device_id_type=MESH)
        pl.semaphore_wait(barrier, len(steps))

    def left(self, copies):
        for made in copies:
            made.wait_send()
            self.sent = [one for one in self.sent if one is not made]

    def finish(self):
        for made in self.sent:
            made.wait_send()


def arrived(copies):
    for made in copies:
        made.wait_recv()


class Weight:
    def __init__(self, links, slice_of, spot):
        self.links, self.spot = links, spot
        l = links
        self.own = l.local(slice_of(l.low), spot(l.x, l.high, l.low, 1))
        self.near, self.far = [], []
        for dh in range(2):
            for dl in range(SQUARE):
                if dh or dl:
                    made = l.copy(
                        slice_of((l.low + dl) % SQUARE),
                        spot(l.x, l.high, l.low, 1),
                        dh=dh,
                        dl=dl,
                    )
                    (self.far if dh else self.near).append(made)

    def pass_near(self):
        self.own.wait()
        arrived(self.near)
        l = self.links
        part = self.spot(l.x, l.high, 0, SQUARE)
        self.across = [l.copy(part, part, dx=1)]

    def pass_far(self):
        arrived(self.far)
        l = self.links
        part = self.spot(l.x, 1 - l.high, 0, SQUARE)
        self.across.append(l.copy(part, part, dx=1))

    def wait(self):
        arrived(self.across)


def gather_push(l, everyone, source):
    return [
        l.copy(source(part), everyone(l.core, l.low, part), flip=flip)
        for flip, part in ((1, 0), (2, 1), (1, 1), (2, 0))
    ]


def gather_across(l, everyone, pushed):
    handed, corner = [], []
    for k, (flip, part) in enumerate(((1, 0), (2, 1), (1, 1), (2, 0))):
        pushed[k].wait_recv()
        block = everyone(l.core, l.beside(flip), part)
        if k < 2:
            corner.append(l.copy(block, block, flip=3 - flip))
        handed.append(l.copy(block, block, dc=1))
    for part in range(2):
        corner[part].wait_recv()
        block = everyone(l.core, l.beside(3), part)
        handed.append(l.copy(block, block, dc=1))
    return handed, corner


def square_push(l, total_of, send, relay, landed, split=False):
    lines = send.shape[1]
    first, second = pl.ds(0, lines // 2), pl.ds(lines // 2, lines // 2)
    one, two, corner = (l.beside(flip) for flip in (1, 2, 3))
    send[corner] = total_of(corner).astype(jnp.bfloat16)
    made = [
        l.copy(send.at[corner, first], relay.at[0], flip=1),
        l.copy(send.at[corner, second], relay.at[1], flip=2),
    ]
    send[one] = total_of(one).astype(jnp.bfloat16)
    made.append(l.copy(send.at[one, first], landed.at[0, first], flip=1))
    send[two] = total_of(two).astype(jnp.bfloat16)
    made.append(l.copy(send.at[two, second], landed.at[1, second], flip=2))
    if not split:
        square_relay(l, made, send, relay, landed)
    return made


def square_relay(l, made, send, relay, landed):
    lines = send.shape[1]
    first, second = pl.ds(0, lines // 2), pl.ds(lines // 2, lines // 2)
    one, two = l.beside(1), l.beside(2)
    made[0].wait_recv()
    value = send[two, first].astype(jnp.float32) + relay[0].astype(jnp.float32)
    send[two, first] = value.astype(jnp.bfloat16)
    made.append(l.copy(send.at[two, first], landed.at[1, first], flip=2))
    made[1].wait_recv()
    value = send[one, second].astype(jnp.float32) + relay[1].astype(jnp.float32)
    send[one, second] = value.astype(jnp.bfloat16)
    made.append(l.copy(send.at[one, second], landed.at[0, second], flip=1))


def square_settle(l, total_of, made, landed, both):
    total = total_of(l.low)
    arrived(made[2:])
    total = total + landed[0].astype(jnp.float32) + landed[1].astype(jnp.float32)
    both[l.core] = total.astype(jnp.bfloat16)
    return l.copy(both.at[l.core], both.at[l.core], dc=1)


def roll_heads(value):
    width = value.shape[1]
    lane = lax.broadcasted_iota(jnp.int32, value.shape, 1)
    left = pltpu.roll(value, width - HD // 2, 1)
    right = pltpu.roll(value, HD // 2, 1)
    return jnp.where(lane % HD < HD // 2, left, right)


def rope_rows(cos, sin, at, copies):
    return (
        jnp.concatenate([cos[at]] * copies, axis=1),
        jnp.concatenate([sin[at]] * copies, axis=1),
    )


def rope_key_rows(cos, sin, at):
    lane = lax.broadcasted_iota(jnp.int32, (1, 2 * HD), 1)
    return (jnp.where(lane < HD, cos[at], 1.0), jnp.where(lane < HD, sin[at], 0.0))


def allowed_keys(l, lengths, row, span, keys):
    def segment_of(place):
        total = jnp.zeros_like(place)
        end = lengths[row, 0]
        for doc in range(4):
            if doc:
                end = end + lengths[row, doc]
            total = total + (place >= end).astype(jnp.int32)
        return total

    query = l.high * span + lax.broadcasted_iota(jnp.int32, (span, 1), 0)
    key = lax.broadcasted_iota(jnp.int32, (1, keys), 1)
    return (segment_of(query) == segment_of(key)) & (query >= key)


def front_kernel(
    sizes,
    lengths,
    x_in,
    g_in,
    qkv_in,
    gain_in,
    wo_in,
    wg_in,
    wu_in,
    wd_in,
    cos_in,
    sin_in,
    qkv_out,
    wo_out,
    gain_out,
    normed_one_out,
    q_out,
    kv_out,
    attn_out,
    residual_out,
    dwg_out,
    dwu_out,
    dwd_out,
    normed_two_part,
    layer_part,
    x_all,
    normed,
    wqkv,
    wo,
    gains,
    gain_rows,
    cos,
    sin,
    q,
    kv,
    attn,
    low_attn,
    send_core,
    recv_core,
    send_block,
    recv_block,
    relay,
    both,
    residual,
    normed_two,
    g_all,
    wg,
    wu,
    wd,
    hidden,
    gate_act,
    up_act,
    send_sem,
    recv_sem,
    local_sem,
):
    rows, local, model, high_size = sizes
    own = rows * local
    tokens = SQUARE * own
    half = model // 2
    block = qkv_in.shape[0]
    heads = q.shape[2] // HD
    span = SQUARE * local
    keys = high_size * span
    l = Links(send_sem, recv_sem, local_sem, high_size)
    near = [dict(dl=dl) for dl in range(1, SQUARE)]
    far = [dict(dh=1, dl=dl) for dl in range(SQUARE)]
    l.greet(near + far + [dict(dx=1), dict(dc=1)])

    def row_spot(ref):
        def spot(x, h, low, n):
            start = ((x * high_size + h) * SQUARE + low) * block
            return ref.at[pl.ds(pl.multiple_of(start, block), n * block)]

        return spot

    def block_spot(ref):
        return lambda x, h, low, n: ref.at[pl.ds((x * high_size + h) * SQUARE + low, n)]

    def half_spot(ref):
        def spot(x, h, low, n):
            start = pl.multiple_of((h * SQUARE + low) * block, block)
            return ref.at[x, :, pl.ds(start, n * block)]

        return spot

    def row_half_spot(ref):
        def spot(x, h, low, n):
            start = pl.multiple_of((h * SQUARE + low) * block, block)
            return ref.at[x, pl.ds(start, n * block)]

        return spot

    def columns(ref, width):
        return lambda j: ref.at[:, pl.ds(pl.multiple_of(j * width, width), width)]

    def lines(ref, width):
        return lambda j: ref.at[pl.ds(pl.multiple_of(j * width, width), width)]

    def part_at(low, part):
        if part is None:
            return pl.ds(pl.multiple_of(low * own, own), own)
        return pl.ds(pl.multiple_of(low * own + part * (own // 2), own // 2), own // 2)

    def x_spot(side, low, part=None):
        return x_all.at[side, part_at(low, part)]

    def g_spot(side, low, part=None):
        return g_all.at[side, part_at(low, part)]

    def normed_two_spot(side, low, part=None):
        return normed_two.at[side, part_at(low, part)]

    def own_part_of(ref):
        return lambda part: ref.at[
            pl.ds(part * (own // 2), own // 2), pl.ds(pl.multiple_of(l.core * half, half), half)
        ]

    def side_of(ref, side):
        return ref.at[:, pl.ds(pl.multiple_of(side * half, half), half)]

    loads = [l.local(side_of(x_in, side), x_spot(side, l.low)) for side in range(2)]
    loads += [l.local(cos_in, cos), l.local(sin_in, sin)]
    w_gain = Weight(l, lambda j: gain_in.at[pl.ds(0, 1)], block_spot(gains))
    w_qkv = Weight(l, columns(qkv_in, wqkv.shape[1]), row_spot(wqkv))
    x_pushed = gather_push(l, x_spot, own_part_of(x_in))
    w_o = Weight(l, lines(wo_in, wo.shape[1]), half_spot(wo))
    w_gate = Weight(l, columns(wg_in, wg.shape[2]), row_half_spot(wg))

    w_gain.pass_near()
    w_qkv.pass_near()
    x_handed, _ = gather_across(l, x_spot, x_pushed)
    w_gain.pass_far()
    w_qkv.pass_far()
    w_o.pass_near()
    w_o.pass_far()
    for made in loads:
        made.wait()
    w_gain.wait()
    for b in range(gains.shape[0]):
        tile = gains[b].astype(jnp.float32)
        gain_rows[0:1, b * block : (b + 1) * block] = tile[0:1]
        gain_rows[1:2, b * block : (b + 1) * block] = tile[1:2]
    arrived(x_handed)

    step = 128

    def norm_step(i, carry):
        at = pl.ds(pl.multiple_of(i * step, step), step)
        first, second = x_all[0, at].astype(jnp.float32), x_all[1, at].astype(jnp.float32)
        total = jnp.sum(first * first, axis=1, keepdims=True)
        total = total + jnp.sum(second * second, axis=1, keepdims=True)
        scale = lax.rsqrt(total / model + EPSILON)
        normed[0, at] = (first * scale * gain_rows[0:1, :half]).astype(jnp.bfloat16)
        normed[1, at] = (second * scale * gain_rows[0:1, half:]).astype(jnp.bfloat16)
        return carry

    lax.fori_loop(0, tokens // step, norm_step, 0)
    normed_store = l.local(normed, normed_one_out)
    stores = []
    w_qkv.wait()
    stores += [l.local(wqkv, qkv_out), l.local(gain_rows, gain_out)]

    def project_step(i, carry):
        at = pl.ds(pl.multiple_of(i * local, local), local)
        pre = dot(normed[0, at], wqkv[:half]) + dot(normed[1, at], wqkv[half:])
        cos_q, sin_q = rope_rows(cos, sin, at, heads // 2)
        cos_k, sin_k = rope_key_rows(cos, sin, at)
        cos_all = jnp.concatenate([cos_q, cos_k], axis=1)
        sin_all = jnp.concatenate([sin_q, sin_k], axis=1)
        turned = pre * cos_all + roll_heads(pre) * sin_all
        spot = pl.ds(pl.multiple_of((i // rows) * local, local), local)
        q[i % rows, spot] = (turned[:, : heads * HD].astype(jnp.bfloat16) * HD ** (-0.5)).astype(
            jnp.bfloat16
        )
        kv[l.high, i % rows, spot] = turned[:, heads * HD :].astype(jnp.bfloat16)
        return carry

    lax.fori_loop(0, SQUARE * rows, project_step, 0)
    kv_copy = l.copy(kv.at[l.high], kv.at[l.high], dh=1)
    stores.append(l.local(q, q_out))
    w_gate.pass_near()
    w_up = Weight(l, columns(wu_in, wu.shape[2]), row_half_spot(wu))
    kv_copy.wait_recv()
    stores.append(l.local(kv, kv_out))

    def attend_row(r, carry):
        allowed = allowed_keys(l, lengths, r, span, keys)
        kv_row = kv[:, r].reshape(keys, 2 * HD)
        k, v = kv_row[:, :HD], kv_row[:, HD:]
        q_row = q[r]
        outs = []
        for head in range(heads):
            score = dot(q_row[:, head * HD : (head + 1) * HD], k, ((1,), (1,)))
            score = jnp.where(allowed, score, MASKED)
            top = jnp.max(score, axis=1, keepdims=True)
            grown = jnp.exp(score - top)
            total = jnp.sum(grown, axis=1, keepdims=True)
            probs = (grown * (1.0 / total)).astype(jnp.bfloat16)
            outs.append(dot(probs, v))
        out = jnp.concatenate(outs, axis=1)
        for j in range(SQUARE):
            at = pl.ds(pl.multiple_of(j * own + r * local, local), local)
            part = out[j * local : (j + 1) * local]
            attn[at] = part
            low_attn[at] = part.astype(jnp.bfloat16)
        return carry

    lax.fori_loop(0, rows, attend_row, 0)
    stores.append(l.local(attn, attn_out))
    w_gate.pass_far()
    w_o.wait()
    stores.append(l.local(wo, wo_out))

    def project_out(j, side):
        at = pl.ds(pl.multiple_of(j * own, own), own)
        return dot(low_attn[at], wo[side])

    handed = []
    for j in range(SQUARE):
        send_core[j] = project_out(j, 1 - l.core).astype(jnp.bfloat16)
        handed.append(l.copy(send_core.at[j], recv_core.at[j], dc=1))
    arrived(handed)

    def total_out(j):
        return project_out(j, l.core) + recv_core[j].astype(jnp.float32)

    pushed = square_push(l, total_out, send_block, relay, recv_block)
    w_up.pass_near()
    square_settle(l, total_out, pushed, recv_block, both).wait_recv()
    at_own = pl.ds(pl.multiple_of(l.low * own, own), own)
    total = jnp.zeros((own, 1), jnp.float32)
    for side in range(2):
        value = x_all[side, at_own].astype(jnp.float32) + both[side].astype(jnp.float32)
        residual[:, side * half : (side + 1) * half] = value
        total = total + jnp.sum(value * value, axis=1, keepdims=True)
    scale = lax.rsqrt(total / model + EPSILON)
    for side in range(2):
        at = slice(side * half, (side + 1) * half)
        normed_two[side, at_own] = (residual[:, at] * scale * gain_rows[1:2, at]).astype(
            jnp.bfloat16
        )
    stores.append(l.local(residual, residual_out))
    pushed = gather_push(
        l, normed_two_spot, lambda part: normed_two_spot(l.core, l.low, part)
    )
    w_up.pass_far()
    w_down = Weight(l, lines(wd_in, wd.shape[1]), half_spot(wd))
    handed, _ = gather_across(l, normed_two_spot, pushed)
    loads = [l.local(side_of(g_in, side), g_spot(side, l.low)) for side in range(2)]
    g_pushed = gather_push(l, g_spot, own_part_of(g_in))
    w_down.pass_near()
    arrived(handed)
    normed_store.wait()
    w_gate.wait()
    w_up.wait()

    def unit_step(j, carry):
        at = part_at(j, None)
        first, second = normed_two[0, at], normed_two[1, at]
        gate = dot(first, wg[0]) + dot(second, wg[1])
        up = dot(first, wu[0]) + dot(second, wu[1])
        sigmoid = jax.nn.sigmoid(gate)
        silu = gate * sigmoid
        hidden[at] = (silu * up).astype(jnp.bfloat16)
        gate_act[at] = (up * sigmoid * (1.0 + gate * (1.0 - sigmoid))).astype(jnp.bfloat16)
        up_act[at] = silu.astype(jnp.bfloat16)
        return carry

    lax.fori_loop(0, SQUARE, unit_step, 0)
    g_handed, _ = gather_across(l, g_spot, g_pushed)
    w_down.pass_far()
    for made in loads:
        made.wait()
    arrived(g_handed)
    busy = [(0, None), (1, None)]

    def fill(product, out):
        k, made = busy.pop(0)
        if made is not None:
            made.wait()
        buffer = normed.at[k]

        def step(i, carry):
            at = pl.ds(pl.multiple_of(i * own, own), own)
            buffer[at] = product(at).astype(jnp.bfloat16)
            return carry

        lax.fori_loop(0, half // own, step, 0)
        busy.append((k, l.local(buffer, out)))

    for side in range(2):
        fill(
            lambda at, side=side: dot(hidden[:, at], g_all[side], ((0,), (0,))),
            dwd_out.at[side],
        )
    w_down.wait()

    def act_step(j, carry):
        at = part_at(j, None)
        grad = dot(g_all[0, at], wd[0], ((1,), (1,))) + dot(g_all[1, at], wd[1], ((1,), (1,)))
        gate_act[at] = (grad * gate_act[at].astype(jnp.float32)).astype(jnp.bfloat16)
        up_act[at] = (grad * up_act[at].astype(jnp.float32)).astype(jnp.bfloat16)
        return carry

    lax.fori_loop(0, SQUARE, act_step, 0)
    for side in range(2):
        fill(
            lambda at, side=side: dot(gate_act[at], wg[side], ((1,), (1,)))
            + dot(up_act[at], wu[side], ((1,), (1,))),
            normed_two_part.at[side],
        )
    for side in range(2):
        fill(lambda at, side=side: dot(hidden[at], wd[side]), layer_part.at[side])
    for act, out in ((gate_act, dwg_out), (up_act, dwu_out)):
        for side in range(2):
            fill(
                lambda at, side=side, act=act: dot(
                    normed_two[side, :, at], act[...], ((0,), (0,))
                ),
                out.at[side],
            )
    for _, made in busy:
        made.wait()
    for made in stores:
        made.wait()
    l.finish()


def front(sizes, lengths, x, g, qkv, gain, wo, wg, wu, wd, cos, sin):
    rows, local, model, high_size = sizes
    own = rows * local
    tokens = SQUARE * own
    half = model // 2
    heads = wo.shape[0] // SQUARE // HD
    width = qkv.shape[1] // SQUARE
    ff = wg.shape[1] // SQUARE
    blocks = model // qkv.shape[0]
    span = SQUARE * local
    low, f32 = jnp.bfloat16, jnp.float32
    shape = jax.ShapeDtypeStruct
    outs = (
        shape((model, width), low),
        shape((2, heads * HD, half), low),
        shape((8, model), f32),
        shape((2, tokens, half), low),
        shape((rows, span, heads * HD), low),
        shape((high_size, rows, span, 2 * HD), low),
        shape((tokens, heads * HD), f32),
        shape((own, model), f32),
        shape((2, half, ff), low),
        shape((2, half, ff), low),
        shape((2, ff, half), low),
        shape((2, tokens, half), low),
        shape((2, tokens, half), low),
    )
    anywhere = pl.BlockSpec(memory_space=pl.ANY)
    vmem = pltpu.VMEM
    return pl.pallas_call(
        functools.partial(front_kernel, sizes),
        out_shape=outs,
        in_specs=[pl.BlockSpec(memory_space=pltpu.SMEM)] + [anywhere] * 10,
        out_specs=[anywhere] * len(outs),
        scratch_shapes=[
            vmem((2, tokens, half), low),
            vmem((2, tokens, half), low),
            vmem((model, width), low),
            vmem((2, heads * HD, half), low),
            vmem((blocks,) + gain.shape[1:], low),
            vmem((8, model), f32),
            vmem((tokens, 2 * HD), f32),
            vmem((tokens, 2 * HD), f32),
            vmem((rows, span, heads * HD), low),
            vmem((high_size, rows, span, 2 * HD), low),
            vmem((tokens, heads * HD), f32),
            vmem((tokens, heads * HD), low),
            vmem((SQUARE, own, half), low),
            vmem((SQUARE, own, half), low),
            vmem((SQUARE, own, half), low),
            vmem((2, own, half), low),
            vmem((2, own // 2, half), low),
            vmem((2, own, half), low),
            vmem((own, model), f32),
            vmem((2, tokens, half), low),
            vmem((2, tokens, half), low),
            vmem((2, half, ff), low),
            vmem((2, half, ff), low),
            vmem((2, ff, half), low),
            vmem((tokens, ff), low),
            vmem((tokens, ff), low),
            vmem((tokens, ff), low),
            pltpu.SemaphoreType.DMA((128,)),
            pltpu.SemaphoreType.DMA((128,)),
            pltpu.SemaphoreType.DMA((32,)),
        ],
        compiler_params=pltpu.CompilerParams(
            collective_id=0, has_side_effects=True, vmem_limit_bytes=VMEM
        ),
        name="front",
    )(lengths, x, g, qkv, gain, wo, wg, wu, wd, cos, sin)


class Grad:
    def __init__(self, links, half_of, kept, crossed, block_of, landed):
        self.links, self.kept, self.crossed = links, kept, crossed
        self.block_of, self.landed = block_of, landed
        l = links
        self.own = l.local(half_of(l.x), kept) if half_of else None
        if half_of:
            self.cross = l.copy(half_of(1 - l.x), crossed, dx=1)

    def deal(self):
        l = self.links
        if self.own is not None:
            self.own.wait()
        self.cross.wait_recv()
        kept, crossed = self.kept, self.crossed
        lines = kept.shape[0]
        step = min(128, lines)

        def add(i, carry):
            at = pl.ds(pl.multiple_of(i * step, step), step)
            kept[at] = (kept[at].astype(jnp.float32) + crossed[at].astype(jnp.float32)).astype(
                jnp.bfloat16
            )
            return carry

        lax.fori_loop(0, lines // step, add, 0)
        self.dealt = []
        for dh in range(2):
            for dl in range(SQUARE):
                if dh or dl:
                    block = self.block_of((l.high + dh) % 2, (l.low + dl) % SQUARE)
                    self.dealt.append(
                        l.copy(block, self.landed(l.high, l.low), dh=dh, dl=dl)
                    )
        self.mine = l.local(self.block_of(l.high, l.low), self.landed(l.high, l.low))


def back_kernel(
    sizes,
    lengths,
    x_in,
    g_in,
    residual_in,
    gain_in,
    normed_two_part,
    layer_part,
    dwg_in,
    dwu_in,
    dwd_in,
    qkv_in,
    wo_in,
    normed_one_in,
    q_in,
    kv_in,
    attn_in,
    cos_in,
    sin_in,
    layer_out,
    input_out,
    land_q,
    land_o,
    land_g,
    land_u,
    land_d,
    gains_out,
    kept_g,
    kept_u,
    kept_d,
    cross_g,
    cross_u,
    cross_d,
    kept_q,
    cross_q,
    kept_o,
    cross_o,
    send_q,
    send_o,
    own_a,
    recv_core,
    recv_block,
    relay,
    recv_block_b,
    relay_b,
    both,
    both_b,
    x_own,
    g_own,
    residual,
    gain_rows,
    low_all,
    wqkv,
    wo,
    q,
    kv,
    attn,
    attn_grad,
    dkv,
    dkv_send,
    dkv_recv,
    dqkv,
    cos,
    sin,
    gain_send,
    gain_recv,
    out_low,
    gain_sum,
    send_sem,
    recv_sem,
    local_sem,
):
    rows, local, model, high_size = sizes
    own = rows * local
    tokens = SQUARE * own
    half = model // 2
    block = x_own.shape[1] // 16
    heads = q.shape[2] // HD
    span = SQUARE * local
    keys = high_size * span
    f32, b16 = jnp.float32, jnp.bfloat16
    l = Links(send_sem, recv_sem, local_sem, high_size)
    steps = [
        dict(dx=dx, dh=dh, dl=dl)
        for dx in range(2)
        for dh in range(2)
        for dl in range(SQUARE)
        if dx or dh or dl
    ]
    l.greet(steps + [dict(dc=1)])

    def row_block(ref):
        def at(h, low):
            start = pl.multiple_of((h * SQUARE + low) * block, block)
            return ref.at[pl.ds(start, block)]

        return at

    def column_block(ref):
        def at(h, low):
            start = pl.multiple_of((h * SQUARE + low) * block, block)
            return ref.at[:, pl.ds(start, block)]

        return at

    def tall(ref):
        lines = ref.shape[1] // SQUARE
        return lambda h, low: ref.at[h, pl.ds(pl.multiple_of(low * lines, lines), lines)]

    def broad(ref):
        wide = ref.shape[2] // SQUARE
        return lambda h, low: ref.at[h, :, pl.ds(pl.multiple_of(low * wide, wide), wide)]

    def block_at(j):
        return pl.ds(pl.multiple_of(j * own, own), own)

    def part_at(ref, j, side):
        return ref.at[side, block_at(j)]

    handed = [
        l.copy(part_at(normed_two_part, j, 1 - l.core), recv_core.at[j], dc=1)
        for j in range(SQUARE)
    ]
    owned = [l.local(part_at(normed_two_part, j, l.core), own_a.at[j]) for j in range(SQUARE)]
    loads = [
        l.local(residual_in, residual),
        l.local(gain_in, gain_rows),
        l.local(g_in, g_own),
    ]
    grad_d = Grad(
        l, lambda x: dwd_in.at[x], kept_d, cross_d, column_block(kept_d), tall(land_d)
    )
    later = [
        l.local(x_in, x_own),
        l.local(wo_in, wo),
        l.local(attn_in, attn),
        l.local(q_in, q),
        l.local(kv_in, kv),
        l.local(qkv_in, wqkv),
        l.local(cos_in, cos),
        l.local(sin_in, sin),
    ]

    def own_total(j):
        return own_a[j].astype(f32) + recv_core[j].astype(f32)

    def norm_back(value_of, gain_row, grads):
        squares = jnp.zeros((own, 1), f32)
        inner = jnp.zeros((own, 1), f32)
        for side in range(2):
            at = slice(side * half, (side + 1) * half)
            value = value_of(side)
            squares = squares + jnp.sum(value * value, axis=1, keepdims=True)
            weighted = grads[side].astype(f32) * gain_rows[gain_row : gain_row + 1, at]
            inner = inner + jnp.sum(weighted * value, axis=1, keepdims=True)
        scale = lax.rsqrt(squares / model + EPSILON)
        pull = scale * scale * scale * (inner / model)
        outs = []
        for side in range(2):
            at = slice(side * half, (side + 1) * half)
            value = value_of(side)
            grad = grads[side].astype(f32)
            summed = jnp.sum(grad * (value * scale), axis=0, keepdims=True)
            for b in range(half // block):
                gain_send[gain_row, side * (half // block) + b, 0:1] = summed[
                    :, b * block : (b + 1) * block
                ]
            weighted = grad * gain_rows[gain_row : gain_row + 1, at]
            outs.append(weighted * scale - value * pull)
        return outs

    def push_gains(gain_row):
        me = (l.x * 2 + l.high) * SQUARE + l.low
        made = []
        for step in steps:
            to = ((l.x + step["dx"]) % 2 * 2 + (l.high + step["dh"]) % 2) * SQUARE + (
                l.low + step["dl"]
            ) % SQUARE
            made.append(l.copy(gain_send.at[gain_row, to], gain_recv.at[gain_row, me], **step))
        return made, l.local(gain_send.at[gain_row, me], gain_recv.at[gain_row, me])

    for made in owned:
        made.wait()
    arrived(handed)

    pushed = square_push(l, own_total, own_a, relay, recv_block)
    for made in loads:
        made.wait()
    swapped = square_settle(l, own_total, pushed, recv_block, both)
    swapped.wait_recv()
    l.left(pushed + [swapped])
    outs = norm_back(
        lambda side: residual[:, side * half : (side + 1) * half], 1, [both[0], both[1]]
    )
    for side in range(2):
        at = slice(side * half, (side + 1) * half)
        value = g_own[:, at].astype(f32) + outs[side]
        residual[:, at] = value
        low_all[side, block_at(l.low)] = value.astype(b16)

    def low_spot(side, low, part):
        start = pl.multiple_of(low * own + part * (own // 2), own // 2)
        return low_all.at[side, pl.ds(start, own // 2)]

    low_pushed = gather_push(l, low_spot, lambda part: low_spot(l.core, l.low, part))
    grad_g = Grad(l, lambda x: dwg_in.at[x], kept_g, cross_g, row_block(kept_g), broad(land_g))
    ffn_gains = push_gains(1)
    handed_b = [
        l.copy(part_at(layer_part, j, 1 - l.core), recv_core.at[j], dc=1) for j in range(SQUARE)
    ]
    owned = [l.local(part_at(layer_part, j, l.core), own_a.at[j]) for j in range(SQUARE)]
    for made in later:
        made.wait()
    low_handed, low_corner = gather_across(l, low_spot, low_pushed)
    grad_d.deal()
    arrived(low_handed)
    grad_u = Grad(l, lambda x: dwu_in.at[x], kept_u, cross_u, row_block(kept_u), broad(land_u))

    def out_grad_step(j, carry):
        at = block_at(j)
        rows_at = attn[at].astype(b16)
        low_out = dot(low_all[0, at], wo[0], ((1,), (1,)))
        low_out = (low_out + dot(low_all[1, at], wo[1], ((1,), (1,)))).astype(b16)
        for r in range(rows):
            spot = pl.ds(pl.multiple_of(j * local, local), local)
            attn_grad[r, spot] = low_out[r * local : (r + 1) * local]
        out_low[at] = rows_at
        return carry

    lax.fori_loop(0, SQUARE, out_grad_step, 0)
    send_o[...] = dot(out_low[...], low_all[1 - l.x], ((0,), (0,))).astype(b16)
    grad_o = Grad(l, None, kept_o, cross_o, column_block(kept_o), tall(land_o))
    grad_o.cross = l.copy(send_o, cross_o, dx=1)
    kept_o[...] = dot(out_low[...], low_all[l.x], ((0,), (0,))).astype(b16)

    for made in owned:
        made.wait()
    arrived(handed_b)
    pushed_b = square_push(l, own_total, own_a, relay_b, recv_block_b, split=True)

    def attend_row(r, carry):
        allowed = allowed_keys(l, lengths, r, span, keys)
        kv_row = kv[:, r].reshape(keys, 2 * HD)
        k, v = kv_row[:, :HD], kv_row[:, HD:]
        q_row, go_row = q[r], attn_grad[r]
        out_row = jnp.concatenate(
            [
                attn[pl.ds(pl.multiple_of(j * own + r * local, local), local)]
                for j in range(SQUARE)
            ],
            axis=0,
        )
        grads = []
        dk = jnp.zeros((keys, HD), f32)
        dv = jnp.zeros((keys, HD), f32)
        for head in range(heads):
            at = slice(head * HD, (head + 1) * HD)
            qh, go = q_row[:, at], go_row[:, at]
            delta = jnp.sum(go.astype(f32) * out_row[:, at], axis=1, keepdims=True)
            score = jnp.where(allowed, dot(qh, k, ((1,), (1,))), MASKED)
            top = jnp.max(score, axis=1, keepdims=True)
            grown = jnp.exp(score - top)
            probs = grown * (1.0 / jnp.sum(grown, axis=1, keepdims=True))
            dv = dv + dot(probs.astype(b16), go, ((0,), (0,)))
            pull = dot(go, v, ((1,), (1,)))
            score_grad = (probs * (pull - delta)).astype(b16)
            grads.append(dot(score_grad, k) * HD ** (-0.5))
            dk = dk + dot(score_grad, qh, ((0,), (0,)))
        turned = jnp.concatenate(grads, axis=1)
        for j in range(SQUARE):
            at = pl.ds(pl.multiple_of(j * own + r * local, local), local)
            value = turned[j * local : (j + 1) * local]
            cos_q, sin_q = rope_rows(cos, sin, at, heads // 2)
            dqkv[at, : heads * HD] = (value * cos_q - roll_heads(value) * sin_q).astype(b16)
        both_kv = jnp.concatenate([dk, dv], axis=1)
        for part in range(high_size):
            dkv[part, r] = both_kv[part * span : (part + 1) * span]
        return carry

    dkv_copies = []
    for r in range(rows):
        lax.fori_loop(r, r + 1, attend_row, 0)
        dkv_send[r] = dkv[1 - l.high, r].astype(b16)
        dkv_copies.append(l.copy(dkv_send.at[r], dkv_recv.at[r], dh=1))
        if r == 0:
            square_relay(l, pushed_b, own_a, relay_b, recv_block_b)
            grad_g.deal()
    l.left(low_pushed + low_handed + low_corner)
    normed = l.local(normed_one_in, low_all)
    grad_o.deal()
    both_b_copy = square_settle(l, own_total, pushed_b, recv_block_b, both_b)
    arrived(dkv_copies)

    def unrotate_step(i, carry):
        at = pl.ds(pl.multiple_of(i * local, local), local)
        spot = pl.ds(pl.multiple_of((i // rows) * local, local), local)
        kv_sum = dkv[l.high, i % rows, spot] + dkv_recv[i % rows, spot].astype(f32)
        cos_k, sin_k = rope_key_rows(cos, sin, at)
        turned = kv_sum * cos_k - roll_heads(kv_sum) * sin_k
        dqkv[at, heads * HD :] = turned.astype(b16)
        return carry

    lax.fori_loop(0, SQUARE * rows, unrotate_step, 0)

    def project_back(j, side):
        weight = wqkv[pl.ds(pl.multiple_of(side * half, half), half)]
        return dot(dqkv[block_at(j)], weight, ((1,), (1,)))

    both_b_copy.wait_recv()
    l.left(pushed_b)
    handed = []
    for j in range(SQUARE):
        own_a[j] = project_back(j, 1 - l.core).astype(b16)
        handed.append(l.copy(own_a.at[j], recv_core.at[j], dc=1))
    normed.wait()
    send_q[...] = dot(low_all[1 - l.x], dqkv[...], ((0,), (0,))).astype(b16)
    arrived(handed)

    def own_total_c(j):
        return project_back(j, l.core) + recv_core[j].astype(f32)

    l.left(handed)
    pushed = square_push(l, own_total_c, own_a, relay, recv_block)
    grad_q = Grad(l, None, kept_q, cross_q, row_block(kept_q), lambda h, low: land_q.at[h, low])
    grad_q.cross = l.copy(send_q, cross_q, dx=1)
    kept_q[...] = dot(low_all[l.x], dqkv[...], ((0,), (0,))).astype(b16)
    grad_u.deal()
    grad_q.deal()
    square_settle(l, own_total_c, pushed, recv_block, both).wait_recv()
    outs = norm_back(
        lambda side: x_own[:, side * half : (side + 1) * half].astype(f32),
        0,
        [both[0], both[1]],
    )
    attn_gains = push_gains(0)
    for side in range(2):
        at = slice(side * half, (side + 1) * half)
        x_own[:, at] = (residual[:, at] + outs[side]).astype(b16)
    stores = [l.local(x_own, input_out)]
    residual_load = l.local(residual_in, residual)
    residual_load.wait()
    for side in range(2):
        at = slice(side * half, (side + 1) * half)
        g_own[:, at] = (residual[:, at] + both_b[side].astype(f32)).astype(b16)
    stores.append(l.local(g_own, layer_out))
    for made, kept in (ffn_gains, attn_gains):
        arrived(made)
        kept.wait()
    for row in range(2):
        total = jnp.zeros((8, block), f32)
        for b in range(16):
            total = total + gain_recv[row, b]
        gain_sum[row : row + 1] = total[0:1]
    stores.append(l.local(gain_sum, gains_out))
    for grad in (grad_d, grad_o, grad_g, grad_u, grad_q):
        grad.mine.wait()
        arrived(grad.dealt)
    for made in stores:
        made.wait()
    l.finish()


def back(sizes, lengths, *arrays):
    rows, local, model, high_size = sizes
    own = rows * local
    tokens = SQUARE * own
    half = model // 2
    block = model // 16
    ff = arrays[6].shape[2]
    width = arrays[9].shape[1]
    wide = width - 2 * HD
    span = SQUARE * local
    b16, f32 = jnp.bfloat16, jnp.float32
    shape = jax.ShapeDtypeStruct
    vmem = pltpu.VMEM
    outs = (
        shape((own, model), b16),
        shape((own, model), b16),
        shape((2, SQUARE, block, width), b16),
        shape((2, SQUARE * wide, block), b16),
        shape((2, block, SQUARE * ff), b16),
        shape((2, block, SQUARE * ff), b16),
        shape((2, SQUARE * ff, block), b16),
        shape((8, block), f32),
    )
    anywhere = pl.BlockSpec(memory_space=pl.ANY)
    scratch = [
        vmem((half, ff), b16),
        vmem((half, ff), b16),
        vmem((ff, half), b16),
        vmem((half, ff), b16),
        vmem((half, ff), b16),
        vmem((ff, half), b16),
        vmem((half, width), b16),
        vmem((half, width), b16),
        vmem((wide, half), b16),
        vmem((wide, half), b16),
        vmem((half, width), b16),
        vmem((wide, half), b16),
        vmem((SQUARE, own, half), b16),
        vmem((SQUARE, own, half), b16),
        vmem((2, own, half), b16),
        vmem((2, own // 2, half), b16),
        vmem((2, own, half), b16),
        vmem((2, own // 2, half), b16),
        vmem((2, own, half), b16),
        vmem((2, own, half), b16),
        vmem((own, model), b16),
        vmem((own, model), b16),
        vmem((own, model), f32),
        vmem((8, model), f32),
        vmem((2, tokens, half), b16),
        vmem((model, width), b16),
        vmem((2, wide, half), b16),
        vmem((rows, span, wide), b16),
        vmem((high_size, rows, span, 2 * HD), b16),
        vmem((tokens, wide), f32),
        vmem((rows, span, wide), b16),
        vmem((high_size, rows, span, 2 * HD), f32),
        vmem((rows, span, 2 * HD), b16),
        vmem((rows, span, 2 * HD), b16),
        vmem((tokens, width), b16),
        vmem((tokens, 2 * HD), f32),
        vmem((tokens, 2 * HD), f32),
        vmem((2, 16, 8, block), f32),
        vmem((2, 16, 8, block), f32),
        vmem((tokens, wide), b16),
        vmem((8, block), f32),
        pltpu.SemaphoreType.DMA((128,)),
        pltpu.SemaphoreType.DMA((128,)),
        pltpu.SemaphoreType.DMA((64,)),
    ]
    return pl.pallas_call(
        functools.partial(back_kernel, sizes),
        out_shape=outs,
        in_specs=[pl.BlockSpec(memory_space=pltpu.SMEM)] + [anywhere] * len(arrays),
        out_specs=[anywhere] * len(outs),
        scratch_shapes=scratch,
        compiler_params=pltpu.CompilerParams(
            collective_id=1, has_side_effects=True, vmem_limit_bytes=VMEM
        ),
        name="back",
    )(lengths, *arrays)


def norm_back(values, scale, gain, grad):
    weighted = grad * gain
    gain_grad = jnp.sum(grad * values * scale, axis=0)
    inner = jnp.mean(weighted * values, axis=-1, keepdims=True)
    return (weighted * scale - values * scale**3 * inner, gain_grad)


def shards_exchanged(
    hidden_in,
    doc_lengths,
    attn_gain,
    query_weight,
    key_weight,
    value_weight,
    output_weight,
    ffn_gain,
    gate_weight,
    up_weight,
    down_weight,
    out_grad,
):
    rows, local, model = hidden_in.shape
    tokens = rows * local
    seq = lax.axis_index("seq")
    core = lax.axis_index("mp")
    low, high = seq % SQUARE, seq // SQUARE
    high_size = lax.axis_size("seq") // SQUARE
    place = (lax.axis_index("dp"), high, low, lax.axis_size("dp"), high_size)
    group = H // KVH
    span = SQUARE * local

    ends = jnp.cumsum(doc_lengths, axis=-1)
    info = jnp.concatenate([jnp.stack([low, high]), ends.reshape(-1)]).astype(jnp.int32)

    gains = lax.all_gather(jnp.stack([attn_gain, ffn_gain]), ("dp", "seq"), axis=1, tiled=True)
    gain_one, gain_two = gains[0].astype(jnp.float32), gains[1].astype(jnp.float32)

    own_in = hidden_in.reshape(tokens, model)
    all_in = gather_square(own_in, core).astype(jnp.float32)
    query_own = spread_weight(query_weight, 0, place)
    key_own = spread_weight(key_weight, 0, place)
    value_own = spread_weight(value_weight, 0, place)
    output_own = spread_weight(output_weight, 1, place)
    gate_own = spread_weight(gate_weight, 0, place)
    up_own = spread_weight(up_weight, 0, place)
    down_own = spread_weight(down_weight, 1, place)
    all_grad = gather_square(out_grad.reshape(tokens, model), core)

    blocks = low ^ jnp.arange(SQUARE, dtype=jnp.int32)
    spots = (high * span + blocks[:, None] * local + jnp.arange(local, dtype=jnp.int32)[None, :])
    reached = spots[:, None, :, None] >= ends[None, :, None, :]
    begin = jnp.max(jnp.where(reached, ends[None, :, None, :], 0), axis=-1)
    position = (spots[:, None, :] - begin).astype(jnp.float32)
    cosine, sine = rope_tables(position, HD)

    scale_one = lax.rsqrt(jnp.mean(all_in * all_in, axis=-1, keepdims=True) + EPSILON)
    normed_one = (all_in * scale_one * gain_one).astype(jnp.bfloat16)
    query_pre = dot(normed_one, query_own).reshape(SQUARE, rows, local, group, HD)
    key_pre = dot(normed_one, key_own).reshape(SQUARE, rows, local, 1, HD)
    value_pre = dot(normed_one, value_own).reshape(SQUARE, rows, local, HD)
    queries = rotate(query_pre, cosine, sine).astype(jnp.bfloat16)
    queries = queries.reshape(SQUARE, rows, local, group * HD)
    keys = rotate(key_pre, cosine, sine).astype(jnp.bfloat16).reshape(value_pre.shape)
    kv = jnp.concatenate([keys, value_pre.astype(jnp.bfloat16)], axis=-1)[None]
    for bit in bits_of(high_size):
        kv = jnp.concatenate([kv, swap(kv, "seq", SQUARE * bit)], axis=0)
    attn, lse = attend(info, queries, kv)
    attn_low = attn.reshape(SQUARE * tokens, group * HD).astype(jnp.bfloat16)
    residual = own_in.astype(jnp.float32) + scatter_square(dot(attn_low, output_own), core)

    scale_two = lax.rsqrt(jnp.mean(residual * residual, axis=-1, keepdims=True) + EPSILON)
    normed_two = (residual * scale_two * gain_two).astype(jnp.bfloat16)
    normed_two = gather_square(normed_two, core)
    gate_proj = dot(normed_two, gate_own)
    up_proj = dot(normed_two, up_own)
    sigmoid_gate = jax.nn.sigmoid(gate_proj)
    silu_gate = gate_proj * sigmoid_gate
    hidden_units = (silu_gate * up_proj).astype(jnp.bfloat16)
    hidden_grad = dot(all_grad, down_own, ((1,), (1,)))
    gate_act = (
        hidden_grad * up_proj * sigmoid_gate * (1.0 + gate_proj * (1.0 - sigmoid_gate))
    ).astype(jnp.bfloat16)
    up_act = (hidden_grad * silu_gate).astype(jnp.bfloat16)
    down_grad = settle_grad(dot(hidden_units, all_grad, ((0,), (0,))), 1, place)
    normed_two_grad = scatter_square(
        dot(gate_act, gate_own, ((1,), (1,))) + dot(up_act, up_own, ((1,), (1,))), core
    )
    layer_out = residual + scatter_square(dot(hidden_units, down_own), core)
    layer_out = layer_out.astype(jnp.bfloat16).reshape(hidden_in.shape)
    gate_grad = settle_grad(dot(normed_two, gate_act, ((0,), (0,))), 0, place)
    up_grad = settle_grad(dot(normed_two, up_act, ((0,), (0,))), 0, place)

    residual_part, ffn_gain_grad = norm_back(residual, scale_two, gain_two, normed_two_grad)
    residual_grad = out_grad.reshape(tokens, model).astype(jnp.float32) + residual_part
    residual_low = gather_square(residual_grad.astype(jnp.bfloat16), core)
    output_grad = settle_grad(dot(attn_low, residual_low, ((0,), (0,))), 1, place)
    attn_grad = dot(residual_low, output_own, ((1,), (1,))).astype(jnp.bfloat16)
    attn_grad = attn_grad.reshape(queries.shape)
    query_acc, kv_acc = attend_back(info, queries, kv, attn_grad, attn, lse)
    for bit in reversed(bits_of(high_size)):
        sent = kv_acc[bit:].astype(jnp.bfloat16)
        kv_acc = kv_acc[:bit] + swap(sent, "seq", SQUARE * bit).astype(jnp.float32)
    kv_acc = kv_acc[0]
    query_back = unrotate(query_acc.reshape(query_pre.shape), cosine, sine).astype(jnp.bfloat16)
    key_back = unrotate(kv_acc[..., :HD].reshape(key_pre.shape), cosine, sine)
    key_back = key_back.astype(jnp.bfloat16).reshape(SQUARE * tokens, HD)
    value_back = kv_acc[..., HD:].astype(jnp.bfloat16).reshape(SQUARE * tokens, HD)
    query_back = query_back.reshape(SQUARE * tokens, group * HD)
    normed_one_grad = scatter_square(
        dot(query_back, query_own, ((1,), (1,)))
        + dot(key_back, key_own, ((1,), (1,)))
        + dot(value_back, value_own, ((1,), (1,))),
        core,
    )
    query_grad = settle_grad(dot(normed_one, query_back, ((0,), (0,))), 0, place)
    key_grad = settle_grad(dot(normed_one, key_back, ((0,), (0,))), 0, place)
    value_grad = settle_grad(dot(normed_one, value_back, ((0,), (0,))), 0, place)
    own_32 = own_in.astype(jnp.float32)
    own_scale = lax.rsqrt(jnp.mean(own_32 * own_32, axis=-1, keepdims=True) + EPSILON)
    input_part, attn_gain_grad = norm_back(own_32, own_scale, gain_one, normed_one_grad)
    input_grad = (residual_grad + input_part).astype(jnp.bfloat16).reshape(hidden_in.shape)
    gain_grads = lax.psum_scatter(
        jnp.stack([attn_gain_grad, ffn_gain_grad]), ("dp", "seq"), scatter_dimension=1, tiled=True
    )
    return (
        layer_out,
        input_grad,
        gain_grads[0],
        query_grad,
        key_grad,
        value_grad,
        output_grad,
        gain_grads[1],
        gate_grad,
        up_grad,
        down_grad,
    )


def shards(
    hidden_in,
    doc_lengths,
    attn_gain,
    query_weight,
    key_weight,
    value_weight,
    output_weight,
    ffn_gain,
    gate_weight,
    up_weight,
    down_weight,
    out_grad,
):
    rows, local, model = hidden_in.shape
    tokens = rows * local
    seq = lax.axis_index("seq")
    high = seq // SQUARE
    high_size = lax.axis_size("seq") // SQUARE
    block = query_weight.shape[0]
    if block % 128 or high_size != 2 or lax.axis_size("dp") != 2:
        return shards_exchanged(
            hidden_in,
            doc_lengths,
            attn_gain,
            query_weight,
            key_weight,
            value_weight,
            output_weight,
            ffn_gain,
            gate_weight,
            up_weight,
            down_weight,
            out_grad,
        )
    group = H // KVH
    span = SQUARE * local
    width = (group + 2) * HD

    spots = high * span + jnp.arange(span, dtype=jnp.int32).reshape(SQUARE, 1, local)
    begin, end = jnp.zeros((1, rows, 1), jnp.int32), jnp.zeros((1, rows, 1), jnp.int32)
    for doc in range(doc_lengths.shape[1]):
        end = end + doc_lengths[:, doc].reshape(1, rows, 1)
        begin = jnp.where(spots >= end, end, begin)
    position = (spots - begin).astype(jnp.float32).reshape(SQUARE * tokens, 1)
    angles = position * jnp.tile(inverse_freqs(HD), 4)[None, :]
    sign = jnp.where(jnp.arange(2 * HD) % HD < HD // 2, -1.0, 1.0)[None, :]
    cos, sin = jnp.cos(angles), jnp.sin(angles) * sign
    qkv_shard = jnp.concatenate(
        [
            query_weight.reshape(block, SQUARE, group * HD),
            key_weight.reshape(block, SQUARE, HD),
            value_weight.reshape(block, SQUARE, HD),
        ],
        axis=2,
    ).reshape(block, SQUARE * width)
    gain_shard = jnp.concatenate(
        [attn_gain[None, None], ffn_gain[None, None], jnp.zeros((1, 14, block), jnp.bfloat16)],
        axis=1,
    )
    lengths = doc_lengths
    own_in = hidden_in.reshape(tokens, model)
    own_grad = out_grad.reshape(tokens, model)
    (
        qkv_own,
        output_own,
        gains,
        normed_one,
        queries,
        kv,
        attn,
        residual,
        gate_part,
        up_part,
        down_part,
        normed_two_part,
        layer_part,
    ) = front(
        (rows, local, model, high_size),
        lengths,
        own_in,
        own_grad,
        qkv_shard,
        gain_shard,
        output_weight,
        gate_weight,
        up_weight,
        down_weight,
        cos,
        sin,
    )
    (
        layer_out,
        input_grad,
        *landed,
        gain_grads,
    ) = back(
        (rows, local, model, high_size),
        lengths,
        own_in,
        own_grad,
        residual,
        gains,
        normed_two_part,
        layer_part,
        gate_part,
        up_part,
        down_part,
        qkv_own,
        output_own,
        normed_one,
        queries,
        kv,
        attn,
        cos,
        sin,
    )
    qkv_grad, output_grad, gate_grad, up_grad, down_grad = (
        part[0].astype(jnp.float32) + part[1].astype(jnp.float32) for part in landed
    )
    query_grad = qkv_grad[..., : group * HD].transpose(1, 0, 2).reshape(block, -1)
    key_grad = qkv_grad[..., group * HD : (group + 1) * HD].transpose(1, 0, 2).reshape(block, -1)
    value_grad = qkv_grad[..., (group + 1) * HD :].transpose(1, 0, 2).reshape(block, -1)
    return (
        layer_out.reshape(hidden_in.shape),
        input_grad.reshape(hidden_in.shape),
        gain_grads[0],
        query_grad,
        key_grad,
        value_grad,
        output_grad,
        gain_grads[1],
        gate_grad,
        up_grad,
        down_grad,
    )


def solution(mesh):
    return jax.shard_map(
        shards,
        mesh=mesh,
        in_specs=(
            P("dp", "seq", None),
            P("dp", None),
            P(("dp", "seq")),
            P(("dp", "seq"), "mp"),
            P(("dp", "seq"), "mp"),
            P(("dp", "seq"), "mp"),
            P("mp", ("dp", "seq")),
            P(("dp", "seq")),
            P(("dp", "seq"), "mp"),
            P(("dp", "seq"), "mp"),
            P("mp", ("dp", "seq")),
            P("dp", "seq", None),
        ),
        out_specs=(
            P("dp", "seq", None),
            P("dp", "seq", None),
            P(("dp", "seq")),
            P(("dp", "seq"), "mp"),
            P(("dp", "seq"), "mp"),
            P(("dp", "seq"), "mp"),
            P("mp", ("dp", "seq")),
            P(("dp", "seq")),
            P(("dp", "seq"), "mp"),
            P(("dp", "seq"), "mp"),
            P("mp", ("dp", "seq")),
        ),
        check_vma=False,
    )
```
